32 devices in a mesh: grp: 1, row: 8 (over z, y), br: 2 (over core), pb: 2 (over x).
Axes of the slice: x: 2, y: 2, z: 4, core: 2. Of those that a mesh axis runs over, the one named last changes fastest.
Arguments:
- homolog_representation: bfloat16 [128, 64, 256], P(('grp', 'pb'), ('row', 'br')), may hold values from -6 to 6
- pair_state: bfloat16 [64, 64, 128], P(('grp', 'row', 'br'), 'pb'), may hold values from -6 to 6
- genuine_chain_indicator: int32 [128], P('grp'), may hold values from 0 to 1
- resolved_mask: int32 [64], P('grp'), may hold values from 0 to 1
- crop_positions: int32 [64], P('grp'), may hold values from 0 to 12799, as said below
- relative_position_table: bfloat16 [65, 128], replicated, may hold values from -6 to 6
- column_query_key_value_gate: bfloat16 [256, 1024], replicated, may hold values from -48 to 48
- vertical_attention_projector: bfloat16 [256, 256], replicated, may hold values from -1.5 to 1.5
- expansion_coefficients: bfloat16 [256, 1024], replicated, may hold values from -0.375 to 0.375
- contraction_coefficients: bfloat16 [1024, 256], replicated, may hold values from -0.1875 to 0.1875
- operand_duo_projector: bfloat16 [256, 64], replicated, may hold values from -0.375 to 0.375
- tensor_product_projector: bfloat16 [1024, 128], replicated, may hold values from -2 to 2
- triangle_query_key_value_gate: bfloat16 [128, 512], replicated, may hold values from -48 to 48
- triangle_bias_weight: bfloat16 [128, 4], replicated, may hold values from -0.5 to 0.5
- triangle_output_weight: bfloat16 [128, 128], replicated, may hold values from -2 to 2
- pair_up_weight: bfloat16 [128, 512], replicated, may hold values from -0.5 to 0.5
- pair_down_weight: bfloat16 [512, 128], replicated, may hold values from -0.25 to 0.25
Outputs:
- refreshed_homologs: bfloat16 [128, 64, 256], P(('grp', 'pb'), ('row', 'br'))
- pair_updated: bfloat16 [64, 64, 128], P(('grp', 'row', 'br'), 'pb')
The draws below stay inside these ranges and needn't reach their ends.
Inputs may be any that keep to these rules, and one draw needn't show every extreme that they name: `crop_positions`: strictly increasing; the last entry is exactly 12799.
All inputs are finite; a program needn't handle non-finite values.
Results may differ from the reference program's by a relative error of at most 0.012.
Values may be sent and summed in bfloat16 or wider, within the bound.
A program may use at most 64 MiB of HBM per device.

```python
import math
import jax
import jax.numpy as jnp
from jax import lax

ALIGNED_FEATURES = 256
COUPLING_DEPTH = 128
VERTICAL_ATTENDS = 8
TRI_HEADS = 4
SUBSPACE_DEPTH = 32
OPERAND_FEATURES = 32
EXPANSION_NEURONS = 1024
PAIR_FF = 512
RELPOS_MAX = 32
CHAINS_PER_SHARD = 64
WINDOW_AMINOS = 64
ALIGNED_CHAINS = 128


def draw_genuine_chain_indicator(key, part):
    selections = jax.random.randint(key, (ALIGNED_CHAINS,), 0, 4)
    leading_index = jnp.arange(ALIGNED_CHAINS) == 0
    return jnp.where(leading_index, 1, (selections != 0).astype(jnp.int32)).astype(jnp.int32)


def draw_resolved_mask(key, part):
    selections = jax.random.randint(key, (WINDOW_AMINOS,), 0, 8)
    leading_index = jnp.arange(WINDOW_AMINOS) == 0
    return jnp.where(leading_index, 1, (selections != 0).astype(jnp.int32)).astype(jnp.int32)


def draw_crop_positions(key, part):
    key_break, key_jump = jax.random.split(key, 2)
    breaks = jax.random.randint(key_break, (WINDOW_AMINOS,), 0, 16) == 0
    jumps = jax.random.randint(key_jump, (WINDOW_AMINOS,), 2, 200)
    steps_between = jnp.where(breaks, jumps, 1)
    steps_between = jnp.where(jnp.arange(WINDOW_AMINOS) == 0, 0, steps_between).astype(jnp.int32)
    running = jnp.cumsum(steps_between).astype(jnp.int32)
    shift = WINDOW_AMINOS * 200 - 1 - running[WINDOW_AMINOS - 1]
    return (running + shift).astype(jnp.int32)


def paired_coefficients(key, width, heads):
    key_base = jax.random.fold_in(key, 0)
    base = jnp.clip(jax.random.normal(key_base, (width, 4, heads, SUBSPACE_DEPTH), jnp.float32), -6.0, 6.0) * width ** (-0.5)
    return base


def draw_column_query_key_value_gate(key, part):
    return paired_coefficients(key, ALIGNED_FEATURES, VERTICAL_ATTENDS).reshape(ALIGNED_FEATURES, 4 * ALIGNED_FEATURES).astype(jnp.bfloat16)


def draw_triangle_query_key_value_gate(key, part):
    drawn = paired_coefficients(key, COUPLING_DEPTH, TRI_HEADS)
    return jnp.transpose(drawn, (0, 2, 1, 3)).reshape(COUPLING_DEPTH, 4 * COUPLING_DEPTH).astype(jnp.bfloat16)


def block_levels(stream_key, shape, cuts, low, top_value):
    def one(dim, blocks):
        steps = jax.random.uniform(jax.random.fold_in(jax.random.fold_in(stream_key, 6), dim), (blocks,), jnp.float32, low / len(cuts), top_value / len(cuts))
        return jnp.repeat(jnp.exp(steps), shape[dim] // blocks).reshape((-1,) + (1,) * (len(shape) - dim - 1))

    loudness = one(*cuts[0])
    for cut in cuts[1:]:
        loudness = loudness * one(*cut)
    return loudness


def bell_draw(stream_key, dims, scale, reach, pieces=(), dtype=jnp.bfloat16):
    values = scale * jax.random.normal(stream_key, dims, jnp.float32)
    if pieces:
        values = values * block_levels(stream_key, dims, pieces, -0.22, 0.18)
    return jnp.clip(values, -reach, reach).astype(dtype)


def setup_inputs(seed: int = 0, part: int = 0) -> dict:
    keys = jax.random.split(jax.random.key(seed), 18)
    own_keys = jax.random.split(jax.random.fold_in(keys[17], part), 18)
    homolog_representation = bell_draw(own_keys[0], (ALIGNED_CHAINS, WINDOW_AMINOS, ALIGNED_FEATURES), 1.0, 6.0, ((0, 2), (1, 16)))
    pair_state = bell_draw(own_keys[1], (WINDOW_AMINOS, WINDOW_AMINOS, COUPLING_DEPTH), 1.0, 6.0, ((0, 16), (1, 2)))
    genuine_chain_indicator = draw_genuine_chain_indicator(jax.random.fold_in(jax.random.fold_in(keys[17], part), 71), part)
    resolved_mask = draw_resolved_mask(jax.random.fold_in(jax.random.fold_in(keys[17], part), 71), part)
    crop_positions = draw_crop_positions(jax.random.fold_in(jax.random.fold_in(keys[17], part), 71), part)
    relative_position_table = bell_draw(keys[5], (2 * RELPOS_MAX + 1, COUPLING_DEPTH), 1.0, 6.0)
    column_query_key_value_gate = draw_column_query_key_value_gate(jax.random.fold_in(keys[17], 71), part)
    vertical_attention_projector = bell_draw(keys[7], (ALIGNED_FEATURES, ALIGNED_FEATURES), (ALIGNED_FEATURES // 16) ** -0.5, 1.5)
    expansion_coefficients = bell_draw(keys[8], (ALIGNED_FEATURES, EXPANSION_NEURONS), ALIGNED_FEATURES ** -0.5, 0.375)
    contraction_coefficients = bell_draw(keys[9], (EXPANSION_NEURONS, ALIGNED_FEATURES), EXPANSION_NEURONS ** -0.5, 0.1875)
    operand_duo_projector = bell_draw(keys[10], (ALIGNED_FEATURES, 2 * OPERAND_FEATURES), ALIGNED_FEATURES ** -0.5, 0.375)
    tensor_product_projector = bell_draw(keys[11], (OPERAND_FEATURES * OPERAND_FEATURES, COUPLING_DEPTH), (max(1, OPERAND_FEATURES * OPERAND_FEATURES // ALIGNED_CHAINS)) ** -0.5, 2.0)
    triangle_query_key_value_gate = draw_triangle_query_key_value_gate(jax.random.fold_in(keys[17], 71), part)
    triangle_bias_weight = bell_draw(keys[13], (COUPLING_DEPTH, TRI_HEADS), COUPLING_DEPTH ** -0.5, 0.5)
    triangle_output_weight = bell_draw(keys[14], (COUPLING_DEPTH, COUPLING_DEPTH), (COUPLING_DEPTH // 16) ** -0.5, 2.0)
    pair_up_weight = bell_draw(keys[15], (COUPLING_DEPTH, PAIR_FF), COUPLING_DEPTH ** -0.5, 0.5)
    pair_down_weight = bell_draw(keys[16], (PAIR_FF, COUPLING_DEPTH), PAIR_FF ** -0.5, 0.25)
    return dict(homolog_representation=homolog_representation, pair_state=pair_state, genuine_chain_indicator=genuine_chain_indicator, resolved_mask=resolved_mask, crop_positions=crop_positions, relative_position_table=relative_position_table, column_query_key_value_gate=column_query_key_value_gate, vertical_attention_projector=vertical_attention_projector, expansion_coefficients=expansion_coefficients, contraction_coefficients=contraction_coefficients, operand_duo_projector=operand_duo_projector, tensor_product_projector=tensor_product_projector, triangle_query_key_value_gate=triangle_query_key_value_gate, triangle_bias_weight=triangle_bias_weight, triangle_output_weight=triangle_output_weight, pair_up_weight=pair_up_weight, pair_down_weight=pair_down_weight)


NORM_EPS = 1e-05
MASK_NEGATIVE = 1000000000.0

def layer_normalize(values):
    values = values.astype(jnp.float32)
    centre = lax.optimization_barrier(jnp.mean(values, axis=-1, keepdims=True))
    centred = values - centre
    spread = lax.optimization_barrier(jnp.mean(centred * centred, axis=-1, keepdims=True))
    return (centred * lax.rsqrt(spread + NORM_EPS)).astype(jnp.bfloat16)

def rounded_weights(exp_scores):
    return lax.optimization_barrier(exp_scores.astype(jnp.bfloat16)).astype(jnp.float32)

def reference(homolog_representation, pair_state, genuine_chain_indicator, resolved_mask, crop_positions, relative_position_table, column_query_key_value_gate, vertical_attention_projector, expansion_coefficients, contraction_coefficients, operand_duo_projector, tensor_product_projector, triangle_query_key_value_gate, triangle_bias_weight, triangle_output_weight, pair_up_weight, pair_down_weight):
    score_scale = SUBSPACE_DEPTH ** (-0.5)
    standardized_representation = layer_normalize(homolog_representation)
    reshaped_standardized = standardized_representation.reshape(ALIGNED_CHAINS * WINDOW_AMINOS, ALIGNED_FEATURES)
    linear_mapped_representation = jnp.dot(reshaped_standardized, column_query_key_value_gate, preferred_element_type=jnp.float32).astype(jnp.bfloat16)
    linear_mapped_representation = linear_mapped_representation.reshape(ALIGNED_CHAINS, WINDOW_AMINOS, 4, VERTICAL_ATTENDS, SUBSPACE_DEPTH)
    shard_residue_span = math.gcd(WINDOW_AMINOS, 16)
    residuewise_arrangement = jnp.transpose(linear_mapped_representation, (1, 0, 2, 3, 4)).reshape(WINDOW_AMINOS // shard_residue_span, shard_residue_span, ALIGNED_CHAINS, 4, VERTICAL_ATTENDS, SUBSPACE_DEPTH)
    sequence_bias = (genuine_chain_indicator.astype(jnp.float32) - 1.0) * MASK_NEGATIVE

    def column_attention(block):
        block = block.astype(jnp.float32)
        query_matrix_rows = block[:, :, 0]
        key_matrix_rows = block[:, :, 1]
        value_matrix_rows = block[:, :, 2]
        gate_values_rows = block[:, :, 3]
        scores = jnp.einsum('cshd,cthd->chst', query_matrix_rows, key_matrix_rows) * score_scale + sequence_bias
        soft_top = lax.optimization_barrier(jnp.max(scores, axis=-1, keepdims=True))
        exp_scores = jnp.exp(scores - soft_top)
        soft_total = lax.optimization_barrier(jnp.sum(exp_scores, axis=-1))
        weights = rounded_weights(exp_scores)
        mixed_out = jnp.einsum('chst,cthd->cshd', weights, value_matrix_rows) / jnp.transpose(soft_total, (0, 2, 1))[..., None]
        return (jax.nn.sigmoid(gate_values_rows) * mixed_out).astype(jnp.bfloat16)
    mixed_contributions = lax.map(column_attention, residuewise_arrangement)
    mixed_contributions = jnp.transpose(mixed_contributions.reshape(WINDOW_AMINOS, ALIGNED_CHAINS, ALIGNED_FEATURES), (1, 0, 2)).reshape(ALIGNED_CHAINS * WINDOW_AMINOS, ALIGNED_FEATURES)
    intermediate_representation = homolog_representation.astype(jnp.float32).reshape(ALIGNED_CHAINS * WINDOW_AMINOS, ALIGNED_FEATURES) + jnp.dot(mixed_contributions, vertical_attention_projector, preferred_element_type=jnp.float32)
    expanded_activation = jax.nn.relu(jnp.dot(layer_normalize(intermediate_representation), expansion_coefficients, preferred_element_type=jnp.float32)).astype(jnp.bfloat16)
    refreshed_homologs = (intermediate_representation + jnp.dot(expanded_activation, contraction_coefficients, preferred_element_type=jnp.float32)).astype(jnp.bfloat16).reshape(ALIGNED_CHAINS, WINDOW_AMINOS, ALIGNED_FEATURES)
    rel_bins = jnp.clip(crop_positions[:, None] - crop_positions[None, :], -RELPOS_MAX, RELPOS_MAX) + RELPOS_MAX
    pair_in = pair_state.astype(jnp.float32) + relative_position_table.astype(jnp.float32)[rel_bins]
    pair_norm = layer_normalize(pair_in).reshape(WINDOW_AMINOS * WINDOW_AMINOS, COUPLING_DEPTH)
    tri_proj = jnp.dot(pair_norm, triangle_query_key_value_gate, preferred_element_type=jnp.float32).astype(jnp.bfloat16)
    tri_proj = tri_proj.reshape(WINDOW_AMINOS, WINDOW_AMINOS, TRI_HEADS, 4, SUBSPACE_DEPTH)
    tri_bias = jnp.dot(pair_norm, triangle_bias_weight, preferred_element_type=jnp.float32).astype(jnp.bfloat16)
    key_mask = (resolved_mask.astype(jnp.float32) - 1.0) * MASK_NEGATIVE
    head_bias = jnp.transpose(tri_bias.reshape(WINDOW_AMINOS, WINDOW_AMINOS, TRI_HEADS), (2, 0, 1)).astype(jnp.float32) + key_mask
    chain_partitions = ALIGNED_CHAINS // CHAINS_PER_SHARD
    tensor_operand_entries = (jnp.dot(reshaped_standardized, operand_duo_projector, preferred_element_type=jnp.float32).reshape(ALIGNED_CHAINS, WINDOW_AMINOS, 2 * OPERAND_FEATURES) * genuine_chain_indicator.astype(jnp.float32)[:, None, None]).astype(jnp.bfloat16)
    left_groups = tensor_operand_entries[:, :, :OPERAND_FEATURES].reshape(chain_partitions, CHAINS_PER_SHARD, WINDOW_AMINOS, OPERAND_FEATURES)
    right_groups = tensor_operand_entries[:, :, OPERAND_FEATURES:].reshape(chain_partitions, CHAINS_PER_SHARD, WINDOW_AMINOS, OPERAND_FEATURES).astype(jnp.float32)
    sequence_total = jnp.sum(genuine_chain_indicator.astype(jnp.float32))
    block_rows = math.gcd(WINDOW_AMINOS, 8)
    proj_blocks = tri_proj.reshape(WINDOW_AMINOS // block_rows, block_rows, WINDOW_AMINOS, TRI_HEADS, 4, SUBSPACE_DEPTH)
    left_blocks = jnp.transpose(left_groups, (2, 0, 1, 3)).reshape(WINDOW_AMINOS // block_rows, block_rows, chain_partitions, CHAINS_PER_SHARD, OPERAND_FEATURES)

    def row_update(block):
        block_proj, block_left = block
        block_proj = block_proj.astype(jnp.float32)
        query_matrix_rows = block_proj[:, :, :, 0]
        key_matrix_rows = block_proj[:, :, :, 1]
        value_matrix_rows = block_proj[:, :, :, 2]
        gate_values_rows = block_proj[:, :, :, 3]
        scores = jnp.einsum('ijhd,ikhd->ihjk', query_matrix_rows, key_matrix_rows) * score_scale + head_bias
        soft_top = lax.optimization_barrier(jnp.max(scores, axis=-1, keepdims=True))
        exp_scores = jnp.exp(scores - soft_top)
        soft_total = lax.optimization_barrier(jnp.sum(exp_scores, axis=-1))
        weights = rounded_weights(exp_scores)
        mixed_out = jnp.einsum('ihjk,ikhd->ijhd', weights, value_matrix_rows) / jnp.transpose(soft_total, (0, 2, 1))[..., None]
        gated = (jax.nn.sigmoid(gate_values_rows) * mixed_out).astype(jnp.bfloat16).reshape(block_rows * WINDOW_AMINOS, COUPLING_DEPTH)
        tri_update = jnp.dot(gated, triangle_output_weight, preferred_element_type=jnp.float32).reshape(block_rows, WINDOW_AMINOS, COUPLING_DEPTH)
        outer_prod = jnp.einsum('igsc,gsje->gijce', block_left.astype(jnp.float32), right_groups).astype(jnp.bfloat16)
        projected = jnp.dot(outer_prod.reshape(chain_partitions * block_rows * WINDOW_AMINOS, OPERAND_FEATURES * OPERAND_FEATURES), tensor_product_projector, preferred_element_type=jnp.float32)
        opm_update = lax.optimization_barrier(jnp.sum(projected.reshape(chain_partitions, block_rows, WINDOW_AMINOS, COUPLING_DEPTH) / sequence_total, axis=0))
        return tri_update + opm_update
    update = lax.map(row_update, (proj_blocks, left_blocks)).reshape(WINDOW_AMINOS, WINDOW_AMINOS, COUPLING_DEPTH)
    pair_mid = (pair_in + update).reshape(WINDOW_AMINOS * WINDOW_AMINOS, COUPLING_DEPTH)
    pair_hidden = jax.nn.relu(jnp.dot(layer_normalize(pair_mid), pair_up_weight, preferred_element_type=jnp.float32)).astype(jnp.bfloat16)
    pair_updated = (pair_mid + jnp.dot(pair_hidden, pair_down_weight, preferred_element_type=jnp.float32)).astype(jnp.bfloat16).reshape(WINDOW_AMINOS, WINDOW_AMINOS, COUPLING_DEPTH)
    return (refreshed_homologs, pair_updated)
```

```python
import functools

import jax
import jax.numpy as jnp
from jax import lax
from jax.experimental import pallas as pl
from jax.experimental.pallas import tpu as pltpu
from jax.sharding import PartitionSpec as P

VERTICAL_ATTENDS = 8
TRI_HEADS = 4
SUBSPACE_DEPTH = 32
RELPOS_MAX = 32

NORM_EPS = 1e-05
MASK_NEGATIVE = 1000000000.0
LANES = 128
SUBLANES = 8
MESH = pl.DeviceIdType.MESH
F32 = jnp.float32
BF16 = jnp.bfloat16

WEIGHTS = (
    "rel", "qkvg", "vproj", "expand", "contract", "duo", "tensor", "tri", "tbias", "tout", "up", "down",
)


def normalize(values):
    centre = jnp.mean(values, axis=-1, keepdims=True)
    centred = values - centre
    spread = jnp.mean(centred * centred, axis=-1, keepdims=True)
    return (centred * lax.rsqrt(spread + NORM_EPS)).astype(BF16)


def matmul(a, b):
    return jnp.dot(a, b, preferred_element_type=F32)


def matmul_nt(a, b):
    return lax.dot_general(a, b, (((1,), (1,)), ((), ())), preferred_element_type=F32)


def matmul_tn(a, b):
    return lax.dot_general(a, b, (((0,), (0,)), ((), ())), preferred_element_type=F32)


def softmax_rows(scores):
    exp_scores = jnp.exp(scores - jnp.max(scores, axis=-1, keepdims=True))
    return (exp_scores / jnp.sum(exp_scores, axis=-1, keepdims=True)).astype(BF16)


def head_stack(values, heads):
    rows, width = values.shape
    lane = lax.broadcasted_iota(jnp.int32, (rows, width), 1) // SUBSPACE_DEPTH
    return jnp.concatenate(
        [jnp.where(lane == h, values, 0.0) for h in range(heads)], axis=0
    ).astype(BF16)


def head_merge(stacked, heads):
    rows, width = stacked.shape[0] // heads, stacked.shape[1]
    lane = lax.broadcasted_iota(jnp.int32, (rows, width), 1) // SUBSPACE_DEPTH
    total = jnp.zeros((rows, width), F32)
    for h in range(heads):
        total = jnp.where(lane == h, stacked[h * rows : (h + 1) * rows], total)
    return total


def kernel(sizes, *refs):
    n_pb, n_a, n_b, n_c = sizes
    x_ref, pair_ref, chain_ref, res_ref, pos_ref, pos_smem = refs[:6]
    hbm = dict(zip(WEIGHTS, refs[6:18]))
    out_msa, out_pair = refs[18:20]
    w = dict(zip(WEIGHTS, refs[20:32]))
    (xg, pg, xn_s, k_s, v_s, left_s, msg_s, gather, bias_s, pairin_s, tkv_s, wf_s, wp_s, opm_s,
     bt_s, wsem, sx, rx, sp, rp, s1, r1, s2, r2) = refs[32:]
    rows_i, seqs, width = x_ref.shape
    cells, pwidth = pair_ref.shape
    cols = cells // rows_i
    residues = res_ref.shape[1]
    n_as = n_a // n_pb
    n_src = n_as * n_b * n_c
    hpl = LANES // SUBSPACE_DEPTH
    factor = w["duo"].shape[1] // 2
    eparts = factor // SUBLANES
    seq_blocks = n_pb * eparts * seqs // LANES
    bias_blocks = -(-residues // LANES)
    factor_rows = rows_i * SUBLANES

    grp = lax.axis_index("grp")
    row = lax.axis_index("row")
    c_me = lax.axis_index("br")
    p_me = lax.axis_index("pb")
    a_me, b_me = row // n_b, row % n_b
    scale = SUBSPACE_DEPTH ** (-0.5)

    def device(a, b, c, p):
        return (grp, a * n_b + b, c, p)

    loads = {}
    for n, name in enumerate(WEIGHTS):
        loads[name] = pltpu.make_async_copy(hbm[name], w[name], wsem.at[n])
    for name in ("qkvg", "rel", "tri", "tbias", "duo", "tensor", "vproj", "expand", "contract", "tout", "up", "down"):
        loads[name].start()

    barrier = pltpu.get_barrier_semaphore()
    for d in range(1, n_pb):
        pl.semaphore_signal(barrier, inc=1, device_id=device(a_me, b_me, c_me, (p_me + d) % n_pb), device_id_type=MESH)
    for d in range(1, n_a):
        pl.semaphore_signal(barrier, inc=1, device_id=device((a_me + d) % n_a, b_me, c_me, p_me), device_id_type=MESH)
    mates = [(db, dc) for db in range(n_b) for dc in range(n_c) if (db, dc) != (0, 0)]
    for db, dc in mates:
        pl.semaphore_signal(
            barrier, inc=1, device_id=device(a_me, (b_me + db) % n_b, (c_me + dc) % n_c, p_me), device_id_type=MESH
        )
    pl.semaphore_wait(barrier, n_pb - 1 + n_a - 1 + len(mates))

    exchange = []
    for d in range(1, n_pb):
        peer = device(a_me, b_me, c_me, (p_me + d) % n_pb)
        exchange.append((
            pltpu.make_async_remote_copy(
                src_ref=pair_ref, dst_ref=pg.at[n_pb - d], send_sem=sp.at[d], recv_sem=rp.at[n_pb - d],
                device_id=peer, device_id_type=MESH),
            pltpu.make_async_remote_copy(
                src_ref=x_ref, dst_ref=xg.at[n_pb - d], send_sem=sx.at[d], recv_sem=rx.at[n_pb - d],
                device_id=peer, device_id_type=MESH),
        ))
    for copy, _ in exchange:
        copy.start()
    for _, copy in exchange:
        copy.start()

    x_own = x_ref[...].reshape(rows_i * seqs, width)
    xn_own = normalize(x_own.astype(F32))
    loads["qkvg"].wait()
    proj = matmul(xn_own, w["qkvg"][...])
    query = proj[:, :width].astype(BF16).astype(F32)
    gate = jax.nn.sigmoid(proj[:, 3 * width :].astype(BF16).astype(F32))
    xn_s[p_me] = xn_own
    k_s[p_me] = proj[:, width : 2 * width].astype(BF16)
    v_s[p_me] = proj[:, 2 * width : 3 * width].astype(BF16)

    loads["rel"].wait()
    loads["tri"].wait()
    loads["tbias"].wait()
    loads["duo"].wait()
    loads["tensor"].wait()
    tri_w = w["tri"][...].astype(F32)
    tri_w = jnp.concatenate(
        [
            tri_w[:, (h * 4 + kind) * SUBSPACE_DEPTH : (h * 4 + kind + 1) * SUBSPACE_DEPTH]
            for kind in range(4)
            for h in range(TRI_HEADS)
        ],
        axis=1,
    ).astype(BF16)
    wf_s[...] = w["tensor"][...].astype(F32)
    for e in range(factor):
        wp_s[e * factor : (e + 1) * factor, :] = wf_s[pl.ds(e, factor, stride=factor), :].astype(BF16)
    duo = w["duo"][...].astype(F32)
    left_w = jnp.concatenate([duo[:, :factor]] * eparts, axis=1).astype(BF16)
    right_w = jnp.transpose(duo)[factor:].astype(BF16)

    row_first = (row * n_c + c_me) * rows_i
    bins = 2 * RELPOS_MAX + 1

    def relpos(i, positions):
        offset = jnp.clip(pos_smem[row_first + i] - positions, -RELPOS_MAX, RELPOS_MAX) + RELPOS_MAX
        hot = lax.broadcasted_iota(jnp.int32, (bins, positions.shape[1]), 0) == offset
        return matmul_tn(jnp.where(hot, 1.0, 0.0).astype(BF16), w["rel"][...])

    relpos_all = [relpos(i, pos_ref[...]) for i in range(rows_i)]
    for i in range(rows_i):
        for p in range(n_pb):
            pairin_s[p, i * cols : (i + 1) * cols] = relpos_all[i][p * cols : (p + 1) * cols]
    for slot in range(1, n_pb):
        exchange[n_pb - slot - 1][0].wait_recv()
    for d in range(n_pb):
        p = (p_me + d) % n_pb
        held = pair_ref[...] if d == 0 else pg[d]
        total = pairin_s[p] + held.astype(F32)
        pairin_s[p] = total
        pn = normalize(total)
        tproj = matmul(pn, tri_w)
        tkv_s[p] = tproj[:, pwidth : 3 * pwidth].astype(BF16)
        bt = lax.dot_general(
            w["tbias"][...], pn, (((0,), (1,)), ((), ())), preferred_element_type=F32
        )
        bt_s[p] = bt
        if d == 0:
            tri_q = tproj[:, :pwidth].astype(BF16).astype(F32)
            tri_gate = jax.nn.sigmoid(tproj[:, 3 * pwidth :].astype(BF16).astype(F32))

    for slot in range(1, n_pb):
        exchange[n_pb - slot - 1][1].wait_recv()
    for d in range(1, n_pb):
        p = (p_me + d) % n_pb
        xn = normalize(xg[d].reshape(rows_i * seqs, width).astype(F32))
        xn_s[p] = xn
        kv = matmul(xn, w["qkvg"][:, width : 3 * width])
        k_s[p] = kv[:, :width].astype(BF16)
        v_s[p] = kv[:, width:].astype(BF16)

    a_slot = a_me - p_me * n_as
    is_source = jnp.logical_and(a_slot >= 0, a_slot < n_as)
    chain = chain_ref[...].astype(F32)

    def slot_of(a, b, c):
        return (a * n_b + b) * n_c + c

    first = [
        pltpu.make_async_remote_copy(
            src_ref=msg_s, dst_ref=gather.at[slot_of(a_slot, b_me, c_me)], send_sem=s1.at[d],
            recv_sem=r1.at[a_slot], device_id=device((a_me + d) % n_a, b_me, c_me, p_me), device_id_type=MESH)
        for d in range(1, n_a)
    ]

    @pl.when(is_source)
    def _():
        per_p = []
        for p in range(n_pb):
            rt = matmul_nt(right_w, xn_s[p])
            rt = rt * jnp.concatenate([chain[:, p * seqs : (p + 1) * seqs]] * rows_i, axis=1)
            per_p.append(rt)
        for p in range(n_pb):
            for j in range(rows_i):
                line = jnp.concatenate(
                    [
                        per_p[p][q * SUBLANES : (q + 1) * SUBLANES, j * seqs : (j + 1) * seqs]
                        for q in range(eparts)
                    ],
                    axis=1,
                )
                blocks = line.shape[1] // LANES
                for b in range(blocks):
                    bt_at = (p * blocks + b) * factor_rows + j * SUBLANES
                    opm_s[bt_at : bt_at + SUBLANES, :] = line[:, b * LANES : (b + 1) * LANES]
        base = seq_blocks * factor_rows
        for i in range(rows_i):
            line = jnp.concatenate(
                [bt_s[p][:, i * cols : (i + 1) * cols] for p in range(n_pb)], axis=1
            )
            if residues < LANES:
                line = jnp.concatenate([line, jnp.zeros((TRI_HEADS, LANES - residues), F32)], axis=1)
            for b in range(bias_blocks):
                at = base + b * rows_i * TRI_HEADS
                for h in range(TRI_HEADS):
                    opm_s[at + h * rows_i + i : at + h * rows_i + i + 1, :] = line[h : h + 1, b * LANES : (b + 1) * LANES]
        msg_s[...] = opm_s[: msg_s.shape[0], :].astype(BF16)
        for copy in first:
            copy.start()
        gather[slot_of(a_slot, b_me, c_me)] = msg_s[...]

    lane_part = lax.broadcasted_iota(jnp.int32, (seqs, LANES), 1) // factor
    for p in range(n_pb):
        left4 = matmul(xn_s[p], left_w)
        for i in range(rows_i):
            block = left4[i * seqs : (i + 1) * seqs]
            for q in range(eparts):
                left_s[(p * eparts + q) * seqs : (p * eparts + q + 1) * seqs, i * LANES : (i + 1) * LANES] = (
                    jnp.where(lane_part == q, block, 0.0).astype(BF16)
                )

    seq_bias = (chain - 1.0) * MASK_NEGATIVE
    mixed = []
    for r in range(rows_i):
        span = slice(r * seqs, (r + 1) * seqs)
        keys = jnp.concatenate([k_s[p, span, :] for p in range(n_pb)], axis=0)
        values = jnp.concatenate([v_s[p, span, :] for p in range(n_pb)], axis=0)
        scores = matmul_nt(head_stack(query[span], VERTICAL_ATTENDS), keys) * scale + seq_bias
        weighted = matmul(softmax_rows(scores), values)
        mixed.append((gate[span] * head_merge(weighted, VERTICAL_ATTENDS)).astype(BF16))

    second = []
    for a in range(n_as):
        slot = slot_of(a, b_me, c_me)

        @pl.when(a_slot != a)
        def _():
            pltpu.make_async_remote_copy(
                src_ref=msg_s, dst_ref=gather.at[slot], send_sem=s1.at[0], recv_sem=r1.at[a],
                device_id=device((a_me + 1) % n_a, b_me, c_me, p_me), device_id_type=MESH).wait_recv()

        for m, (db, dc) in enumerate(mates):
            copy = pltpu.make_async_remote_copy(
                src_ref=gather.at[slot], dst_ref=gather.at[slot], send_sem=s2.at[a * len(mates) + m],
                recv_sem=r2.at[slot],
                device_id=device(a_me, (b_me + db) % n_b, (c_me + dc) % n_c, p_me), device_id_type=MESH)
            copy.start()
            second.append(copy)

    loads["vproj"].wait()
    mid = x_own.astype(F32) + matmul(jnp.concatenate(mixed, axis=0), w["vproj"][...])
    loads["expand"].wait()
    hidden = jnp.maximum(matmul(normalize(mid), w["expand"][...]), 0.0).astype(BF16)
    loads["contract"].wait()
    fresh = mid + matmul(hidden, w["contract"][...])
    out_msa[...] = fresh.astype(BF16).reshape(out_msa.shape)

    for a in range(n_as):
        for db, dc in mates:
            slot = slot_of(a, (b_me + db) % n_b, (c_me + dc) % n_c)
            pltpu.make_async_remote_copy(
                src_ref=gather.at[slot], dst_ref=gather.at[slot], send_sem=s2.at[0], recv_sem=r2.at[slot],
                device_id=device(a_me, (b_me + db) % n_b, (c_me + dc) % n_c, p_me), device_id_type=MESH).wait_recv()

    right_all = jnp.concatenate(
        [
            jnp.concatenate(
                [gather[s, b * factor_rows : (b + 1) * factor_rows, :] for b in range(seq_blocks)], axis=1
            )
            for s in range(n_src)
        ],
        axis=0,
    )
    outer = matmul(right_all, left_s[...])
    opm_s[: rows_i * cols * SUBLANES, :] = jnp.concatenate(
        [outer[:, i * LANES : (i + 1) * LANES] for i in range(rows_i)], axis=0
    )
    lhs = jnp.concatenate(
        [opm_s[pl.ds(e, cells, stride=SUBLANES), :].astype(BF16) for e in range(SUBLANES)], axis=1
    )
    rhs = jnp.concatenate(
        [
            wp_s[(q * SUBLANES + e) * factor : (q * SUBLANES + e + 1) * factor, :]
            for e in range(SUBLANES)
            for q in range(eparts)
        ],
        axis=0,
    )
    opm = matmul(lhs, rhs) / jnp.sum(chain)

    base = seq_blocks * factor_rows
    for s in range(n_src):
        part = jnp.concatenate(
            [
                gather[s, base + b * rows_i * TRI_HEADS : base + (b + 1) * rows_i * TRI_HEADS, :]
                for b in range(bias_blocks)
            ],
            axis=1,
        ).astype(F32)
        for h in range(TRI_HEADS):
            bias_s[h * cols + s * rows_i : h * cols + (s + 1) * rows_i, :] = part[h * rows_i : (h + 1) * rows_i, :]
    bias = bias_s[:, :residues] + (res_ref[...].astype(F32) - 1.0) * MASK_NEGATIVE
    tri_mixed = []
    for i in range(rows_i):
        span = slice(i * cols, (i + 1) * cols)
        keys = jnp.concatenate([tkv_s[p, span, :pwidth] for p in range(n_pb)], axis=0)
        values = jnp.concatenate([tkv_s[p, span, pwidth:] for p in range(n_pb)], axis=0)
        scores = matmul_nt(head_stack(tri_q[span], TRI_HEADS), keys) * scale + bias
        weighted = matmul(softmax_rows(scores), values)
        tri_mixed.append((tri_gate[span] * head_merge(weighted, TRI_HEADS)).astype(BF16))
    loads["tout"].wait()
    pair_mid = pairin_s[p_me] + matmul(jnp.concatenate(tri_mixed, axis=0), w["tout"][...]) + opm
    loads["up"].wait()
    pair_hidden = jnp.maximum(matmul(normalize(pair_mid), w["up"][...]), 0.0).astype(BF16)
    loads["down"].wait()
    out_pair[...] = (pair_mid + matmul(pair_hidden, w["down"][...])).astype(BF16)

    for copies in exchange:
        for copy in copies:
            copy.wait_send()
    for copy in second:
        copy.wait_send()

    @pl.when(is_source)
    def _():
        for copy in first:
            copy.wait_send()


def on_device(sizes, x, pair, chain, resolved, positions, *weights):
    seqs, rows_i, width = x.shape
    cols, pwidth = pair.shape[1:]
    n_pb, n_a, n_b, n_c = sizes
    cells = rows_i * cols
    chains, residues = chain.shape[0], resolved.shape[0]
    n_as = n_a // n_pb
    n_src = n_as * n_b * n_c
    factor = weights[5].shape[1] // 2
    eparts = factor // SUBLANES
    factor_rows = rows_i * SUBLANES
    bias_blocks = -(-residues // LANES)
    msg_rows = n_pb * eparts * seqs // LANES * factor_rows + bias_blocks * rows_i * TRI_HEADS
    mates = n_b * n_c - 1
    vmem = pl.BlockSpec(memory_space=pltpu.VMEM)
    hbm = pl.BlockSpec(memory_space=pl.ANY)
    dma = pltpu.SemaphoreType.DMA
    x_t = jnp.transpose(x, (1, 0, 2))
    msa, pair_out = pl.pallas_call(
        functools.partial(kernel, sizes),
        out_shape=(
            jax.ShapeDtypeStruct((rows_i, seqs, width), BF16),
            jax.ShapeDtypeStruct((cells, pwidth), BF16),
        ),
        in_specs=[vmem] * 5 + [pl.BlockSpec(memory_space=pltpu.SMEM)] + [hbm] * len(weights),
        out_specs=(vmem, vmem),
        scratch_shapes=[pltpu.VMEM(v.shape, v.dtype) for v in weights]
        + [
            pltpu.VMEM((n_pb, rows_i, seqs, width), BF16),
            pltpu.VMEM((n_pb, cells, pwidth), BF16),
            pltpu.VMEM((n_pb, rows_i * seqs, width), BF16),
            pltpu.VMEM((n_pb, rows_i * seqs, width), BF16),
            pltpu.VMEM((n_pb, rows_i * seqs, width), BF16),
            pltpu.VMEM((n_pb * eparts * seqs, rows_i * LANES), BF16),
            pltpu.VMEM((msg_rows, LANES), BF16),
            pltpu.VMEM((n_src, msg_rows, LANES), BF16),
            pltpu.VMEM((TRI_HEADS * cols, bias_blocks * LANES), F32),
            pltpu.VMEM((n_pb, cells, pwidth), F32),
            pltpu.VMEM((n_pb, cells, 2 * pwidth), BF16),
            pltpu.VMEM(weights[6].shape, F32),
            pltpu.VMEM(weights[6].shape, BF16),
            pltpu.VMEM((max(cells * SUBLANES, msg_rows), LANES), F32),
            pltpu.VMEM((n_pb, TRI_HEADS, cells), F32),
            dma((len(weights),)),
            dma((n_pb,)),
            dma((n_pb,)),
            dma((n_pb,)),
            dma((n_pb,)),
            dma((n_a,)),
            dma((n_as,)),
            dma((n_as * mates,)),
            dma((n_src,)),
        ],
        compiler_params=pltpu.CompilerParams(
            collective_id=0, has_side_effects=True, vmem_limit_bytes=40 * 1024 * 1024
        ),
    )(
        x_t,
        pair.reshape(cells, pwidth),
        chain.reshape(1, chains),
        resolved.reshape(1, residues),
        positions.reshape(1, residues),
        positions,
        *weights,
    )
    return jnp.transpose(msa, (1, 0, 2)), pair_out.reshape(rows_i, cols, pwidth)


def solution(mesh):
    n_row, n_br, n_pb = mesh.shape["row"], mesh.shape["br"], mesh.shape["pb"]
    n_b = 2 if n_row % (2 * n_pb) == 0 else 1
    sizes = (n_pb, n_row // n_b, n_b, n_br)
    return jax.shard_map(
        functools.partial(on_device, sizes),
        mesh=mesh,
        in_specs=(
            P(("grp", "pb"), ("row", "br"), None),
            P(("grp", "row", "br"), "pb", None),
            P("grp"),
            P("grp"),
            P("grp"),
        )
        + (P(),) * 12,
        out_specs=(P(("grp", "pb"), ("row", "br"), None), P(("grp", "row", "br"), "pb", None)),
        check_vma=False,
    )
```

```python
import functools

import jax
import jax.numpy as jnp
from jax import lax
from jax.experimental import pallas as pl
from jax.experimental.pallas import tpu as pltpu
from jax.sharding import PartitionSpec as P

VERTICAL_ATTENDS = 8
TRI_HEADS = 4
SUBSPACE_DEPTH = 32
RELPOS_MAX = 32

NORM_EPS = 1e-05
MASK_NEGATIVE = 1000000000.0
LANES = 128
SUBLANES = 8
MESH = pl.DeviceIdType.MESH
F32 = jnp.float32
BF16 = jnp.bfloat16

WEIGHTS = (
    "rel", "qkvg", "vproj", "expand", "contract", "duo", "tensor", "tri", "tbias", "tout", "up", "down",
)


INPUTS = (
    "chain", "duo", "positions", "scalars", "rel", "pair", "tbias", "qkvg", "tri", "tensor",
    "vproj", "expand", "contract", "resolved", "tout", "up", "down",
)


def normalize(values):
    centre = jnp.mean(values, axis=-1, keepdims=True)
    centred = values - centre
    spread = jnp.mean(centred * centred, axis=-1, keepdims=True)
    return (centred * lax.rsqrt(spread + NORM_EPS)).astype(BF16)


def matmul(a, b):
    return jnp.dot(a, b, preferred_element_type=F32)


def matmul_nt(a, b):
    return lax.dot_general(a, b, (((1,), (1,)), ((), ())), preferred_element_type=F32)


def matmul_tn(a, b):
    return lax.dot_general(a, b, (((0,), (0,)), ((), ())), preferred_element_type=F32)


def softmax_rows(scores):
    exp_scores = jnp.exp(scores - jnp.max(scores, axis=-1, keepdims=True))
    return (exp_scores * (1.0 / jnp.sum(exp_scores, axis=-1, keepdims=True))).astype(BF16)


def head_stack(values, heads):
    rows, width = values.shape
    lane = lax.broadcasted_iota(jnp.int32, (rows, width), 1) // SUBSPACE_DEPTH
    return jnp.concatenate(
        [jnp.where(lane == h, values, 0.0) for h in range(heads)], axis=0
    ).astype(BF16)


def head_merge(stacked, heads):
    rows, width = stacked.shape[0] // heads, stacked.shape[1]
    lane = lax.broadcasted_iota(jnp.int32, (rows, width), 1) // SUBSPACE_DEPTH
    total = jnp.zeros((rows, width), F32)
    for h in range(heads):
        total = jnp.where(lane == h, stacked[h * rows : (h + 1) * rows], total)
    return total


def kernel(sizes, *refs):
    n_pb, n_a, n_b, n_c = sizes
    x_ref = refs[0]
    hbm = dict(zip(INPUTS, refs[1 : 1 + len(INPUTS)]))
    out_msa, out_pair = refs[1 + len(INPUTS) : 3 + len(INPUTS)]
    w = dict(zip(INPUTS, refs[3 + len(INPUTS) : 3 + 2 * len(INPUTS)]))
    (xg, pg, xn_s, k_s, v_s, left_s, msg_s, gather, bias_s, pairin_s, tkv_s, wf_s, wp_s, opm_s,
     wsem, sx, rx, sp, rp, s1, r1, s2, r2) = refs[3 + 2 * len(INPUTS) :]
    pair_ref = w["pair"]
    rows_i, seqs, width = x_ref.shape
    cells, pwidth = pair_ref.shape
    cols = cells // rows_i
    residues = w["resolved"].shape[1]
    n_as = n_a // n_pb
    n_src = n_as * n_b * n_c
    factor = w["duo"].shape[0] // 2
    eparts = factor // SUBLANES
    seq_blocks = eparts * seqs // LANES
    factor_rows = rows_i * SUBLANES
    base = seq_blocks * factor_rows

    grp = lax.axis_index("grp")
    row = lax.axis_index("row")
    c_me = lax.axis_index("br")
    p_me = lax.axis_index("pb")
    a_me, b_me = row // n_b, row % n_b
    scale = SUBSPACE_DEPTH ** (-0.5)

    def device(a, b, c, p):
        return (grp, a * n_b + b, c, p)

    loads = {}
    for n, name in enumerate(INPUTS):
        loads[name] = pltpu.make_async_copy(hbm[name], w[name], wsem.at[n])
    for name in INPUTS:
        loads[name].start()

    barrier = pltpu.get_barrier_semaphore()
    line = [(da, dp) for da in range(n_a) for dp in range(n_pb) if (da, dp) != (0, 0)]
    mates = [(db, dc) for db in range(n_b) for dc in range(n_c) if (db, dc) != (0, 0)]
    for da, dp in line:
        pl.semaphore_signal(
            barrier, inc=1, device_id=device((a_me + da) % n_a, b_me, c_me, (p_me + dp) % n_pb), device_id_type=MESH
        )
    for db, dc in mates:
        pl.semaphore_signal(
            barrier, inc=1, device_id=device(a_me, (b_me + db) % n_b, (c_me + dc) % n_c, p_me), device_id_type=MESH
        )

    x_own = x_ref[...].reshape(rows_i * seqs, width)
    xn_own = normalize(x_own.astype(F32))
    xn_s[p_me] = xn_own
    loads["chain"].wait()
    loads["duo"].wait()
    chain = w["chain"][...].astype(F32)
    own_chain = jnp.zeros((1, seqs), F32)
    for p in range(n_pb):
        own_chain = jnp.where(p_me == p, chain[:, p * seqs : (p + 1) * seqs], own_chain)
    rt = matmul_nt(w["duo"][factor:, :], xn_own) * jnp.concatenate([own_chain] * rows_i, axis=1)
    for j in range(rows_i):
        parts = jnp.concatenate(
            [rt[q * SUBLANES : (q + 1) * SUBLANES, j * seqs : (j + 1) * seqs] for q in range(eparts)], axis=1
        )
        for b in range(seq_blocks):
            at = b * factor_rows + j * SUBLANES
            opm_s[at : at + SUBLANES, :] = parts[:, b * LANES : (b + 1) * LANES]

    row_first = (row * n_c + c_me) * rows_i
    bins = 2 * RELPOS_MAX + 1
    loads["positions"].wait()
    loads["scalars"].wait()
    loads["rel"].wait()
    for i in range(rows_i):
        offset = jnp.clip(w["scalars"][row_first + i] - w["positions"][...], -RELPOS_MAX, RELPOS_MAX) + RELPOS_MAX
        hot = lax.broadcasted_iota(jnp.int32, (bins, residues), 0) == offset
        added = matmul_tn(jnp.where(hot, 1.0, 0.0).astype(BF16), w["rel"][...])
        for p in range(n_pb):
            pairin_s[p, i * cols : (i + 1) * cols] = added[p * cols : (p + 1) * cols]
    loads["pair"].wait()
    pair_in = pairin_s[p_me] + pair_ref[...].astype(F32)
    pn_own = normalize(pair_in)
    loads["tbias"].wait()
    bt = matmul_nt(w["tbias"][...], pn_own)
    for i in range(rows_i):
        for h in range(TRI_HEADS):
            at = base + h * rows_i + i
            opm_s[at : at + 1, :cols] = bt[h : h + 1, i * cols : (i + 1) * cols]
    msg_s[...] = opm_s[: msg_s.shape[0], :].astype(BF16)

    pl.semaphore_wait(barrier, len(line) + len(mates))

    p_to, a_slot = a_me // n_as, a_me % n_as
    stays = p_to == p_me

    def slot_of(a, b, c):
        return (a * n_b + b) * n_c + c

    def first(d):
        return pltpu.make_async_remote_copy(
            src_ref=msg_s, dst_ref=gather.at[slot_of(a_slot, b_me, c_me), p_me], send_sem=s1.at[d],
            recv_sem=r1.at[a_slot * n_pb + p_me], device_id=device((a_me + d) % n_a, b_me, c_me, p_to),
            device_id_type=MESH)

    for d in range(1, n_a):
        first(d).start()

    @pl.when(jnp.logical_not(stays))
    def _():
        first(0).start()

    @pl.when(stays)
    def _():
        gather[slot_of(a_slot, b_me, c_me), p_me] = msg_s[...]

    exchange = []
    for d in range(1, n_pb):
        peer = device(a_me, b_me, c_me, (p_me + d) % n_pb)
        exchange.append((
            pltpu.make_async_remote_copy(
                src_ref=pair_ref, dst_ref=pg.at[n_pb - d], send_sem=sp.at[d], recv_sem=rp.at[n_pb - d],
                device_id=peer, device_id_type=MESH),
            pltpu.make_async_remote_copy(
                src_ref=x_ref, dst_ref=xg.at[n_pb - d], send_sem=sx.at[d], recv_sem=rx.at[n_pb - d],
                device_id=peer, device_id_type=MESH),
        ))
    for copy, _ in exchange:
        copy.start()
    for _, copy in exchange:
        copy.start()

    loads["qkvg"].wait()
    proj = matmul(xn_own, w["qkvg"][...])
    query = proj[:, :width].astype(BF16).astype(F32)
    gate = jax.nn.sigmoid(proj[:, 3 * width :].astype(BF16).astype(F32))
    k_s[p_me] = proj[:, width : 2 * width].astype(BF16)
    v_s[p_me] = proj[:, 2 * width : 3 * width].astype(BF16)

    loads["tri"].wait()
    tri_w = w["tri"][...].astype(F32)
    tri_w = jnp.concatenate(
        [
            tri_w[:, (h * 4 + kind) * SUBSPACE_DEPTH : (h * 4 + kind + 1) * SUBSPACE_DEPTH]
            for kind in range(4)
            for h in range(TRI_HEADS)
        ],
        axis=1,
    ).astype(BF16)
    tproj = matmul(pn_own, tri_w)
    tkv_s[p_me] = tproj[:, pwidth : 3 * pwidth].astype(BF16)
    tri_q = tproj[:, :pwidth].astype(BF16).astype(F32)
    tri_gate = jax.nn.sigmoid(tproj[:, 3 * pwidth :].astype(BF16).astype(F32))
    loads["tensor"].wait()
    wf_s[...] = w["tensor"][...].astype(F32)
    for e in range(SUBLANES):
        for q in range(eparts):
            at = (e * eparts + q) * factor
            wp_s[at : at + factor, :] = wf_s[pl.ds(q * SUBLANES + e, factor, stride=factor), :].astype(BF16)

    for slot in range(1, n_pb):
        exchange[n_pb - slot - 1][0].wait_recv()
    for d in range(1, n_pb):
        p = (p_me + d) % n_pb
        pn = normalize(pairin_s[p] + pg[d].astype(F32))
        tkv_s[p] = matmul(pn, tri_w[:, pwidth : 3 * pwidth]).astype(BF16)

    second = []
    for a in range(n_as):
        slot = slot_of(a, b_me, c_me)
        for p in range(n_pb):
            here = jnp.logical_and(stays, jnp.logical_and(a_slot == a, p_me == p))

            @pl.when(jnp.logical_not(here))
            def _():
                pltpu.make_async_remote_copy(
                    src_ref=msg_s, dst_ref=gather.at[slot, p], send_sem=s1.at[0], recv_sem=r1.at[a * n_pb + p],
                    device_id=device((a_me + 1) % n_a, b_me, c_me, p_me), device_id_type=MESH).wait_recv()

        for m, (db, dc) in enumerate(mates):
            copy = pltpu.make_async_remote_copy(
                src_ref=gather.at[slot], dst_ref=gather.at[slot], send_sem=s2.at[a * len(mates) + m],
                recv_sem=r2.at[slot],
                device_id=device(a_me, (b_me + db) % n_b, (c_me + dc) % n_c, p_me), device_id_type=MESH)
            copy.start()
            second.append(copy)

    for slot in range(1, n_pb):
        exchange[n_pb - slot - 1][1].wait_recv()
    for d in range(1, n_pb):
        p = (p_me + d) % n_pb
        xn = normalize(xg[d].reshape(rows_i * seqs, width).astype(F32))
        xn_s[p] = xn
        kv = matmul(xn, w["qkvg"][:, width : 3 * width])
        k_s[p] = kv[:, :width].astype(BF16)
        v_s[p] = kv[:, width:].astype(BF16)

    left_w = jnp.concatenate([w["duo"][:factor, :]] * eparts, axis=0)
    lane_part = lax.broadcasted_iota(jnp.int32, (seqs, LANES), 1) // factor
    for p in range(n_pb):
        left4 = matmul_nt(xn_s[p], left_w)
        for i in range(rows_i):
            block = left4[i * seqs : (i + 1) * seqs]
            for q in range(eparts):
                left_s[(p * eparts + q) * seqs : (p * eparts + q + 1) * seqs, i * LANES : (i + 1) * LANES] = (
                    jnp.where(lane_part == q, block, 0.0).astype(BF16)
                )

    seq_bias = (chain - 1.0) * MASK_NEGATIVE
    mixed = []
    for r in range(rows_i):
        span = slice(r * seqs, (r + 1) * seqs)
        keys = jnp.concatenate([k_s[p, span, :] for p in range(n_pb)], axis=0)
        values = jnp.concatenate([v_s[p, span, :] for p in range(n_pb)], axis=0)
        scores = matmul_nt(head_stack(query[span], VERTICAL_ATTENDS), keys) * scale + seq_bias
        weighted = matmul(softmax_rows(scores), values)
        mixed.append((gate[span] * head_merge(weighted, VERTICAL_ATTENDS)).astype(BF16))

    loads["vproj"].wait()
    mid = x_own.astype(F32) + matmul(jnp.concatenate(mixed, axis=0), w["vproj"][...])
    loads["expand"].wait()
    hidden = jnp.maximum(matmul(normalize(mid), w["expand"][...]), 0.0).astype(BF16)
    loads["contract"].wait()
    fresh = mid + matmul(hidden, w["contract"][...])
    out_msa[...] = fresh.astype(BF16).reshape(out_msa.shape)

    for a in range(n_as):
        for db, dc in mates:
            slot = slot_of(a, (b_me + db) % n_b, (c_me + dc) % n_c)
            pltpu.make_async_remote_copy(
                src_ref=gather.at[slot], dst_ref=gather.at[slot], send_sem=s2.at[0], recv_sem=r2.at[slot],
                device_id=device(a_me, (b_me + db) % n_b, (c_me + dc) % n_c, p_me), device_id_type=MESH).wait_recv()

    right_all = jnp.concatenate(
        [
            jnp.concatenate(
                [
                    gather[s, p, b * factor_rows : (b + 1) * factor_rows, :]
                    for p in range(n_pb)
                    for b in range(seq_blocks)
                ],
                axis=1,
            )
            for s in range(n_src)
        ],
        axis=0,
    )
    outer = matmul(right_all, left_s[...])
    opm_s[: cells * SUBLANES, :] = jnp.concatenate(
        [outer[:, i * LANES : (i + 1) * LANES] for i in range(rows_i)], axis=0
    )
    lhs = jnp.concatenate(
        [opm_s[pl.ds(e, cells, stride=SUBLANES), :].astype(BF16) for e in range(SUBLANES)], axis=1
    )
    opm = matmul(lhs, wp_s[...]) / jnp.sum(chain)

    for s in range(n_src):
        part = jnp.concatenate(
            [gather[s, p, base : base + rows_i * TRI_HEADS, :].astype(F32)[:, :cols] for p in range(n_pb)], axis=1
        )
        for h in range(TRI_HEADS):
            bias_s[h * cols + s * rows_i : h * cols + (s + 1) * rows_i, :] = part[h * rows_i : (h + 1) * rows_i, :]
    loads["resolved"].wait()
    bias = bias_s[...] + (w["resolved"][...].astype(F32) - 1.0) * MASK_NEGATIVE
    tri_mixed = []
    for i in range(rows_i):
        span = slice(i * cols, (i + 1) * cols)
        keys = jnp.concatenate([tkv_s[p, span, :pwidth] for p in range(n_pb)], axis=0)
        values = jnp.concatenate([tkv_s[p, span, pwidth:] for p in range(n_pb)], axis=0)
        scores = matmul_nt(head_stack(tri_q[span], TRI_HEADS), keys) * scale + bias
        weighted = matmul(softmax_rows(scores), values)
        tri_mixed.append((tri_gate[span] * head_merge(weighted, TRI_HEADS)).astype(BF16))
    loads["tout"].wait()
    pair_mid = pair_in + matmul(jnp.concatenate(tri_mixed, axis=0), w["tout"][...]) + opm
    loads["up"].wait()
    pair_hidden = jnp.maximum(matmul(normalize(pair_mid), w["up"][...]), 0.0).astype(BF16)
    loads["down"].wait()
    out_pair[...] = (pair_mid + matmul(pair_hidden, w["down"][...])).astype(BF16)

    for copies in exchange:
        for copy in copies:
            copy.wait_send()
    for copy in second:
        copy.wait_send()
    for d in range(1, n_a):
        first(d).wait_send()

    @pl.when(jnp.logical_not(stays))
    def _():
        first(0).wait_send()


def on_device(sizes, x, pair, chain, resolved, positions, *weights):
    seqs, rows_i, width = x.shape
    cols, pwidth = pair.shape[1:]
    n_pb, n_a, n_b, n_c = sizes
    cells = rows_i * cols
    chains, residues = chain.shape[0], resolved.shape[0]
    n_as = n_a // n_pb
    n_src = n_as * n_b * n_c
    arrays = dict(zip(WEIGHTS, weights))
    arrays["duo"] = arrays["duo"].T
    arrays["tbias"] = arrays["tbias"].T
    arrays["pair"] = pair.reshape(cells, pwidth)
    arrays["chain"] = chain.reshape(1, chains)
    arrays["resolved"] = resolved.reshape(1, residues)
    arrays["positions"] = positions.reshape(1, residues)
    arrays["scalars"] = positions
    inputs = [arrays[name] for name in INPUTS]
    factor = arrays["duo"].shape[0] // 2
    eparts = factor // SUBLANES
    msg_rows = eparts * seqs // LANES * rows_i * SUBLANES + rows_i * TRI_HEADS
    mates = n_b * n_c - 1
    vmem = pl.BlockSpec(memory_space=pltpu.VMEM)
    dma = pltpu.SemaphoreType.DMA
    x_t = jnp.transpose(x, (1, 0, 2))
    msa, pair_out = pl.pallas_call(
        functools.partial(kernel, sizes),
        out_shape=(
            jax.ShapeDtypeStruct((rows_i, seqs, width), BF16),
            jax.ShapeDtypeStruct((cells, pwidth), BF16),
        ),
        in_specs=[vmem] + [pl.BlockSpec(memory_space=pltpu.HBM)] * len(inputs),
        out_specs=(vmem, vmem),
        scratch_shapes=[
            (pltpu.SMEM if name == "scalars" else pltpu.VMEM)(v.shape, v.dtype) for name, v in zip(INPUTS, inputs)
        ]
        + [
            pltpu.VMEM((n_pb, rows_i, seqs, width), BF16),
            pltpu.VMEM((n_pb, cells, pwidth), BF16),
            pltpu.VMEM((n_pb, rows_i * seqs, width), BF16),
            pltpu.VMEM((n_pb, rows_i * seqs, width), BF16),
            pltpu.VMEM((n_pb, rows_i * seqs, width), BF16),
            pltpu.VMEM((n_pb * eparts * seqs, rows_i * LANES), BF16),
            pltpu.VMEM((msg_rows, LANES), BF16),
            pltpu.VMEM((n_src, n_pb, msg_rows, LANES), BF16),
            pltpu.VMEM((TRI_HEADS * cols, residues), F32),
            pltpu.VMEM((n_pb, cells, pwidth), F32),
            pltpu.VMEM((n_pb, cells, 2 * pwidth), BF16),
            pltpu.VMEM(arrays["tensor"].shape, F32),
            pltpu.VMEM(arrays["tensor"].shape, BF16),
            pltpu.VMEM((max(cells * SUBLANES, msg_rows), LANES), F32),
            dma((len(inputs),)),
            dma((n_pb,)),
            dma((n_pb,)),
            dma((n_pb,)),
            dma((n_pb,)),
            dma((n_a,)),
            dma((n_as * n_pb,)),
            dma((n_as * mates,)),
            dma((n_src,)),
        ],
        compiler_params=pltpu.CompilerParams(
            collective_id=0, has_side_effects=True, vmem_limit_bytes=56 * 1024 * 1024
        ),
    )(x_t, *inputs)
    return jnp.transpose(msa, (1, 0, 2)), pair_out.reshape(rows_i, cols, pwidth)


def solution(mesh):
    n_row, n_br, n_pb = mesh.shape["row"], mesh.shape["br"], mesh.shape["pb"]
    n_b = 2 if n_row % (2 * n_pb) == 0 else 1
    sizes = (n_pb, n_row // n_b, n_b, n_br)
    return jax.shard_map(
        functools.partial(on_device, sizes),
        mesh=mesh,
        in_specs=(
            P(("grp", "pb"), ("row", "br"), None),
            P(("grp", "row", "br"), "pb", None),
            P("grp"),
            P("grp"),
            P("grp"),
        )
        + (P(),) * 12,
        out_specs=(P(("grp", "pb"), ("row", "br"), None), P(("grp", "row", "br"), "pb", None)),
        check_vma=False,
    )
```

```python
import functools

import jax
import jax.numpy as jnp
from jax import lax
from jax.experimental import pallas as pl
from jax.experimental.pallas import tpu as pltpu
from jax.sharding import PartitionSpec as P

VERTICAL_ATTENDS = 8
TRI_HEADS = 4
SUBSPACE_DEPTH = 32
RELPOS_MAX = 32

NORM_EPS = 1e-05
MASK_NEGATIVE = 1000000000.0
LANES = 128
SUBLANES = 8
MESH = pl.DeviceIdType.MESH
F32 = jnp.float32
BF16 = jnp.bfloat16

WEIGHTS = (
    "rel", "qkvg", "vproj", "expand", "contract", "duo", "tensor", "tri", "tbias", "tout", "up", "down",
)


INPUTS = (
    "x", "chain", "duo", "positions", "scalars", "rel", "pair", "tbias", "qkvg", "tri", "tensor",
    "vproj", "expand", "contract", "resolved", "tout", "up", "down",
)


def normalize(values):
    centre = jnp.mean(values, axis=-1, keepdims=True)
    centred = values - centre
    spread = jnp.mean(centred * centred, axis=-1, keepdims=True)
    return (centred * lax.rsqrt(spread + NORM_EPS)).astype(BF16)


def matmul(a, b):
    return jnp.dot(a, b, preferred_element_type=F32)


def matmul_nt(a, b):
    return lax.dot_general(a, b, (((1,), (1,)), ((), ())), preferred_element_type=F32)


def matmul_tn(a, b):
    return lax.dot_general(a, b, (((0,), (0,)), ((), ())), preferred_element_type=F32)


def softmax_rows(scores):
    exp_scores = jnp.exp(scores - jnp.max(scores, axis=-1, keepdims=True))
    return (exp_scores * (1.0 / jnp.sum(exp_scores, axis=-1, keepdims=True))).astype(BF16)


def head_stack(values, heads):
    rows, width = values.shape
    lane = lax.broadcasted_iota(jnp.int32, (rows, width), 1) // SUBSPACE_DEPTH
    return jnp.concatenate(
        [jnp.where(lane == h, values, 0.0) for h in range(heads)], axis=0
    ).astype(BF16)


def head_merge(stacked, heads):
    rows, width = stacked.shape[0] // heads, stacked.shape[1]
    lane = lax.broadcasted_iota(jnp.int32, (rows, width), 1) // SUBSPACE_DEPTH
    total = jnp.zeros((rows, width), F32)
    for h in range(heads):
        total = jnp.where(lane == h, stacked[h * rows : (h + 1) * rows], total)
    return total


def kernel(sizes, shape, *refs):
    n_pb, n_a, n_b, n_c = sizes
    count = len(INPUTS)
    hbm = dict(zip(INPUTS, refs[:count]))
    out_msa, out_pair = refs[count : 2 + count]
    w = dict(zip(INPUTS, refs[2 + count : 2 + 2 * count]))
    (xg, pg, xn_s, k_s, v_s, left_s, msg_s, gather, bias_s, pairin_s, tkv_s, wf_s, wp_s, opm_s,
     flat_s, msa_s, pair_s, wsem, sx, rx, sp, rp, s1, r1, s2, r2) = refs[2 + 2 * count :]
    x_ref, pair_ref = w["x"], w["pair"]
    rows_i, seqs, width = shape
    tiles = width // LANES
    cells, pwidth = pair_ref.shape
    cols = cells // rows_i
    residues = w["resolved"].shape[1]
    n_as = n_a // n_pb
    n_src = n_as * n_b * n_c
    factor = w["duo"].shape[0] // 2
    eparts = factor // SUBLANES
    seq_blocks = eparts * seqs // LANES
    factor_rows = rows_i * SUBLANES
    base = seq_blocks * factor_rows

    grp = lax.axis_index("grp")
    row = lax.axis_index("row")
    c_me = lax.axis_index("br")
    p_me = lax.axis_index("pb")
    a_me, b_me = row // n_b, row % n_b
    scale = SUBSPACE_DEPTH ** (-0.5)

    def device(a, b, c, p):
        return (grp, a * n_b + b, c, p)

    loads = {}
    for n, name in enumerate(INPUTS):
        loads[name] = pltpu.make_async_copy(hbm[name], w[name], wsem.at[n])
    for name in INPUTS:
        loads[name].start()

    barrier = pltpu.get_barrier_semaphore()
    line = [(da, dp) for da in range(n_a) for dp in range(n_pb) if (da, dp) != (0, 0)]
    mates = [(db, dc) for db in range(n_b) for dc in range(n_c) if (db, dc) != (0, 0)]
    for da, dp in line:
        pl.semaphore_signal(
            barrier, inc=1, device_id=device((a_me + da) % n_a, b_me, c_me, (p_me + dp) % n_pb), device_id_type=MESH
        )
    for db, dc in mates:
        pl.semaphore_signal(
            barrier, inc=1, device_id=device(a_me, (b_me + db) % n_b, (c_me + dc) % n_c, p_me), device_id_type=MESH
        )

    def by_residue(block):
        flat_s[...] = block.astype(F32)
        return jnp.concatenate(
            [
                jnp.concatenate(
                    [flat_s[pl.ds(t * rows_i + r, seqs, stride=tiles * rows_i), :] for t in range(tiles)], axis=1
                )
                for r in range(rows_i)
            ],
            axis=0,
        )

    loads["x"].wait()
    x_own = by_residue(x_ref[...])
    xn_own = normalize(x_own)
    xn_s[p_me] = xn_own
    loads["chain"].wait()
    loads["duo"].wait()
    chain = w["chain"][...].astype(F32)
    own_chain = jnp.zeros((1, seqs), F32)
    for p in range(n_pb):
        own_chain = jnp.where(p_me == p, chain[:, p * seqs : (p + 1) * seqs], own_chain)
    rt = matmul_nt(w["duo"][factor:, :], xn_own) * jnp.concatenate([own_chain] * rows_i, axis=1)
    for j in range(rows_i):
        parts = jnp.concatenate(
            [rt[q * SUBLANES : (q + 1) * SUBLANES, j * seqs : (j + 1) * seqs] for q in range(eparts)], axis=1
        )
        for b in range(seq_blocks):
            at = b * factor_rows + j * SUBLANES
            opm_s[at : at + SUBLANES, :] = parts[:, b * LANES : (b + 1) * LANES]

    row_first = (row * n_c + c_me) * rows_i
    bins = 2 * RELPOS_MAX + 1
    loads["positions"].wait()
    loads["scalars"].wait()
    loads["rel"].wait()
    for i in range(rows_i):
        offset = jnp.clip(w["scalars"][row_first + i] - w["positions"][...], -RELPOS_MAX, RELPOS_MAX) + RELPOS_MAX
        hot = lax.broadcasted_iota(jnp.int32, (bins, residues), 0) == offset
        added = matmul_tn(jnp.where(hot, 1.0, 0.0).astype(BF16), w["rel"][...])
        for p in range(n_pb):
            pairin_s[p, i * cols : (i + 1) * cols] = added[p * cols : (p + 1) * cols]
    loads["pair"].wait()
    pair_in = pairin_s[p_me] + pair_ref[...].astype(F32)
    pn_own = normalize(pair_in)
    loads["tbias"].wait()
    bt = matmul_nt(w["tbias"][...], pn_own)
    for i in range(rows_i):
        for h in range(TRI_HEADS):
            at = base + h * rows_i + i
            opm_s[at : at + 1, :cols] = bt[h : h + 1, i * cols : (i + 1) * cols]
    msg_s[...] = opm_s[: msg_s.shape[0], :].astype(BF16)

    pl.semaphore_wait(barrier, len(line) + len(mates))

    p_to, a_slot = a_me // n_as, a_me % n_as
    stays = p_to == p_me

    def slot_of(a, b, c):
        return (a * n_b + b) * n_c + c

    def first(d):
        return pltpu.make_async_remote_copy(
            src_ref=msg_s, dst_ref=gather.at[slot_of(a_slot, b_me, c_me), p_me], send_sem=s1.at[d],
            recv_sem=r1.at[a_slot * n_pb + p_me], device_id=device((a_me + d) % n_a, b_me, c_me, p_to),
            device_id_type=MESH)

    for d in range(1, n_a):
        first(d).start()

    @pl.when(jnp.logical_not(stays))
    def _():
        first(0).start()

    @pl.when(stays)
    def _():
        gather[slot_of(a_slot, b_me, c_me), p_me] = msg_s[...]

    exchange = []
    for d in range(1, n_pb):
        peer = device(a_me, b_me, c_me, (p_me + d) % n_pb)
        exchange.append((
            pltpu.make_async_remote_copy(
                src_ref=pair_ref, dst_ref=pg.at[n_pb - d], send_sem=sp.at[d], recv_sem=rp.at[n_pb - d],
                device_id=peer, device_id_type=MESH),
            pltpu.make_async_remote_copy(
                src_ref=x_ref, dst_ref=xg.at[n_pb - d], send_sem=sx.at[d], recv_sem=rx.at[n_pb - d],
                device_id=peer, device_id_type=MESH),
        ))
    for copy, _ in exchange:
        copy.start()
    for _, copy in exchange:
        copy.start()

    loads["qkvg"].wait()
    proj = matmul(xn_own, w["qkvg"][...])
    query = proj[:, :width].astype(BF16).astype(F32)
    gate = jax.nn.sigmoid(proj[:, 3 * width :].astype(BF16).astype(F32))
    k_s[p_me] = proj[:, width : 2 * width].astype(BF16)
    v_s[p_me] = proj[:, 2 * width : 3 * width].astype(BF16)

    loads["tri"].wait()
    tri_w = w["tri"][...].astype(F32)
    tri_w = jnp.concatenate(
        [
            tri_w[:, (h * 4 + kind) * SUBSPACE_DEPTH : (h * 4 + kind + 1) * SUBSPACE_DEPTH]
            for kind in range(4)
            for h in range(TRI_HEADS)
        ],
        axis=1,
    ).astype(BF16)
    tproj = matmul(pn_own, tri_w)
    tkv_s[p_me] = tproj[:, pwidth : 3 * pwidth].astype(BF16)
    tri_q = tproj[:, :pwidth].astype(BF16).astype(F32)
    tri_gate = jax.nn.sigmoid(tproj[:, 3 * pwidth :].astype(BF16).astype(F32))
    loads["tensor"].wait()
    wf_s[...] = w["tensor"][...].astype(F32)
    for e in range(SUBLANES):
        for q in range(eparts):
            at = (e * eparts + q) * factor
            wp_s[at : at + factor, :] = wf_s[pl.ds(q * SUBLANES + e, factor, stride=factor), :].astype(BF16)

    for slot in range(1, n_pb):
        exchange[n_pb - slot - 1][0].wait_recv()
    for d in range(1, n_pb):
        p = (p_me + d) % n_pb
        pn = normalize(pairin_s[p] + pg[d].astype(F32))
        tkv_s[p] = matmul(pn, tri_w[:, pwidth : 3 * pwidth]).astype(BF16)

    second = []
    for a in range(n_as):
        slot = slot_of(a, b_me, c_me)
        for p in range(n_pb):
            here = jnp.logical_and(stays, jnp.logical_and(a_slot == a, p_me == p))

            @pl.when(jnp.logical_not(here))
            def _():
                pltpu.make_async_remote_copy(
                    src_ref=msg_s, dst_ref=gather.at[slot, p], send_sem=s1.at[0], recv_sem=r1.at[a * n_pb + p],
                    device_id=device((a_me + 1) % n_a, b_me, c_me, p_me), device_id_type=MESH).wait_recv()

        for m, (db, dc) in enumerate(mates):
            copy = pltpu.make_async_remote_copy(
                src_ref=gather.at[slot], dst_ref=gather.at[slot], send_sem=s2.at[a * len(mates) + m],
                recv_sem=r2.at[slot],
                device_id=device(a_me, (b_me + db) % n_b, (c_me + dc) % n_c, p_me), device_id_type=MESH)
            copy.start()
            second.append(copy)

    for slot in range(1, n_pb):
        exchange[n_pb - slot - 1][1].wait_recv()
    for d in range(1, n_pb):
        p = (p_me + d) % n_pb
        xn = normalize(by_residue(xg[d]))
        xn_s[p] = xn
        kv = matmul(xn, w["qkvg"][:, width : 3 * width])
        k_s[p] = kv[:, :width].astype(BF16)
        v_s[p] = kv[:, width:].astype(BF16)

    left_w = jnp.concatenate([w["duo"][:factor, :]] * eparts, axis=0)
    lane_part = lax.broadcasted_iota(jnp.int32, (seqs, LANES), 1) // factor
    for p in range(n_pb):
        left4 = matmul_nt(xn_s[p], left_w)
        for i in range(rows_i):
            block = left4[i * seqs : (i + 1) * seqs]
            for q in range(eparts):
                left_s[(p * eparts + q) * seqs : (p * eparts + q + 1) * seqs, i * LANES : (i + 1) * LANES] = (
                    jnp.where(lane_part == q, block, 0.0).astype(BF16)
                )

    seq_bias = (chain - 1.0) * MASK_NEGATIVE
    mixed = []
    for r in range(rows_i):
        span = slice(r * seqs, (r + 1) * seqs)
        keys = jnp.concatenate([k_s[p, span, :] for p in range(n_pb)], axis=0)
        values = jnp.concatenate([v_s[p, span, :] for p in range(n_pb)], axis=0)
        scores = matmul_nt(head_stack(query[span], VERTICAL_ATTENDS), keys) * scale + seq_bias
        weighted = matmul(softmax_rows(scores), values)
        mixed.append((gate[span] * head_merge(weighted, VERTICAL_ATTENDS)).astype(BF16))

    loads["vproj"].wait()
    mid = x_own + matmul(jnp.concatenate(mixed, axis=0), w["vproj"][...])
    loads["expand"].wait()
    hidden = jnp.maximum(matmul(normalize(mid), w["expand"][...]), 0.0).astype(BF16)
    loads["contract"].wait()
    fresh = mid + matmul(hidden, w["contract"][...])
    for r in range(rows_i):
        for t in range(tiles):
            flat_s[pl.ds(t * rows_i + r, seqs, stride=tiles * rows_i), :] = fresh[
                r * seqs : (r + 1) * seqs, t * LANES : (t + 1) * LANES
            ]
    msa_s[...] = flat_s[...].astype(BF16)
    msa_out = pltpu.make_async_copy(msa_s, out_msa, wsem.at[count])
    msa_out.start()

    for a in range(n_as):
        for db, dc in mates:
            slot = slot_of(a, (b_me + db) % n_b, (c_me + dc) % n_c)
            pltpu.make_async_remote_copy(
                src_ref=gather.at[slot], dst_ref=gather.at[slot], send_sem=s2.at[0], recv_sem=r2.at[slot],
                device_id=device(a_me, (b_me + db) % n_b, (c_me + dc) % n_c, p_me), device_id_type=MESH).wait_recv()

    right_all = jnp.concatenate(
        [
            jnp.concatenate(
                [
                    gather[s, p, b * factor_rows : (b + 1) * factor_rows, :]
                    for p in range(n_pb)
                    for b in range(seq_blocks)
                ],
                axis=1,
            )
            for s in range(n_src)
        ],
        axis=0,
    )
    outer = matmul(right_all, left_s[...])
    opm_s[: cells * SUBLANES, :] = jnp.concatenate(
        [outer[:, i * LANES : (i + 1) * LANES] for i in range(rows_i)], axis=0
    )
    lhs = jnp.concatenate(
        [opm_s[pl.ds(e, cells, stride=SUBLANES), :].astype(BF16) for e in range(SUBLANES)], axis=1
    )
    opm = matmul(lhs, wp_s[...]) / jnp.sum(chain)

    for s in range(n_src):
        part = jnp.concatenate(
            [gather[s, p, base : base + rows_i * TRI_HEADS, :].astype(F32)[:, :cols] for p in range(n_pb)], axis=1
        )
        for h in range(TRI_HEADS):
            bias_s[h * cols + s * rows_i : h * cols + (s + 1) * rows_i, :] = part[h * rows_i : (h + 1) * rows_i, :]
    loads["resolved"].wait()
    bias = bias_s[...] + (w["resolved"][...].astype(F32) - 1.0) * MASK_NEGATIVE
    tri_mixed = []
    for i in range(rows_i):
        span = slice(i * cols, (i + 1) * cols)
        keys = jnp.concatenate([tkv_s[p, span, :pwidth] for p in range(n_pb)], axis=0)
        values = jnp.concatenate([tkv_s[p, span, pwidth:] for p in range(n_pb)], axis=0)
        scores = matmul_nt(head_stack(tri_q[span], TRI_HEADS), keys) * scale + bias
        weighted = matmul(softmax_rows(scores), values)
        tri_mixed.append((tri_gate[span] * head_merge(weighted, TRI_HEADS)).astype(BF16))
    loads["tout"].wait()
    pair_mid = pair_in + matmul(jnp.concatenate(tri_mixed, axis=0), w["tout"][...]) + opm
    loads["up"].wait()
    pair_hidden = jnp.maximum(matmul(normalize(pair_mid), w["up"][...]), 0.0).astype(BF16)
    loads["down"].wait()
    pair_s[...] = (pair_mid + matmul(pair_hidden, w["down"][...])).astype(BF16)
    pair_out = pltpu.make_async_copy(pair_s, out_pair, wsem.at[count + 1])
    pair_out.start()

    msa_out.wait()
    pair_out.wait()
    for copies in exchange:
        for copy in copies:
            copy.wait_send()
    for copy in second:
        copy.wait_send()
    for d in range(1, n_a):
        first(d).wait_send()

    @pl.when(jnp.logical_not(stays))
    def _():
        first(0).wait_send()


def on_device(sizes, x, pair, chain, resolved, positions, *weights):
    seqs, rows_i, width = x.shape
    cols, pwidth = pair.shape[1:]
    n_pb, n_a, n_b, n_c = sizes
    cells = rows_i * cols
    chains, residues = chain.shape[0], resolved.shape[0]
    n_as = n_a // n_pb
    n_src = n_as * n_b * n_c
    arrays = dict(zip(WEIGHTS, weights))
    arrays["duo"] = arrays["duo"].T
    arrays["tbias"] = arrays["tbias"].T
    tiles = width // LANES
    arrays["x"] = x.reshape(seqs, rows_i, tiles, LANES).transpose(0, 2, 1, 3).reshape(-1, LANES)
    arrays["pair"] = pair.reshape(cells, pwidth)
    arrays["chain"] = chain.reshape(1, chains)
    arrays["resolved"] = resolved.reshape(1, residues)
    arrays["positions"] = positions.reshape(1, residues)
    arrays["scalars"] = positions
    inputs = [arrays[name] for name in INPUTS]
    factor = arrays["duo"].shape[0] // 2
    eparts = factor // SUBLANES
    msg_rows = eparts * seqs // LANES * rows_i * SUBLANES + rows_i * TRI_HEADS
    mates = n_b * n_c - 1
    dma = pltpu.SemaphoreType.DMA
    msa, pair_out = pl.pallas_call(
        functools.partial(kernel, sizes, (rows_i, seqs, width)),
        out_shape=(
            jax.ShapeDtypeStruct(arrays["x"].shape, BF16),
            jax.ShapeDtypeStruct((cells, pwidth), BF16),
        ),
        in_specs=[pl.BlockSpec(memory_space=pltpu.HBM)] * len(inputs),
        out_specs=(pl.BlockSpec(memory_space=pltpu.HBM),) * 2,
        scratch_shapes=[
            (pltpu.SMEM if name == "scalars" else pltpu.VMEM)(v.shape, v.dtype) for name, v in zip(INPUTS, inputs)
        ]
        + [
            pltpu.VMEM((n_pb,) + arrays["x"].shape, BF16),
            pltpu.VMEM((n_pb, cells, pwidth), BF16),
            pltpu.VMEM((n_pb, rows_i * seqs, width), BF16),
            pltpu.VMEM((n_pb, rows_i * seqs, width), BF16),
            pltpu.VMEM((n_pb, rows_i * seqs, width), BF16),
            pltpu.VMEM((n_pb * eparts * seqs, rows_i * LANES), BF16),
            pltpu.VMEM((msg_rows, LANES), BF16),
            pltpu.VMEM((n_src, n_pb, msg_rows, LANES), BF16),
            pltpu.VMEM((TRI_HEADS * cols, residues), F32),
            pltpu.VMEM((n_pb, cells, pwidth), F32),
            pltpu.VMEM((n_pb, cells, 2 * pwidth), BF16),
            pltpu.VMEM(arrays["tensor"].shape, F32),
            pltpu.VMEM(arrays["tensor"].shape, BF16),
            pltpu.VMEM((max(cells * SUBLANES, msg_rows), LANES), F32),
            pltpu.VMEM(arrays["x"].shape, F32),
            pltpu.VMEM(arrays["x"].shape, BF16),
            pltpu.VMEM((cells, pwidth), BF16),
            dma((len(inputs) + 2,)),
            dma((n_pb,)),
            dma((n_pb,)),
            dma((n_pb,)),
            dma((n_pb,)),
            dma((n_a,)),
            dma((n_as * n_pb,)),
            dma((n_as * mates,)),
            dma((n_src,)),
        ],
        compiler_params=pltpu.CompilerParams(
            collective_id=0, has_side_effects=True, vmem_limit_bytes=56 * 1024 * 1024
        ),
    )(*inputs)
    msa = msa.reshape(seqs, tiles, rows_i, LANES).transpose(0, 2, 1, 3).reshape(x.shape)
    return msa, pair_out.reshape(rows_i, cols, pwidth)


def solution(mesh):
    n_row, n_br, n_pb = mesh.shape["row"], mesh.shape["br"], mesh.shape["pb"]
    n_b = 2 if n_row % (2 * n_pb) == 0 else 1
    sizes = (n_pb, n_row // n_b, n_b, n_br)
    return jax.shard_map(
        functools.partial(on_device, sizes),
        mesh=mesh,
        in_specs=(
            P(("grp", "pb"), ("row", "br"), None),
            P(("grp", "row", "br"), "pb", None),
            P("grp"),
            P("grp"),
            P("grp"),
        )
        + (P(),) * 12,
        out_specs=(P(("grp", "pb"), ("row", "br"), None), P(("grp", "row", "br"), "pb", None)),
        check_vma=False,
    )
```

```python
import functools

import jax
import jax.numpy as jnp
from jax import lax
from jax.experimental import pallas as pl
from jax.experimental.pallas import tpu as pltpu
from jax.sharding import PartitionSpec as P

VERTICAL_ATTENDS = 8
TRI_HEADS = 4
SUBSPACE_DEPTH = 32
RELPOS_MAX = 32

NORM_EPS = 1e-05
MASK_NEGATIVE = 1000000000.0
LANES = 128
SUBLANES = 8
MESH = pl.DeviceIdType.MESH
F32 = jnp.float32
BF16 = jnp.bfloat16

WEIGHTS = (
    "rel", "qkvg", "vproj", "expand", "contract", "duo", "tensor", "tri", "tbias", "tout", "up", "down",
)


INPUTS = (
    "x", "chain", "duo", "positions", "scalars", "rel", "pair", "tbias", "qkvg", "tri", "tensor",
    "vproj", "expand", "contract", "resolved", "tout", "up", "down",
)


def normalize(values):
    centre = jnp.mean(values, axis=-1, keepdims=True)
    centred = values - centre
    spread = jnp.mean(centred * centred, axis=-1, keepdims=True)
    return (centred * lax.rsqrt(spread + NORM_EPS)).astype(BF16)


def matmul(a, b):
    return jnp.dot(a, b, preferred_element_type=F32)


def matmul_nt(a, b):
    return lax.dot_general(a, b, (((1,), (1,)), ((), ())), preferred_element_type=F32)


def matmul_tn(a, b):
    return lax.dot_general(a, b, (((0,), (0,)), ((), ())), preferred_element_type=F32)


def softmax_rows(scores):
    exp_scores = jnp.exp(scores - jnp.max(scores, axis=-1, keepdims=True))
    return (exp_scores * (1.0 / jnp.sum(exp_scores, axis=-1, keepdims=True))).astype(BF16)


def head_stack(values, heads):
    rows, width = values.shape
    lane = lax.broadcasted_iota(jnp.int32, (rows, width), 1) // SUBSPACE_DEPTH
    return jnp.concatenate(
        [jnp.where(lane == h, values, 0.0) for h in range(heads)], axis=0
    ).astype(BF16)


def head_merge(stacked, heads):
    rows, width = stacked.shape[0] // heads, stacked.shape[1]
    lane = lax.broadcasted_iota(jnp.int32, (rows, width), 1) // SUBSPACE_DEPTH
    total = jnp.zeros((rows, width), F32)
    for h in range(heads):
        total = jnp.where(lane == h, stacked[h * rows : (h + 1) * rows], total)
    return total


def kernel(sizes, shape, *refs):
    n_pb, n_a, n_b, n_c = sizes
    count = len(INPUTS)
    hbm = dict(zip(INPUTS, refs[:count]))
    out_msa, out_pair = refs[count : 2 + count]
    w = dict(zip(INPUTS, refs[2 + count : 2 + 2 * count]))
    (xg, pg, xn_s, k_s, v_s, left_s, msg_s, gather, bias_s, pairin_s, tkv_s, wf_s, wp_s, opm_s,
     flat_s, msa_s, pair_s, wsem, sx, rx, sp, rp, bt_s, bmsg_s, bgather, s1, r1, s2, r2, sb1, rb1, sb2, rb2) = refs[2 + 2 * count :]
    x_ref, pair_ref = w["x"], w["pair"]
    rows_i, seqs, width = shape
    tiles = width // LANES
    cells, pwidth = pair_ref.shape
    cols = cells // rows_i
    residues = w["resolved"].shape[1]
    n_as = n_a // n_pb
    n_src = n_as * n_b * n_c
    factor = w["duo"].shape[0] // 2
    eparts = factor // SUBLANES
    seq_blocks = eparts * seqs // LANES
    factor_rows = rows_i * SUBLANES

    grp = lax.axis_index("grp")
    row = lax.axis_index("row")
    c_me = lax.axis_index("br")
    p_me = lax.axis_index("pb")
    a_me, b_me = row // n_b, row % n_b
    scale = SUBSPACE_DEPTH ** (-0.5)

    def device(a, b, c, p):
        return (grp, a * n_b + b, c, p)

    loads = {}
    for n, name in enumerate(INPUTS):
        loads[name] = pltpu.make_async_copy(hbm[name], w[name], wsem.at[n])
    for name in INPUTS:
        loads[name].start()

    barrier = pltpu.get_barrier_semaphore()
    line = [(da, dp) for da in range(n_a) for dp in range(n_pb) if (da, dp) != (0, 0)]
    mates = [(db, dc) for db in range(n_b) for dc in range(n_c) if (db, dc) != (0, 0)]
    for da, dp in line:
        pl.semaphore_signal(
            barrier, inc=1, device_id=device((a_me + da) % n_a, b_me, c_me, (p_me + dp) % n_pb), device_id_type=MESH
        )
    for db, dc in mates:
        pl.semaphore_signal(
            barrier, inc=1, device_id=device(a_me, (b_me + db) % n_b, (c_me + dc) % n_c, p_me), device_id_type=MESH
        )

    pl.semaphore_wait(barrier, len(line) + len(mates))

    exchange = []
    for d in range(1, n_pb):
        peer = device(a_me, b_me, c_me, (p_me + d) % n_pb)
        exchange.append((
            pltpu.make_async_remote_copy(
                src_ref=hbm["pair"], dst_ref=pg.at[n_pb - d], send_sem=sp.at[d], recv_sem=rp.at[n_pb - d],
                device_id=peer, device_id_type=MESH),
            pltpu.make_async_remote_copy(
                src_ref=hbm["x"], dst_ref=xg.at[n_pb - d], send_sem=sx.at[d], recv_sem=rx.at[n_pb - d],
                device_id=peer, device_id_type=MESH),
        ))
    for copy, _ in exchange:
        copy.start()
    for _, copy in exchange:
        copy.start()

    def by_residue(block):
        flat_s[...] = block.astype(F32)
        return jnp.concatenate(
            [
                jnp.concatenate(
                    [flat_s[pl.ds(t * rows_i + r, seqs, stride=tiles * rows_i), :] for t in range(tiles)], axis=1
                )
                for r in range(rows_i)
            ],
            axis=0,
        )

    loads["x"].wait()
    x_own = by_residue(x_ref[...])
    xn_own = normalize(x_own)
    xn_s[p_me] = xn_own
    loads["chain"].wait()
    loads["duo"].wait()
    chain = w["chain"][...].astype(F32)
    own_chain = jnp.zeros((1, seqs), F32)
    for p in range(n_pb):
        own_chain = jnp.where(p_me == p, chain[:, p * seqs : (p + 1) * seqs], own_chain)
    rt = matmul_nt(w["duo"][factor:, :], xn_own) * jnp.concatenate([own_chain] * rows_i, axis=1)
    for j in range(rows_i):
        parts = jnp.concatenate(
            [rt[q * SUBLANES : (q + 1) * SUBLANES, j * seqs : (j + 1) * seqs] for q in range(eparts)], axis=1
        )
        for b in range(seq_blocks):
            at = b * factor_rows + j * SUBLANES
            opm_s[at : at + SUBLANES, :] = parts[:, b * LANES : (b + 1) * LANES]

    msg_s[...] = opm_s[: msg_s.shape[0], :].astype(BF16)

    p_to, a_slot = a_me // n_as, a_me % n_as
    stays = p_to == p_me

    def slot_of(a, b, c):
        return (a * n_b + b) * n_c + c

    def first(d):
        return pltpu.make_async_remote_copy(
            src_ref=msg_s, dst_ref=gather.at[slot_of(a_slot, b_me, c_me), p_me], send_sem=s1.at[d],
            recv_sem=r1.at[a_slot * n_pb + p_me], device_id=device((a_me + d) % n_a, b_me, c_me, p_to),
            device_id_type=MESH)

    def first_bias(d):
        return pltpu.make_async_remote_copy(
            src_ref=bmsg_s, dst_ref=bgather.at[b_me, c_me, a_slot, p_me], send_sem=sb1.at[d],
            recv_sem=rb1.at[a_slot * n_pb + p_me], device_id=device((a_me + d) % n_a, b_me, c_me, p_to),
            device_id_type=MESH)

    def second(da, dp, m):
        a, p = (a_slot + da) % n_as, (p_me + dp) % n_pb
        slot = slot_of(a, b_me, c_me)
        db, dc = mates[m]
        return pltpu.make_async_remote_copy(
            src_ref=gather.at[slot, p], dst_ref=gather.at[slot, p],
            send_sem=s2.at[(da * n_pb + dp) * len(mates) + m], recv_sem=r2.at[slot * n_pb + p],
            device_id=device(a_me, (b_me + db) % n_b, (c_me + dc) % n_c, p_me), device_id_type=MESH)

    def second_bias(m):
        db, dc = mates[m]
        return pltpu.make_async_remote_copy(
            src_ref=bgather.at[b_me, c_me], dst_ref=bgather.at[b_me, c_me], send_sem=sb2.at[m],
            recv_sem=rb2.at[b_me * n_c + c_me],
            device_id=device(a_me, (b_me + db) % n_b, (c_me + dc) % n_c, p_me), device_id_type=MESH)

    for d in range(1, n_a):
        first(d).start()

    @pl.when(jnp.logical_not(stays))
    def _():
        first(0).start()

    @pl.when(stays)
    def _():
        gather[slot_of(a_slot, b_me, c_me), p_me] = msg_s[...]
        for m in range(len(mates)):
            second(0, 0, m).start()

    row_first = (row * n_c + c_me) * rows_i
    bins = 2 * RELPOS_MAX + 1
    loads["positions"].wait()
    loads["scalars"].wait()
    loads["rel"].wait()
    for i in range(rows_i):
        offset = jnp.clip(w["scalars"][row_first + i] - w["positions"][...], -RELPOS_MAX, RELPOS_MAX) + RELPOS_MAX
        hot = lax.broadcasted_iota(jnp.int32, (bins, residues), 0) == offset
        added = matmul_tn(jnp.where(hot, 1.0, 0.0).astype(BF16), w["rel"][...])
        for p in range(n_pb):
            pairin_s[p, i * cols : (i + 1) * cols] = added[p * cols : (p + 1) * cols]
    loads["pair"].wait()
    pair_in = pairin_s[p_me] + pair_ref[...].astype(F32)
    pn_own = normalize(pair_in)
    loads["tbias"].wait()
    bt = matmul_nt(w["tbias"][...], pn_own)
    bt_s[...] = jnp.zeros_like(bt_s)
    for i in range(rows_i):
        for h in range(TRI_HEADS):
            at = h * rows_i + i
            bt_s[at : at + 1, :cols] = bt[h : h + 1, i * cols : (i + 1) * cols]
    bmsg_s[...] = bt_s[...].astype(BF16)
    for d in range(1, n_a):
        first_bias(d).start()

    @pl.when(jnp.logical_not(stays))
    def _():
        first_bias(0).start()

    @pl.when(stays)
    def _():
        bgather[b_me, c_me, a_slot, p_me] = bmsg_s[...]

    loads["qkvg"].wait()
    proj = matmul(xn_own, w["qkvg"][...])
    query = proj[:, :width].astype(BF16).astype(F32)
    gate = jax.nn.sigmoid(proj[:, 3 * width :].astype(BF16).astype(F32))
    k_s[p_me] = proj[:, width : 2 * width].astype(BF16)
    v_s[p_me] = proj[:, 2 * width : 3 * width].astype(BF16)

    loads["tri"].wait()
    tri_w = w["tri"][...].astype(F32)
    tri_w = jnp.concatenate(
        [
            tri_w[:, (h * 4 + kind) * SUBSPACE_DEPTH : (h * 4 + kind + 1) * SUBSPACE_DEPTH]
            for kind in range(4)
            for h in range(TRI_HEADS)
        ],
        axis=1,
    ).astype(BF16)
    tproj = matmul(pn_own, tri_w)
    tkv_s[p_me] = tproj[:, pwidth : 3 * pwidth].astype(BF16)
    tri_q = tproj[:, :pwidth].astype(BF16).astype(F32)
    tri_gate = jax.nn.sigmoid(tproj[:, 3 * pwidth :].astype(BF16).astype(F32))
    loads["tensor"].wait()
    wf_s[...] = w["tensor"][...].astype(F32)
    for e in range(SUBLANES):
        for q in range(eparts):
            at = (e * eparts + q) * factor
            wp_s[at : at + factor, :] = wf_s[pl.ds(q * SUBLANES + e, factor, stride=factor), :].astype(BF16)

    def hand_on(da, dp):
        a, p = (a_slot + da) % n_as, (p_me + dp) % n_pb
        pltpu.make_async_remote_copy(
            src_ref=msg_s, dst_ref=gather.at[slot_of(a, b_me, c_me), p], send_sem=s1.at[0],
            recv_sem=r1.at[a * n_pb + p], device_id=device((a_me + 1) % n_a, b_me, c_me, p_me),
            device_id_type=MESH).wait_recv()
        for m in range(len(mates)):
            second(da, dp, m).start()

    def bias_in(da, dp):
        a, p = (a_slot + da) % n_as, (p_me + dp) % n_pb
        pltpu.make_async_remote_copy(
            src_ref=bmsg_s, dst_ref=bgather.at[b_me, c_me, a, p], send_sem=sb1.at[0],
            recv_sem=rb1.at[a * n_pb + p], device_id=device((a_me + 1) % n_a, b_me, c_me, p_me),
            device_id_type=MESH).wait_recv()

    arrivals = [(da, dp) for da in range(n_as) for dp in range(n_pb)]
    for da, dp in arrivals[1:]:
        hand_on(da, dp)

    @pl.when(jnp.logical_not(stays))
    def _():
        hand_on(0, 0)
        bias_in(0, 0)

    for da, dp in arrivals[1:]:
        bias_in(da, dp)
    for m in range(len(mates)):
        second_bias(m).start()

    for slot in range(1, n_pb):
        exchange[n_pb - slot - 1][0].wait_recv()
    for d in range(1, n_pb):
        p = (p_me + d) % n_pb
        pn = normalize(pairin_s[p] + pg[d].astype(F32))
        tkv_s[p] = matmul(pn, tri_w[:, pwidth : 3 * pwidth]).astype(BF16)

    for slot in range(1, n_pb):
        exchange[n_pb - slot - 1][1].wait_recv()
    for d in range(1, n_pb):
        p = (p_me + d) % n_pb
        xn = normalize(by_residue(xg[d]))
        xn_s[p] = xn
        kv = matmul(xn, w["qkvg"][:, width : 3 * width])
        k_s[p] = kv[:, :width].astype(BF16)
        v_s[p] = kv[:, width:].astype(BF16)

    left_w = jnp.concatenate([w["duo"][:factor, :]] * eparts, axis=0)
    lane_part = lax.broadcasted_iota(jnp.int32, (seqs, LANES), 1) // factor
    for p in range(n_pb):
        left4 = matmul_nt(xn_s[p], left_w)
        for i in range(rows_i):
            block = left4[i * seqs : (i + 1) * seqs]
            for q in range(eparts):
                left_s[(p * eparts + q) * seqs : (p * eparts + q + 1) * seqs, i * LANES : (i + 1) * LANES] = (
                    jnp.where(lane_part == q, block, 0.0).astype(BF16)
                )

    seq_bias = (chain - 1.0) * MASK_NEGATIVE
    mixed = []
    for r in range(rows_i):
        span = slice(r * seqs, (r + 1) * seqs)
        keys = jnp.concatenate([k_s[p, span, :] for p in range(n_pb)], axis=0)
        values = jnp.concatenate([v_s[p, span, :] for p in range(n_pb)], axis=0)
        scores = matmul_nt(head_stack(query[span], VERTICAL_ATTENDS), keys) * scale + seq_bias
        weighted = matmul(softmax_rows(scores), values)
        mixed.append((gate[span] * head_merge(weighted, VERTICAL_ATTENDS)).astype(BF16))

    loads["vproj"].wait()
    mid = x_own + matmul(jnp.concatenate(mixed, axis=0), w["vproj"][...])
    loads["expand"].wait()
    hidden = jnp.maximum(matmul(normalize(mid), w["expand"][...]), 0.0).astype(BF16)
    loads["contract"].wait()
    fresh = mid + matmul(hidden, w["contract"][...])
    for r in range(rows_i):
        for t in range(tiles):
            flat_s[pl.ds(t * rows_i + r, seqs, stride=tiles * rows_i), :] = fresh[
                r * seqs : (r + 1) * seqs, t * LANES : (t + 1) * LANES
            ]
    msa_s[...] = flat_s[...].astype(BF16)
    msa_out = pltpu.make_async_copy(msa_s, out_msa, wsem.at[count])
    msa_out.start()

    for db, dc in mates:
        b, c = (b_me + db) % n_b, (c_me + dc) % n_c
        pltpu.make_async_remote_copy(
            src_ref=bgather.at[b, c], dst_ref=bgather.at[b, c], send_sem=sb2.at[0], recv_sem=rb2.at[b * n_c + c],
            device_id=device(a_me, b, c, p_me), device_id_type=MESH).wait_recv()
    for s in range(n_src):
        part = jnp.concatenate(
            [bgather[s // n_c % n_b, s % n_c, s // (n_b * n_c), p].astype(F32)[:, :cols] for p in range(n_pb)], axis=1
        )
        for h in range(TRI_HEADS):
            bias_s[h * cols + s * rows_i : h * cols + (s + 1) * rows_i, :] = part[h * rows_i : (h + 1) * rows_i, :]
    loads["resolved"].wait()
    bias = bias_s[...] + (w["resolved"][...].astype(F32) - 1.0) * MASK_NEGATIVE
    tri_mixed = []
    for i in range(rows_i):
        span = slice(i * cols, (i + 1) * cols)
        keys = jnp.concatenate([tkv_s[p, span, :pwidth] for p in range(n_pb)], axis=0)
        values = jnp.concatenate([tkv_s[p, span, pwidth:] for p in range(n_pb)], axis=0)
        scores = matmul_nt(head_stack(tri_q[span], TRI_HEADS), keys) * scale + bias
        weighted = matmul(softmax_rows(scores), values)
        tri_mixed.append((tri_gate[span] * head_merge(weighted, TRI_HEADS)).astype(BF16))
    loads["tout"].wait()
    tri_update = matmul(jnp.concatenate(tri_mixed, axis=0), w["tout"][...])

    for a in range(n_as):
        for p in range(n_pb):
            for db, dc in mates:
                b, c = (b_me + db) % n_b, (c_me + dc) % n_c
                slot = slot_of(a, b, c)
                pltpu.make_async_remote_copy(
                    src_ref=gather.at[slot, p], dst_ref=gather.at[slot, p], send_sem=s2.at[0],
                    recv_sem=r2.at[slot * n_pb + p], device_id=device(a_me, b, c, p_me),
                    device_id_type=MESH).wait_recv()

    right_all = jnp.concatenate(
        [
            jnp.concatenate(
                [
                    gather[s, p, b * factor_rows : (b + 1) * factor_rows, :]
                    for p in range(n_pb)
                    for b in range(seq_blocks)
                ],
                axis=1,
            )
            for s in range(n_src)
        ],
        axis=0,
    )
    outer = matmul(right_all, left_s[...])
    opm_s[: cells * SUBLANES, :] = jnp.concatenate(
        [outer[:, i * LANES : (i + 1) * LANES] for i in range(rows_i)], axis=0
    )
    lhs = jnp.concatenate(
        [opm_s[pl.ds(e, cells, stride=SUBLANES), :].astype(BF16) for e in range(SUBLANES)], axis=1
    )
    opm = matmul(lhs, wp_s[...]) / jnp.sum(chain)

    pair_mid = pair_in + tri_update + opm
    loads["up"].wait()
    pair_hidden = jnp.maximum(matmul(normalize(pair_mid), w["up"][...]), 0.0).astype(BF16)
    loads["down"].wait()
    pair_s[...] = (pair_mid + matmul(pair_hidden, w["down"][...])).astype(BF16)
    pair_out = pltpu.make_async_copy(pair_s, out_pair, wsem.at[count + 1])
    pair_out.start()

    msa_out.wait()
    pair_out.wait()
    for copies in exchange:
        for copy in copies:
            copy.wait_send()
    for m in range(len(mates)):
        for da, dp in arrivals:
            second(da, dp, m).wait_send()
        second_bias(m).wait_send()
    for d in range(1, n_a):
        first(d).wait_send()
        first_bias(d).wait_send()

    @pl.when(jnp.logical_not(stays))
    def _():
        first(0).wait_send()
        first_bias(0).wait_send()


def finish(msa_ref, pair_ref, out_msa, out_pair, sem):
    copies = [
        pltpu.make_async_copy(msa_ref, out_msa, sem.at[0]),
        pltpu.make_async_copy(pair_ref, out_pair, sem.at[1]),
    ]
    for copy in copies:
        copy.start()
    for copy in copies:
        copy.wait()


def on_device(sizes, x, pair, chain, resolved, positions, *weights):
    seqs, rows_i, width = x.shape
    cols, pwidth = pair.shape[1:]
    n_pb, n_a, n_b, n_c = sizes
    cells = rows_i * cols
    chains, residues = chain.shape[0], resolved.shape[0]
    n_as = n_a // n_pb
    n_src = n_as * n_b * n_c
    arrays = dict(zip(WEIGHTS, weights))
    arrays["duo"] = arrays["duo"].T
    arrays["tbias"] = arrays["tbias"].T
    tiles = width // LANES
    arrays["x"] = x.reshape(seqs, rows_i, tiles, LANES).transpose(0, 2, 1, 3).reshape(-1, LANES)
    arrays["pair"] = pair.reshape(cells, pwidth)
    arrays["chain"] = chain.reshape(1, chains)
    arrays["resolved"] = resolved.reshape(1, residues)
    arrays["positions"] = positions.reshape(1, residues)
    arrays["scalars"] = positions
    inputs = [arrays[name] for name in INPUTS]
    factor = arrays["duo"].shape[0] // 2
    eparts = factor // SUBLANES
    msg_rows = eparts * seqs // LANES * rows_i * SUBLANES
    mates = n_b * n_c - 1
    cols_padded = -(-cols // LANES) * LANES
    dma = pltpu.SemaphoreType.DMA
    msa, pair_out = pl.pallas_call(
        functools.partial(kernel, sizes, (rows_i, seqs, width)),
        out_shape=(
            jax.ShapeDtypeStruct(arrays["x"].shape, BF16),
            jax.ShapeDtypeStruct((cells, pwidth), BF16),
        ),
        in_specs=[pl.BlockSpec(memory_space=pltpu.HBM)] * len(inputs),
        out_specs=(pl.BlockSpec(memory_space=pltpu.HBM),) * 2,
        scratch_shapes=[
            (pltpu.SMEM if name == "scalars" else pltpu.VMEM)(v.shape, v.dtype) for name, v in zip(INPUTS, inputs)
        ]
        + [
            pltpu.VMEM((n_pb,) + arrays["x"].shape, BF16),
            pltpu.VMEM((n_pb, cells, pwidth), BF16),
            pltpu.VMEM((n_pb, rows_i * seqs, width), BF16),
            pltpu.VMEM((n_pb, rows_i * seqs, width), BF16),
            pltpu.VMEM((n_pb, rows_i * seqs, width), BF16),
            pltpu.VMEM((n_pb * eparts * seqs, rows_i * LANES), BF16),
            pltpu.VMEM((msg_rows, LANES), BF16),
            pltpu.VMEM((n_src, n_pb, msg_rows, LANES), BF16),
            pltpu.VMEM((TRI_HEADS * cols, residues), F32),
            pltpu.VMEM((n_pb, cells, pwidth), F32),
            pltpu.VMEM((n_pb, cells, 2 * pwidth), BF16),
            pltpu.VMEM(arrays["tensor"].shape, F32),
            pltpu.VMEM(arrays["tensor"].shape, BF16),
            pltpu.VMEM((max(cells * SUBLANES, msg_rows), LANES), F32),
            pltpu.VMEM(arrays["x"].shape, F32),
            pltpu.VMEM(arrays["x"].shape, BF16),
            pltpu.VMEM((cells, pwidth), BF16),
            dma((len(inputs) + 2,)),
            dma((n_pb,)),
            dma((n_pb,)),
            dma((n_pb,)),
            dma((n_pb,)),
            pltpu.VMEM((rows_i * TRI_HEADS, cols_padded), F32),
            pltpu.VMEM((rows_i * TRI_HEADS, cols_padded), BF16),
            pltpu.VMEM((n_b, n_c, n_as, n_pb, rows_i * TRI_HEADS, cols_padded), BF16),
            dma((n_a,)),
            dma((n_as * n_pb,)),
            dma((n_as * n_pb * mates,)),
            dma((n_src * n_pb,)),
            dma((n_a,)),
            dma((n_as * n_pb,)),
            dma((mates,)),
            dma((n_b * n_c,)),
        ],
        compiler_params=pltpu.CompilerParams(
            collective_id=0, has_side_effects=True, vmem_limit_bytes=56 * 1024 * 1024
        ),
    )(*inputs)
    hbm = pl.BlockSpec(memory_space=pltpu.HBM)
    msa, pair_out = pl.pallas_call(
        finish,
        out_shape=(
            jax.ShapeDtypeStruct(msa.shape, BF16),
            jax.ShapeDtypeStruct(pair_out.shape, BF16),
        ),
        in_specs=[hbm] * 2,
        out_specs=(hbm, hbm),
        scratch_shapes=[dma((2,))],
        compiler_params=pltpu.CompilerParams(vmem_limit_bytes=56 * 1024 * 1024),
    )(msa, pair_out)
    msa = msa.reshape(seqs, tiles, rows_i, LANES).transpose(0, 2, 1, 3).reshape(x.shape)
    return msa, pair_out.reshape(rows_i, cols, pwidth)


def solution(mesh):
    n_row, n_br, n_pb = mesh.shape["row"], mesh.shape["br"], mesh.shape["pb"]
    n_b = 2 if n_row % (2 * n_pb) == 0 else 1
    sizes = (n_pb, n_row // n_b, n_b, n_br)
    return jax.shard_map(
        functools.partial(on_device, sizes),
        mesh=mesh,
        in_specs=(
            P(("grp", "pb"), ("row", "br"), None),
            P(("grp", "row", "br"), "pb", None),
            P("grp"),
            P("grp"),
            P("grp"),
        )
        + (P(),) * 12,
        out_specs=(P(("grp", "pb"), ("row", "br"), None), P(("grp", "row", "br"), "pb", None)),
        check_vma=False,
    )
```

```python
import functools

import jax
import jax.numpy as jnp
from jax import lax
from jax.experimental import pallas as pl
from jax.experimental.pallas import tpu as pltpu
from jax.sharding import PartitionSpec as P

VERTICAL_ATTENDS = 8
TRI_HEADS = 4
SUBSPACE_DEPTH = 32
RELPOS_MAX = 32

NORM_EPS = 1e-05
MASK_NEGATIVE = 1000000000.0
LANES = 128
SUBLANES = 8
MESH = pl.DeviceIdType.MESH
F32 = jnp.float32
BF16 = jnp.bfloat16

WEIGHTS = (
    "rel", "qkvg", "vproj", "expand", "contract", "duo", "tensor", "tri", "tbias", "tout", "up", "down",
)


INPUTS = (
    "x", "chain", "duo", "positions", "scalars", "rel", "pair", "tbias", "qkvg", "tri", "tensor",
    "vproj", "expand", "contract", "resolved", "tout", "up", "down",
)


def normalize(values):
    centre = jnp.mean(values, axis=-1, keepdims=True)
    centred = values - centre
    spread = jnp.mean(centred * centred, axis=-1, keepdims=True)
    return (centred * lax.rsqrt(spread + NORM_EPS)).astype(BF16)


def matmul(a, b):
    return jnp.dot(a, b, preferred_element_type=F32)


def matmul_nt(a, b):
    return lax.dot_general(a, b, (((1,), (1,)), ((), ())), preferred_element_type=F32)


def matmul_tn(a, b):
    return lax.dot_general(a, b, (((0,), (0,)), ((), ())), preferred_element_type=F32)


def softmax_rows(scores):
    exp_scores = jnp.exp(scores - jnp.max(scores, axis=-1, keepdims=True))
    return (exp_scores * (1.0 / jnp.sum(exp_scores, axis=-1, keepdims=True))).astype(BF16)


def head_stack(values, heads):
    rows, width = values.shape
    lane = lax.broadcasted_iota(jnp.int32, (rows, width), 1) // SUBSPACE_DEPTH
    return jnp.concatenate(
        [jnp.where(lane == h, values, 0.0) for h in range(heads)], axis=0
    ).astype(BF16)


def head_merge(stacked, heads):
    rows, width = stacked.shape[0] // heads, stacked.shape[1]
    lane = lax.broadcasted_iota(jnp.int32, (rows, width), 1) // SUBSPACE_DEPTH
    total = jnp.zeros((rows, width), F32)
    for h in range(heads):
        total = jnp.where(lane == h, stacked[h * rows : (h + 1) * rows], total)
    return total


def kernel(sizes, shape, *refs):
    n_pb, n_a, n_b, n_c = sizes
    count = len(INPUTS)
    hbm = dict(zip(INPUTS, refs[:count]))
    out_msa, out_pair = refs[count : 2 + count]
    w = dict(zip(INPUTS, refs[2 + count : 2 + 2 * count]))
    (xg, pg, xn_s, k_s, v_s, left_s, msg_s, gather, bias_s, pairin_s, tkv_s, wf_s, wp_s, opm_s,
     flat_s, msa_s, pair_s, wsem, sx, rx, sp, rp, bt_s, bmsg_s, bgather, s1, r1, s2, r2, sb1, rb1, sb2, rb2) = refs[2 + 2 * count :]
    x_ref, pair_ref = w["x"], w["pair"]
    rows_i, seqs, width = shape
    tiles = width // LANES
    cells, pwidth = pair_ref.shape
    cols = cells // rows_i
    residues = w["resolved"].shape[1]
    n_as = n_a // n_pb
    n_src = n_as * n_b * n_c
    factor = w["duo"].shape[0] // 2
    eparts = factor // SUBLANES
    seq_blocks = eparts * seqs // LANES
    factor_rows = rows_i * SUBLANES

    grp = lax.axis_index("grp")
    row = lax.axis_index("row")
    c_me = lax.axis_index("br")
    p_me = lax.axis_index("pb")
    a_me, b_me = row // n_b, row % n_b
    scale = SUBSPACE_DEPTH ** (-0.5)

    def device(a, b, c, p):
        return (grp, a * n_b + b, c, p)

    loads = {}
    for n, name in enumerate(INPUTS):
        loads[name] = pltpu.make_async_copy(hbm[name], w[name], wsem.at[n])
    for name in INPUTS:
        loads[name].start()

    barrier = pltpu.get_barrier_semaphore()
    line = [(da, dp) for da in range(n_a) for dp in range(n_pb) if (da, dp) != (0, 0)]
    mates = [(db, dc) for db in range(n_b) for dc in range(n_c) if (db, dc) != (0, 0)]
    for da, dp in line:
        pl.semaphore_signal(
            barrier, inc=1, device_id=device((a_me + da) % n_a, b_me, c_me, (p_me + dp) % n_pb), device_id_type=MESH
        )
    for db, dc in mates:
        pl.semaphore_signal(
            barrier, inc=1, device_id=device(a_me, (b_me + db) % n_b, (c_me + dc) % n_c, p_me), device_id_type=MESH
        )

    def by_residue(block):
        flat_s[...] = block.astype(F32)
        return jnp.concatenate(
            [
                jnp.concatenate(
                    [flat_s[pl.ds(t * rows_i + r, seqs, stride=tiles * rows_i), :] for t in range(tiles)], axis=1
                )
                for r in range(rows_i)
            ],
            axis=0,
        )

    loads["x"].wait()
    x_own = by_residue(x_ref[...])
    xn_own = normalize(x_own)
    xn_s[p_me] = xn_own
    loads["chain"].wait()
    loads["duo"].wait()
    chain = w["chain"][...].astype(F32)
    own_chain = jnp.zeros((1, seqs), F32)
    for p in range(n_pb):
        own_chain = jnp.where(p_me == p, chain[:, p * seqs : (p + 1) * seqs], own_chain)
    rt = matmul_nt(w["duo"][factor:, :], xn_own) * jnp.concatenate([own_chain] * rows_i, axis=1)
    for j in range(rows_i):
        parts = jnp.concatenate(
            [rt[q * SUBLANES : (q + 1) * SUBLANES, j * seqs : (j + 1) * seqs] for q in range(eparts)], axis=1
        )
        for b in range(seq_blocks):
            at = b * factor_rows + j * SUBLANES
            opm_s[at : at + SUBLANES, :] = parts[:, b * LANES : (b + 1) * LANES]

    msg_s[...] = opm_s[: msg_s.shape[0], :].astype(BF16)

    p_to, a_slot = a_me // n_as, a_me % n_as
    stays = p_to == p_me

    def slot_of(a, b, c):
        return (a * n_b + b) * n_c + c

    def first(d):
        return pltpu.make_async_remote_copy(
            src_ref=msg_s, dst_ref=gather.at[slot_of(a_slot, b_me, c_me), p_me], send_sem=s1.at[d],
            recv_sem=r1.at[a_slot * n_pb + p_me], device_id=device((a_me + d) % n_a, b_me, c_me, p_to),
            device_id_type=MESH)

    def first_bias(d):
        return pltpu.make_async_remote_copy(
            src_ref=bmsg_s, dst_ref=bgather.at[b_me, c_me, a_slot, p_me], send_sem=sb1.at[d],
            recv_sem=rb1.at[a_slot * n_pb + p_me], device_id=device((a_me + d) % n_a, b_me, c_me, p_to),
            device_id_type=MESH)

    def second(da, dp, m):
        a, p = (a_slot + da) % n_as, (p_me + dp) % n_pb
        slot = slot_of(a, b_me, c_me)
        db, dc = mates[m]
        return pltpu.make_async_remote_copy(
            src_ref=gather.at[slot, p], dst_ref=gather.at[slot, p],
            send_sem=s2.at[(da * n_pb + dp) * len(mates) + m], recv_sem=r2.at[slot * n_pb + p],
            device_id=device(a_me, (b_me + db) % n_b, (c_me + dc) % n_c, p_me), device_id_type=MESH)

    def second_bias(m):
        db, dc = mates[m]
        return pltpu.make_async_remote_copy(
            src_ref=bgather.at[b_me, c_me], dst_ref=bgather.at[b_me, c_me], send_sem=sb2.at[m],
            recv_sem=rb2.at[b_me * n_c + c_me],
            device_id=device(a_me, (b_me + db) % n_b, (c_me + dc) % n_c, p_me), device_id_type=MESH)

    pl.semaphore_wait(barrier, len(line) + len(mates))

    for d in range(1, n_a):
        first(d).start()

    @pl.when(jnp.logical_not(stays))
    def _():
        first(0).start()

    @pl.when(stays)
    def _():
        gather[slot_of(a_slot, b_me, c_me), p_me] = msg_s[...]
        for m in range(len(mates)):
            second(0, 0, m).start()

    exchange = []
    for d in range(1, n_pb):
        peer = device(a_me, b_me, c_me, (p_me + d) % n_pb)
        exchange.append((
            pltpu.make_async_remote_copy(
                src_ref=pair_ref, dst_ref=pg.at[n_pb - d], send_sem=sp.at[d], recv_sem=rp.at[n_pb - d],
                device_id=peer, device_id_type=MESH),
            pltpu.make_async_remote_copy(
                src_ref=x_ref, dst_ref=xg.at[n_pb - d], send_sem=sx.at[d], recv_sem=rx.at[n_pb - d],
                device_id=peer, device_id_type=MESH),
        ))
    loads["pair"].wait()
    for copy, _ in exchange:
        copy.start()
    for _, copy in exchange:
        copy.start()

    row_first = (row * n_c + c_me) * rows_i
    bins = 2 * RELPOS_MAX + 1
    loads["positions"].wait()
    loads["scalars"].wait()
    loads["rel"].wait()
    for i in range(rows_i):
        offset = jnp.clip(w["scalars"][row_first + i] - w["positions"][...], -RELPOS_MAX, RELPOS_MAX) + RELPOS_MAX
        hot = lax.broadcasted_iota(jnp.int32, (bins, residues), 0) == offset
        added = matmul_tn(jnp.where(hot, 1.0, 0.0).astype(BF16), w["rel"][...])
        for p in range(n_pb):
            pairin_s[p, i * cols : (i + 1) * cols] = added[p * cols : (p + 1) * cols]
    pair_in = pairin_s[p_me] + pair_ref[...].astype(F32)
    pn_own = normalize(pair_in)
    loads["tbias"].wait()
    bt = matmul_nt(w["tbias"][...], pn_own)
    bt_s[...] = jnp.zeros_like(bt_s)
    for i in range(rows_i):
        for h in range(TRI_HEADS):
            at = h * rows_i + i
            bt_s[at : at + 1, :cols] = bt[h : h + 1, i * cols : (i + 1) * cols]
    bmsg_s[...] = bt_s[...].astype(BF16)
    for d in range(1, n_a):
        first_bias(d).start()

    @pl.when(jnp.logical_not(stays))
    def _():
        first_bias(0).start()

    @pl.when(stays)
    def _():
        bgather[b_me, c_me, a_slot, p_me] = bmsg_s[...]

    loads["qkvg"].wait()
    proj = matmul(xn_own, w["qkvg"][...])
    query = proj[:, :width].astype(BF16).astype(F32)
    gate = jax.nn.sigmoid(proj[:, 3 * width :].astype(BF16).astype(F32))
    k_s[p_me] = proj[:, width : 2 * width].astype(BF16)
    v_s[p_me] = proj[:, 2 * width : 3 * width].astype(BF16)

    loads["tri"].wait()
    tri_w = w["tri"][...].astype(F32)
    tri_w = jnp.concatenate(
        [
            tri_w[:, (h * 4 + kind) * SUBSPACE_DEPTH : (h * 4 + kind + 1) * SUBSPACE_DEPTH]
            for kind in range(4)
            for h in range(TRI_HEADS)
        ],
        axis=1,
    ).astype(BF16)
    tproj = matmul(pn_own, tri_w)
    tkv_s[p_me] = tproj[:, pwidth : 3 * pwidth].astype(BF16)
    tri_q = tproj[:, :pwidth].astype(BF16).astype(F32)
    tri_gate = jax.nn.sigmoid(tproj[:, 3 * pwidth :].astype(BF16).astype(F32))
    loads["tensor"].wait()
    wf_s[...] = w["tensor"][...].astype(F32)
    for e in range(SUBLANES):
        for q in range(eparts):
            at = (e * eparts + q) * factor
            wp_s[at : at + factor, :] = wf_s[pl.ds(q * SUBLANES + e, factor, stride=factor), :].astype(BF16)

    def hand_on(da, dp):
        a, p = (a_slot + da) % n_as, (p_me + dp) % n_pb
        pltpu.make_async_remote_copy(
            src_ref=msg_s, dst_ref=gather.at[slot_of(a, b_me, c_me), p], send_sem=s1.at[0],
            recv_sem=r1.at[a * n_pb + p], device_id=device((a_me + 1) % n_a, b_me, c_me, p_me),
            device_id_type=MESH).wait_recv()
        for m in range(len(mates)):
            second(da, dp, m).start()

    def bias_in(da, dp):
        a, p = (a_slot + da) % n_as, (p_me + dp) % n_pb
        pltpu.make_async_remote_copy(
            src_ref=bmsg_s, dst_ref=bgather.at[b_me, c_me, a, p], send_sem=sb1.at[0],
            recv_sem=rb1.at[a * n_pb + p], device_id=device((a_me + 1) % n_a, b_me, c_me, p_me),
            device_id_type=MESH).wait_recv()

    arrivals = [(da, dp) for da in range(n_as) for dp in range(n_pb)]
    for da, dp in arrivals[1:]:
        hand_on(da, dp)

    @pl.when(jnp.logical_not(stays))
    def _():
        hand_on(0, 0)
        bias_in(0, 0)

    for da, dp in arrivals[1:]:
        bias_in(da, dp)
    for m in range(len(mates)):
        second_bias(m).start()

    for slot in range(1, n_pb):
        exchange[n_pb - slot - 1][0].wait_recv()
    for d in range(1, n_pb):
        p = (p_me + d) % n_pb
        pn = normalize(pairin_s[p] + pg[d].astype(F32))
        tkv_s[p] = matmul(pn, tri_w[:, pwidth : 3 * pwidth]).astype(BF16)

    for slot in range(1, n_pb):
        exchange[n_pb - slot - 1][1].wait_recv()
    for d in range(1, n_pb):
        p = (p_me + d) % n_pb
        xn = normalize(by_residue(xg[d]))
        xn_s[p] = xn
        kv = matmul(xn, w["qkvg"][:, width : 3 * width])
        k_s[p] = kv[:, :width].astype(BF16)
        v_s[p] = kv[:, width:].astype(BF16)

    left_w = jnp.concatenate([w["duo"][:factor, :]] * eparts, axis=0)
    lane_part = lax.broadcasted_iota(jnp.int32, (seqs, LANES), 1) // factor
    for p in range(n_pb):
        left4 = matmul_nt(xn_s[p], left_w)
        for i in range(rows_i):
            block = left4[i * seqs : (i + 1) * seqs]
            for q in range(eparts):
                left_s[(p * eparts + q) * seqs : (p * eparts + q + 1) * seqs, i * LANES : (i + 1) * LANES] = (
                    jnp.where(lane_part == q, block, 0.0).astype(BF16)
                )

    seq_bias = (chain - 1.0) * MASK_NEGATIVE
    mixed = []
    for r in range(rows_i):
        span = slice(r * seqs, (r + 1) * seqs)
        keys = jnp.concatenate([k_s[p, span, :] for p in range(n_pb)], axis=0)
        values = jnp.concatenate([v_s[p, span, :] for p in range(n_pb)], axis=0)
        scores = matmul_nt(head_stack(query[span], VERTICAL_ATTENDS), keys) * scale + seq_bias
        weighted = matmul(softmax_rows(scores), values)
        mixed.append((gate[span] * head_merge(weighted, VERTICAL_ATTENDS)).astype(BF16))

    loads["vproj"].wait()
    mid = x_own + matmul(jnp.concatenate(mixed, axis=0), w["vproj"][...])
    loads["expand"].wait()
    hidden = jnp.maximum(matmul(normalize(mid), w["expand"][...]), 0.0).astype(BF16)
    loads["contract"].wait()
    fresh = mid + matmul(hidden, w["contract"][...])
    for r in range(rows_i):
        for t in range(tiles):
            flat_s[pl.ds(t * rows_i + r, seqs, stride=tiles * rows_i), :] = fresh[
                r * seqs : (r + 1) * seqs, t * LANES : (t + 1) * LANES
            ]
    out_msa[...] = flat_s[...].astype(BF16)

    for db, dc in mates:
        b, c = (b_me + db) % n_b, (c_me + dc) % n_c
        pltpu.make_async_remote_copy(
            src_ref=bgather.at[b, c], dst_ref=bgather.at[b, c], send_sem=sb2.at[0], recv_sem=rb2.at[b * n_c + c],
            device_id=device(a_me, b, c, p_me), device_id_type=MESH).wait_recv()
    for s in range(n_src):
        part = jnp.concatenate(
            [bgather[s // n_c % n_b, s % n_c, s // (n_b * n_c), p].astype(F32)[:, :cols] for p in range(n_pb)], axis=1
        )
        for h in range(TRI_HEADS):
            bias_s[h * cols + s * rows_i : h * cols + (s + 1) * rows_i, :] = part[h * rows_i : (h + 1) * rows_i, :]
    loads["resolved"].wait()
    bias = bias_s[...] + (w["resolved"][...].astype(F32) - 1.0) * MASK_NEGATIVE
    tri_mixed = []
    for i in range(rows_i):
        span = slice(i * cols, (i + 1) * cols)
        keys = jnp.concatenate([tkv_s[p, span, :pwidth] for p in range(n_pb)], axis=0)
        values = jnp.concatenate([tkv_s[p, span, pwidth:] for p in range(n_pb)], axis=0)
        scores = matmul_nt(head_stack(tri_q[span], TRI_HEADS), keys) * scale + bias
        weighted = matmul(softmax_rows(scores), values)
        tri_mixed.append((tri_gate[span] * head_merge(weighted, TRI_HEADS)).astype(BF16))
    loads["tout"].wait()
    tri_update = matmul(jnp.concatenate(tri_mixed, axis=0), w["tout"][...])

    for a in range(n_as):
        for p in range(n_pb):
            for db, dc in mates:
                b, c = (b_me + db) % n_b, (c_me + dc) % n_c
                slot = slot_of(a, b, c)
                pltpu.make_async_remote_copy(
                    src_ref=gather.at[slot, p], dst_ref=gather.at[slot, p], send_sem=s2.at[0],
                    recv_sem=r2.at[slot * n_pb + p], device_id=device(a_me, b, c, p_me),
                    device_id_type=MESH).wait_recv()

    right_all = jnp.concatenate(
        [
            jnp.concatenate(
                [
                    gather[s, p, b * factor_rows : (b + 1) * factor_rows, :]
                    for p in range(n_pb)
                    for b in range(seq_blocks)
                ],
                axis=1,
            )
            for s in range(n_src)
        ],
        axis=0,
    )
    outer = matmul(right_all, left_s[...])
    opm_s[: cells * SUBLANES, :] = jnp.concatenate(
        [outer[:, i * LANES : (i + 1) * LANES] for i in range(rows_i)], axis=0
    )
    lhs = jnp.concatenate(
        [opm_s[pl.ds(e, cells, stride=SUBLANES), :].astype(BF16) for e in range(SUBLANES)], axis=1
    )
    opm = matmul(lhs, wp_s[...]) / jnp.sum(chain)

    pair_mid = pair_in + tri_update + opm
    loads["up"].wait()
    pair_hidden = jnp.maximum(matmul(normalize(pair_mid), w["up"][...]), 0.0).astype(BF16)
    loads["down"].wait()
    out_pair[...] = (pair_mid + matmul(pair_hidden, w["down"][...])).astype(BF16)

    for copies in exchange:
        for copy in copies:
            copy.wait_send()
    for m in range(len(mates)):
        for da, dp in arrivals:
            second(da, dp, m).wait_send()
        second_bias(m).wait_send()
    for d in range(1, n_a):
        first(d).wait_send()
        first_bias(d).wait_send()

    @pl.when(jnp.logical_not(stays))
    def _():
        first(0).wait_send()
        first_bias(0).wait_send()


def finish(msa_ref, pair_ref, out_msa, out_pair, sem):
    copies = [
        pltpu.make_async_copy(msa_ref, out_msa, sem.at[0]),
        pltpu.make_async_copy(pair_ref, out_pair, sem.at[1]),
    ]
    for copy in copies:
        copy.start()
    for copy in copies:
        copy.wait()


def on_device(sizes, x, pair, chain, resolved, positions, *weights):
    seqs, rows_i, width = x.shape
    cols, pwidth = pair.shape[1:]
    n_pb, n_a, n_b, n_c = sizes
    cells = rows_i * cols
    chains, residues = chain.shape[0], resolved.shape[0]
    n_as = n_a // n_pb
    n_src = n_as * n_b * n_c
    arrays = dict(zip(WEIGHTS, weights))
    arrays["duo"] = arrays["duo"].T
    arrays["tbias"] = arrays["tbias"].T
    tiles = width // LANES
    arrays["x"] = x.reshape(seqs, rows_i, tiles, LANES).transpose(0, 2, 1, 3).reshape(-1, LANES)
    arrays["pair"] = pair.reshape(cells, pwidth)
    arrays["chain"] = chain.reshape(1, chains)
    arrays["resolved"] = resolved.reshape(1, residues)
    arrays["positions"] = positions.reshape(1, residues)
    arrays["scalars"] = positions
    inputs = [arrays[name] for name in INPUTS]
    factor = arrays["duo"].shape[0] // 2
    eparts = factor // SUBLANES
    msg_rows = eparts * seqs // LANES * rows_i * SUBLANES
    mates = n_b * n_c - 1
    cols_padded = -(-cols // LANES) * LANES
    dma = pltpu.SemaphoreType.DMA
    msa, pair_out = pl.pallas_call(
        functools.partial(kernel, sizes, (rows_i, seqs, width)),
        out_shape=(
            pltpu.VMEM(arrays["x"].shape, BF16),
            pltpu.VMEM((cells, pwidth), BF16),
        ),
        in_specs=[pl.BlockSpec(memory_space=pltpu.HBM)] * len(inputs),
        out_specs=(pl.BlockSpec(memory_space=pltpu.VMEM),) * 2,
        scratch_shapes=[
            (pltpu.SMEM if name == "scalars" else pltpu.VMEM)(v.shape, v.dtype) for name, v in zip(INPUTS, inputs)
        ]
        + [
            pltpu.VMEM((n_pb,) + arrays["x"].shape, BF16),
            pltpu.VMEM((n_pb, cells, pwidth), BF16),
            pltpu.VMEM((n_pb, rows_i * seqs, width), BF16),
            pltpu.VMEM((n_pb, rows_i * seqs, width), BF16),
            pltpu.VMEM((n_pb, rows_i * seqs, width), BF16),
            pltpu.VMEM((n_pb * eparts * seqs, rows_i * LANES), BF16),
            pltpu.VMEM((msg_rows, LANES), BF16),
            pltpu.VMEM((n_src, n_pb, msg_rows, LANES), BF16),
            pltpu.VMEM((TRI_HEADS * cols, residues), F32),
            pltpu.VMEM((n_pb, cells, pwidth), F32),
            pltpu.VMEM((n_pb, cells, 2 * pwidth), BF16),
            pltpu.VMEM(arrays["tensor"].shape, F32),
            pltpu.VMEM(arrays["tensor"].shape, BF16),
            pltpu.VMEM((max(cells * SUBLANES, msg_rows), LANES), F32),
            pltpu.VMEM(arrays["x"].shape, F32),
            pltpu.VMEM(arrays["x"].shape, BF16),
            pltpu.VMEM((cells, pwidth), BF16),
            dma((len(inputs) + 2,)),
            dma((n_pb,)),
            dma((n_pb,)),
            dma((n_pb,)),
            dma((n_pb,)),
            pltpu.VMEM((rows_i * TRI_HEADS, cols_padded), F32),
            pltpu.VMEM((rows_i * TRI_HEADS, cols_padded), BF16),
            pltpu.VMEM((n_b, n_c, n_as, n_pb, rows_i * TRI_HEADS, cols_padded), BF16),
            dma((n_a,)),
            dma((n_as * n_pb,)),
            dma((n_as * n_pb * mates,)),
            dma((n_src * n_pb,)),
            dma((n_a,)),
            dma((n_as * n_pb,)),
            dma((mates,)),
            dma((n_b * n_c,)),
        ],
        compiler_params=pltpu.CompilerParams(
            collective_id=0, has_side_effects=True, vmem_limit_bytes=56 * 1024 * 1024
        ),
    )(*inputs)
    hbm = pl.BlockSpec(memory_space=pltpu.HBM)
    vmem = pl.BlockSpec(memory_space=pltpu.VMEM)
    msa, pair_out = pl.pallas_call(
        finish,
        out_shape=(
            jax.ShapeDtypeStruct(msa.shape, BF16),
            jax.ShapeDtypeStruct(pair_out.shape, BF16),
        ),
        in_specs=[vmem] * 2,
        out_specs=(hbm, hbm),
        scratch_shapes=[dma((2,))],
        compiler_params=pltpu.CompilerParams(vmem_limit_bytes=8 * 1024 * 1024),
    )(msa, pair_out)
    msa = msa.reshape(seqs, tiles, rows_i, LANES).transpose(0, 2, 1, 3).reshape(x.shape)
    return msa, pair_out.reshape(rows_i, cols, pwidth)


def solution(mesh):
    n_row, n_br, n_pb = mesh.shape["row"], mesh.shape["br"], mesh.shape["pb"]
    n_b = 2 if n_row % (2 * n_pb) == 0 else 1
    sizes = (n_pb, n_row // n_b, n_b, n_br)
    return jax.shard_map(
        functools.partial(on_device, sizes),
        mesh=mesh,
        in_specs=(
            P(("grp", "pb"), ("row", "br"), None),
            P(("grp", "row", "br"), "pb", None),
            P("grp"),
            P("grp"),
            P("grp"),
        )
        + (P(),) * 12,
        out_specs=(P(("grp", "pb"), ("row", "br"), None), P(("grp", "row", "br"), "pb", None)),
        check_vma=False,
    )
```

```python
import functools

import jax
import jax.numpy as jnp
from jax import lax
from jax.experimental import pallas as pl
from jax.experimental.pallas import tpu as pltpu
from jax.sharding import PartitionSpec as P

VERTICAL_ATTENDS = 8
TRI_HEADS = 4
SUBSPACE_DEPTH = 32
RELPOS_MAX = 32

NORM_EPS = 1e-05
MASK_NEGATIVE = 1000000000.0
LANES = 128
SUBLANES = 8
MESH = pl.DeviceIdType.MESH
F32 = jnp.float32
BF16 = jnp.bfloat16

WEIGHTS = (
    "rel", "qkvg", "vproj", "expand", "contract", "duo", "tensor", "tri", "tbias", "tout", "up", "down",
)


INPUTS = (
    "x", "chain", "duo", "positions", "scalars", "rel", "pair", "tbias", "qkvg", "tri", "tensor",
    "vproj", "expand", "contract", "resolved", "tout", "up", "down",
)


def normalize(values):
    centre = jnp.mean(values, axis=-1, keepdims=True)
    centred = values - centre
    spread = jnp.mean(centred * centred, axis=-1, keepdims=True)
    return (centred * lax.rsqrt(spread + NORM_EPS)).astype(BF16)


def matmul(a, b):
    return jnp.dot(a, b, preferred_element_type=F32)


def matmul_nt(a, b):
    return lax.dot_general(a, b, (((1,), (1,)), ((), ())), preferred_element_type=F32)


def matmul_tn(a, b):
    return lax.dot_general(a, b, (((0,), (0,)), ((), ())), preferred_element_type=F32)


def softmax_rows(scores):
    exp_scores = jnp.exp(scores - jnp.max(scores, axis=-1, keepdims=True))
    return (exp_scores * (1.0 / jnp.sum(exp_scores, axis=-1, keepdims=True))).astype(BF16)


def head_stack(values, heads):
    rows, width = values.shape
    lane = lax.broadcasted_iota(jnp.int32, (rows, width), 1) // SUBSPACE_DEPTH
    return jnp.concatenate(
        [jnp.where(lane == h, values, 0.0) for h in range(heads)], axis=0
    ).astype(BF16)


def head_merge(stacked, heads):
    rows, width = stacked.shape[0] // heads, stacked.shape[1]
    lane = lax.broadcasted_iota(jnp.int32, (rows, width), 1) // SUBSPACE_DEPTH
    total = jnp.zeros((rows, width), F32)
    for h in range(heads):
        total = jnp.where(lane == h, stacked[h * rows : (h + 1) * rows], total)
    return total


def kernel(sizes, shape, *refs):
    n_pb, n_a, n_b, n_c = sizes
    count = len(INPUTS)
    hbm = dict(zip(INPUTS, refs[:count]))
    out_msa, out_pair = refs[count : 2 + count]
    w = dict(zip(INPUTS, refs[2 + count : 2 + 2 * count]))
    (xg, pg, k_s, v_s, left_s, msg_s, gather, bias_s, pairin_s, tkv_s, wf_s, wp_s, opm_s,
     flat_s, wsem, sx, rx, sp, rp, s1, r1, s2, r2) = refs[2 + 2 * count :]
    x_ref, pair_ref = w["x"], w["pair"]
    rows_i, seqs, width = shape
    tiles = width // LANES
    cells, pwidth = pair_ref.shape
    cols = cells // rows_i
    residues = w["resolved"].shape[1]
    n_as = n_a // n_pb
    n_src = n_as * n_b * n_c
    factor = w["duo"].shape[0] // 2
    eparts = factor // SUBLANES
    seq_blocks = eparts * seqs // LANES
    factor_rows = rows_i * SUBLANES
    base = seq_blocks * factor_rows

    grp = lax.axis_index("grp")
    row = lax.axis_index("row")
    c_me = lax.axis_index("br")
    p_me = lax.axis_index("pb")
    a_me, b_me = row // n_b, row % n_b
    scale = SUBSPACE_DEPTH ** (-0.5)

    def device(a, b, c, p):
        return (grp, a * n_b + b, c, p)

    loads = {}
    for n, name in enumerate(INPUTS):
        loads[name] = pltpu.make_async_copy(hbm[name], w[name], wsem.at[n])
    for name in INPUTS:
        loads[name].start()

    barrier = pltpu.get_barrier_semaphore()
    line = [(da, dp) for da in range(n_a) for dp in range(n_pb) if (da, dp) != (0, 0)]
    mates = [(db, dc) for db in range(n_b) for dc in range(n_c) if (db, dc) != (0, 0)]
    for da, dp in line:
        pl.semaphore_signal(
            barrier, inc=1, device_id=device((a_me + da) % n_a, b_me, c_me, (p_me + dp) % n_pb), device_id_type=MESH
        )
    for db, dc in mates:
        pl.semaphore_signal(
            barrier, inc=1, device_id=device(a_me, (b_me + db) % n_b, (c_me + dc) % n_c, p_me), device_id_type=MESH
        )

    def by_residue(block):
        flat_s[...] = block.astype(F32)
        return jnp.concatenate(
            [
                jnp.concatenate(
                    [flat_s[pl.ds(t * rows_i + r, seqs, stride=tiles * rows_i), :] for t in range(tiles)], axis=1
                )
                for r in range(rows_i)
            ],
            axis=0,
        )

    loads["x"].wait()
    x_own = by_residue(x_ref[...])
    xn_own = normalize(x_own)
    loads["chain"].wait()
    loads["duo"].wait()
    chain = w["chain"][...].astype(F32)
    own_chain = jnp.zeros((1, seqs), F32)
    for p in range(n_pb):
        own_chain = jnp.where(p_me == p, chain[:, p * seqs : (p + 1) * seqs], own_chain)
    rt = matmul_nt(w["duo"][factor:, :], xn_own) * jnp.concatenate([own_chain] * rows_i, axis=1)
    for j in range(rows_i):
        parts = jnp.concatenate(
            [rt[q * SUBLANES : (q + 1) * SUBLANES, j * seqs : (j + 1) * seqs] for q in range(eparts)], axis=1
        )
        for b in range(seq_blocks):
            at = b * factor_rows + j * SUBLANES
            opm_s[at : at + SUBLANES, :] = parts[:, b * LANES : (b + 1) * LANES]

    row_first = (row * n_c + c_me) * rows_i
    bins = 2 * RELPOS_MAX + 1
    loads["positions"].wait()
    loads["scalars"].wait()
    loads["rel"].wait()
    for i in range(rows_i):
        offset = jnp.clip(w["scalars"][row_first + i] - w["positions"][...], -RELPOS_MAX, RELPOS_MAX) + RELPOS_MAX
        hot = lax.broadcasted_iota(jnp.int32, (bins, residues), 0) == offset
        added = matmul_tn(jnp.where(hot, 1.0, 0.0).astype(BF16), w["rel"][...])
        for p in range(n_pb):
            pairin_s[p, i * cols : (i + 1) * cols] = added[p * cols : (p + 1) * cols]
    loads["pair"].wait()
    pair_in = pairin_s[p_me] + pair_ref[...].astype(F32)
    pn_own = normalize(pair_in)
    loads["tbias"].wait()
    bt = matmul_nt(w["tbias"][...], pn_own)
    for i in range(rows_i):
        for h in range(TRI_HEADS):
            at = base + h * rows_i + i
            opm_s[at : at + 1, :cols] = bt[h : h + 1, i * cols : (i + 1) * cols]
    msg_s[...] = opm_s[: msg_s.shape[0], :].astype(BF16)

    loads["qkvg"].wait()
    proj = matmul(xn_own, w["qkvg"][...])
    query = proj[:, :width].astype(BF16).astype(F32)
    gate = jax.nn.sigmoid(proj[:, 3 * width :].astype(BF16).astype(F32))
    k_s[p_me] = proj[:, width : 2 * width].astype(BF16)
    v_s[p_me] = proj[:, 2 * width : 3 * width].astype(BF16)

    loads["tri"].wait()
    tri_w = w["tri"][...].astype(F32)
    tri_w = jnp.concatenate(
        [
            tri_w[:, (h * 4 + kind) * SUBSPACE_DEPTH : (h * 4 + kind + 1) * SUBSPACE_DEPTH]
            for kind in range(4)
            for h in range(TRI_HEADS)
        ],
        axis=1,
    ).astype(BF16)
    tproj = matmul(pn_own, tri_w)
    tkv_s[p_me] = tproj[:, pwidth : 3 * pwidth].astype(BF16)
    tri_q = tproj[:, :pwidth].astype(BF16).astype(F32)
    tri_gate = jax.nn.sigmoid(tproj[:, 3 * pwidth :].astype(BF16).astype(F32))
    loads["tensor"].wait()
    wf_s[...] = w["tensor"][...].astype(F32)
    for e in range(SUBLANES):
        for q in range(eparts):
            at = (e * eparts + q) * factor
            wp_s[at : at + factor, :] = wf_s[pl.ds(q * SUBLANES + e, factor, stride=factor), :].astype(BF16)

    left_w = jnp.concatenate([w["duo"][:factor, :]] * eparts, axis=0)
    lane_part = lax.broadcasted_iota(jnp.int32, (seqs, LANES), 1) // factor

    def put_left(p, xn):
        left4 = matmul_nt(xn, left_w)
        for i in range(rows_i):
            block = left4[i * seqs : (i + 1) * seqs]
            for q in range(eparts):
                left_s[p, q * seqs : (q + 1) * seqs, i * LANES : (i + 1) * LANES] = (
                    jnp.where(lane_part == q, block, 0.0).astype(BF16)
                )

    put_left(p_me, xn_own)

    pl.semaphore_wait(barrier, len(line) + len(mates))

    p_to, a_slot = a_me // n_as, a_me % n_as
    stays = p_to == p_me

    def slot_of(a, b, c):
        return (a * n_b + b) * n_c + c

    def first(d):
        return pltpu.make_async_remote_copy(
            src_ref=msg_s, dst_ref=gather.at[slot_of(a_slot, b_me, c_me), p_me], send_sem=s1.at[d],
            recv_sem=r1.at[a_slot * n_pb + p_me], device_id=device((a_me + d) % n_a, b_me, c_me, p_to),
            device_id_type=MESH)

    for d in range(1, n_a):
        first(d).start()

    @pl.when(jnp.logical_not(stays))
    def _():
        first(0).start()

    @pl.when(stays)
    def _():
        gather[slot_of(a_slot, b_me, c_me), p_me] = msg_s[...]

    exchange = []
    for d in range(1, n_pb):
        peer = device(a_me, b_me, c_me, (p_me + d) % n_pb)
        exchange.append((
            pltpu.make_async_remote_copy(
                src_ref=pair_ref, dst_ref=pg.at[n_pb - d], send_sem=sp.at[d], recv_sem=rp.at[n_pb - d],
                device_id=peer, device_id_type=MESH),
            pltpu.make_async_remote_copy(
                src_ref=x_ref, dst_ref=xg.at[n_pb - d], send_sem=sx.at[d], recv_sem=rx.at[n_pb - d],
                device_id=peer, device_id_type=MESH),
        ))
    for copy, _ in exchange:
        copy.start()
    for _, copy in exchange:
        copy.start()

    for slot in range(1, n_pb):
        exchange[n_pb - slot - 1][0].wait_recv()
    for d in range(1, n_pb):
        p = (p_me + d) % n_pb
        pn = normalize(pairin_s[p] + pg[d].astype(F32))
        tkv_s[p] = matmul(pn, tri_w[:, pwidth : 3 * pwidth]).astype(BF16)

    second = []
    for a in range(n_as):
        slot = slot_of(a, b_me, c_me)
        for p in range(n_pb):
            here = jnp.logical_and(stays, jnp.logical_and(a_slot == a, p_me == p))

            @pl.when(jnp.logical_not(here))
            def _():
                pltpu.make_async_remote_copy(
                    src_ref=msg_s, dst_ref=gather.at[slot, p], send_sem=s1.at[0], recv_sem=r1.at[a * n_pb + p],
                    device_id=device((a_me + 1) % n_a, b_me, c_me, p_me), device_id_type=MESH).wait_recv()

        for m, (db, dc) in enumerate(mates):
            copy = pltpu.make_async_remote_copy(
                src_ref=gather.at[slot], dst_ref=gather.at[slot], send_sem=s2.at[a * len(mates) + m],
                recv_sem=r2.at[slot],
                device_id=device(a_me, (b_me + db) % n_b, (c_me + dc) % n_c, p_me), device_id_type=MESH)
            copy.start()
            second.append(copy)

    for slot in range(1, n_pb):
        exchange[n_pb - slot - 1][1].wait_recv()
    for d in range(1, n_pb):
        p = (p_me + d) % n_pb
        xn = normalize(by_residue(xg[d]))
        put_left(p, xn)
        kv = matmul(xn, w["qkvg"][:, width : 3 * width])
        k_s[p] = kv[:, :width].astype(BF16)
        v_s[p] = kv[:, width:].astype(BF16)

    seq_bias = (chain - 1.0) * MASK_NEGATIVE
    mixed = []
    for r in range(rows_i):
        span = slice(r * seqs, (r + 1) * seqs)
        keys = jnp.concatenate([k_s[p, span, :] for p in range(n_pb)], axis=0)
        values = jnp.concatenate([v_s[p, span, :] for p in range(n_pb)], axis=0)
        scores = matmul_nt(head_stack(query[span], VERTICAL_ATTENDS), keys) * scale + seq_bias
        weighted = matmul(softmax_rows(scores), values)
        mixed.append((gate[span] * head_merge(weighted, VERTICAL_ATTENDS)).astype(BF16))

    loads["vproj"].wait()
    mid = x_own + matmul(jnp.concatenate(mixed, axis=0), w["vproj"][...])
    loads["expand"].wait()
    hidden = jnp.maximum(matmul(normalize(mid), w["expand"][...]), 0.0).astype(BF16)
    loads["contract"].wait()
    fresh = mid + matmul(hidden, w["contract"][...])
    for r in range(rows_i):
        for t in range(tiles):
            flat_s[pl.ds(t * rows_i + r, seqs, stride=tiles * rows_i), :] = fresh[
                r * seqs : (r + 1) * seqs, t * LANES : (t + 1) * LANES
            ]
    out_msa[...] = flat_s[...].astype(BF16)

    for a in range(n_as):
        for db, dc in mates:
            slot = slot_of(a, (b_me + db) % n_b, (c_me + dc) % n_c)
            pltpu.make_async_remote_copy(
                src_ref=gather.at[slot], dst_ref=gather.at[slot], send_sem=s2.at[0], recv_sem=r2.at[slot],
                device_id=device(a_me, (b_me + db) % n_b, (c_me + dc) % n_c, p_me), device_id_type=MESH).wait_recv()

    right_all = jnp.concatenate(
        [
            jnp.concatenate(
                [
                    gather[s, p, b * factor_rows : (b + 1) * factor_rows, :]
                    for p in range(n_pb)
                    for b in range(seq_blocks)
                ],
                axis=1,
            )
            for s in range(n_src)
        ],
        axis=0,
    )
    outer = matmul(right_all, left_s[...].reshape(n_pb * eparts * seqs, rows_i * LANES))
    opm_s[: cells * SUBLANES, :] = jnp.concatenate(
        [outer[:, i * LANES : (i + 1) * LANES] for i in range(rows_i)], axis=0
    )
    lhs = jnp.concatenate(
        [opm_s[pl.ds(e, cells, stride=SUBLANES), :].astype(BF16) for e in range(SUBLANES)], axis=1
    )
    opm = matmul(lhs, wp_s[...]) / jnp.sum(chain)

    for s in range(n_src):
        part = jnp.concatenate(
            [gather[s, p, base : base + rows_i * TRI_HEADS, :].astype(F32)[:, :cols] for p in range(n_pb)], axis=1
        )
        for h in range(TRI_HEADS):
            bias_s[h * cols + s * rows_i : h * cols + (s + 1) * rows_i, :] = part[h * rows_i : (h + 1) * rows_i, :]
    loads["resolved"].wait()
    bias = bias_s[...] + (w["resolved"][...].astype(F32) - 1.0) * MASK_NEGATIVE
    tri_mixed = []
    for i in range(rows_i):
        span = slice(i * cols, (i + 1) * cols)
        keys = jnp.concatenate([tkv_s[p, span, :pwidth] for p in range(n_pb)], axis=0)
        values = jnp.concatenate([tkv_s[p, span, pwidth:] for p in range(n_pb)], axis=0)
        scores = matmul_nt(head_stack(tri_q[span], TRI_HEADS), keys) * scale + bias
        weighted = matmul(softmax_rows(scores), values)
        tri_mixed.append((tri_gate[span] * head_merge(weighted, TRI_HEADS)).astype(BF16))
    loads["tout"].wait()
    pair_mid = pair_in + matmul(jnp.concatenate(tri_mixed, axis=0), w["tout"][...]) + opm
    loads["up"].wait()
    pair_hidden = jnp.maximum(matmul(normalize(pair_mid), w["up"][...]), 0.0).astype(BF16)
    loads["down"].wait()
    out_pair[...] = (pair_mid + matmul(pair_hidden, w["down"][...])).astype(BF16)

    for copies in exchange:
        for copy in copies:
            copy.wait_send()
    for copy in second:
        copy.wait_send()
    for d in range(1, n_a):
        first(d).wait_send()

    @pl.when(jnp.logical_not(stays))
    def _():
        first(0).wait_send()


def finish(msa_ref, pair_ref, out_msa, out_pair, sem):
    copies = [
        pltpu.make_async_copy(msa_ref, out_msa, sem.at[0]),
        pltpu.make_async_copy(pair_ref, out_pair, sem.at[1]),
    ]
    for copy in copies:
        copy.start()
    for copy in copies:
        copy.wait()


def on_device(sizes, x, pair, chain, resolved, positions, *weights):
    seqs, rows_i, width = x.shape
    cols, pwidth = pair.shape[1:]
    n_pb, n_a, n_b, n_c = sizes
    cells = rows_i * cols
    chains, residues = chain.shape[0], resolved.shape[0]
    n_as = n_a // n_pb
    n_src = n_as * n_b * n_c
    arrays = dict(zip(WEIGHTS, weights))
    arrays["duo"] = arrays["duo"].T
    arrays["tbias"] = arrays["tbias"].T
    tiles = width // LANES
    arrays["x"] = x.reshape(seqs, rows_i, tiles, LANES).transpose(0, 2, 1, 3).reshape(-1, LANES)
    arrays["pair"] = pair.reshape(cells, pwidth)
    arrays["chain"] = chain.reshape(1, chains)
    arrays["resolved"] = resolved.reshape(1, residues)
    arrays["positions"] = positions.reshape(1, residues)
    arrays["scalars"] = positions
    inputs = [arrays[name] for name in INPUTS]
    factor = arrays["duo"].shape[0] // 2
    eparts = factor // SUBLANES
    msg_rows = eparts * seqs // LANES * rows_i * SUBLANES + rows_i * TRI_HEADS
    mates = n_b * n_c - 1
    dma = pltpu.SemaphoreType.DMA
    msa, pair_out = pl.pallas_call(
        functools.partial(kernel, sizes, (rows_i, seqs, width)),
        out_shape=(
            pltpu.VMEM(arrays["x"].shape, BF16),
            pltpu.VMEM((cells, pwidth), BF16),
        ),
        in_specs=[pl.BlockSpec(memory_space=pltpu.HBM)] * len(inputs),
        out_specs=(pl.BlockSpec(memory_space=pltpu.VMEM),) * 2,
        scratch_shapes=[
            (pltpu.SMEM if name == "scalars" else pltpu.VMEM)(v.shape, v.dtype) for name, v in zip(INPUTS, inputs)
        ]
        + [
            pltpu.VMEM((n_pb,) + arrays["x"].shape, BF16),
            pltpu.VMEM((n_pb, cells, pwidth), BF16),
            pltpu.VMEM((n_pb, rows_i * seqs, width), BF16),
            pltpu.VMEM((n_pb, rows_i * seqs, width), BF16),
            pltpu.VMEM((n_pb, eparts * seqs, rows_i * LANES), BF16),
            pltpu.VMEM((msg_rows, LANES), BF16),
            pltpu.VMEM((n_src, n_pb, msg_rows, LANES), BF16),
            pltpu.VMEM((TRI_HEADS * cols, residues), F32),
            pltpu.VMEM((n_pb, cells, pwidth), F32),
            pltpu.VMEM((n_pb, cells, 2 * pwidth), BF16),
            pltpu.VMEM(arrays["tensor"].shape, F32),
            pltpu.VMEM(arrays["tensor"].shape, BF16),
            pltpu.VMEM((max(cells * SUBLANES, msg_rows), LANES), F32),
            pltpu.VMEM(arrays["x"].shape, F32),
            dma((len(inputs),)),
            dma((n_pb,)),
            dma((n_pb,)),
            dma((n_pb,)),
            dma((n_pb,)),
            dma((n_a,)),
            dma((n_as * n_pb,)),
            dma((n_as * mates,)),
            dma((n_src,)),
        ],
        compiler_params=pltpu.CompilerParams(
            collective_id=0, has_side_effects=True, vmem_limit_bytes=56 * 1024 * 1024
        ),
    )(*inputs)
    hbm = pl.BlockSpec(memory_space=pltpu.HBM)
    vmem = pl.BlockSpec(memory_space=pltpu.VMEM)
    msa, pair_out = pl.pallas_call(
        finish,
        out_shape=(
            jax.ShapeDtypeStruct(msa.shape, BF16),
            jax.ShapeDtypeStruct(pair_out.shape, BF16),
        ),
        in_specs=[vmem] * 2,
        out_specs=(hbm, hbm),
        scratch_shapes=[dma((2,))],
        compiler_params=pltpu.CompilerParams(vmem_limit_bytes=8 * 1024 * 1024),
    )(msa, pair_out)
    msa = msa.reshape(seqs, tiles, rows_i, LANES).transpose(0, 2, 1, 3).reshape(x.shape)
    return msa, pair_out.reshape(rows_i, cols, pwidth)


def solution(mesh):
    n_row, n_br, n_pb = mesh.shape["row"], mesh.shape["br"], mesh.shape["pb"]
    n_b = 2 if n_row % (2 * n_pb) == 0 else 1
    sizes = (n_pb, n_row // n_b, n_b, n_br)
    return jax.shard_map(
        functools.partial(on_device, sizes),
        mesh=mesh,
        in_specs=(
            P(("grp", "pb"), ("row", "br"), None),
            P(("grp", "row", "br"), "pb", None),
            P("grp"),
            P("grp"),
            P("grp"),
        )
        + (P(),) * 12,
        out_specs=(P(("grp", "pb"), ("row", "br"), None), P(("grp", "row", "br"), "pb", None)),
        check_vma=False,
    )
```

```python
import functools

import jax
import jax.numpy as jnp
from jax import lax
from jax.experimental import pallas as pl
from jax.experimental.pallas import tpu as pltpu
from jax.sharding import PartitionSpec as P

VERTICAL_ATTENDS = 8
TRI_HEADS = 4
SUBSPACE_DEPTH = 32
RELPOS_MAX = 32

NORM_EPS = 1e-05
MASK_NEGATIVE = 1000000000.0
LANES = 128
SUBLANES = 8
MESH = pl.DeviceIdType.MESH
F32 = jnp.float32
BF16 = jnp.bfloat16

WEIGHTS = (
    "rel", "qkvg", "vproj", "expand", "contract", "duo", "tensor", "tri", "tbias", "tout", "up", "down",
)


INPUTS = (
    "x", "chain", "duo", "positions", "scalars", "rel", "pair", "tbias", "qkvg", "tri", "tensor",
    "vproj", "expand", "contract", "resolved", "tout", "up", "down",
)


def normalize(values):
    centre = jnp.mean(values, axis=-1, keepdims=True)
    centred = values - centre
    spread = jnp.mean(centred * centred, axis=-1, keepdims=True)
    return (centred * lax.rsqrt(spread + NORM_EPS)).astype(BF16)


def matmul(a, b):
    return jnp.dot(a, b, preferred_element_type=F32)


def matmul_nt(a, b):
    return lax.dot_general(a, b, (((1,), (1,)), ((), ())), preferred_element_type=F32)


def matmul_tn(a, b):
    return lax.dot_general(a, b, (((0,), (0,)), ((), ())), preferred_element_type=F32)


def attend(stacked, keys, values, scale, bias, heads):
    scores = matmul_nt(stacked, keys) * scale + bias
    exp_scores = jnp.exp(scores - jnp.max(scores, axis=-1, keepdims=True))
    total = jnp.sum(exp_scores, axis=-1, keepdims=True)
    weighted = matmul(exp_scores.astype(BF16), values)
    return head_merge(weighted, heads) / head_merge(jnp.broadcast_to(total, weighted.shape), heads)


def head_stack(values, heads):
    rows, width = values.shape
    lane = lax.broadcasted_iota(jnp.int32, (rows, width), 1) // SUBSPACE_DEPTH
    return jnp.concatenate(
        [jnp.where(lane == h, values, 0.0) for h in range(heads)], axis=0
    ).astype(BF16)


def head_merge(stacked, heads):
    rows, width = stacked.shape[0] // heads, stacked.shape[1]
    lane = lax.broadcasted_iota(jnp.int32, (rows, width), 1) // SUBSPACE_DEPTH
    total = jnp.zeros((rows, width), F32)
    for h in range(heads):
        total = jnp.where(lane == h, stacked[h * rows : (h + 1) * rows], total)
    return total


def kernel(sizes, shape, *refs):
    n_pb, n_a, n_b, n_c = sizes
    count = len(INPUTS)
    hbm = dict(zip(INPUTS, refs[:count]))
    out_msa, out_pair = refs[count : 2 + count]
    w = dict(zip(INPUTS, refs[2 + count : 2 + 2 * count]))
    (xg, pg, k_s, v_s, left_s, msg_s, gather, bias_s, pairin_s, tkv_s, wf_s, wp_s, opm_s,
     flat_s, q_s, tq_s, wsem, sx, rx, sp, rp, s1, r1, s2, r2) = refs[2 + 2 * count :]
    x_ref, pair_ref = w["x"], w["pair"]
    rows_i, seqs, width = shape
    tiles = width // LANES
    cells, pwidth = pair_ref.shape
    cols = cells // rows_i
    residues = w["resolved"].shape[1]
    n_as = n_a // n_pb
    n_src = n_as * n_b * n_c
    factor = w["duo"].shape[0] // 2
    eparts = factor // SUBLANES
    seq_blocks = eparts * seqs // LANES
    factor_rows = rows_i * SUBLANES
    base = seq_blocks * factor_rows

    grp = lax.axis_index("grp")
    row = lax.axis_index("row")
    c_me = lax.axis_index("br")
    p_me = lax.axis_index("pb")
    a_me, b_me = row // n_b, row % n_b
    scale = SUBSPACE_DEPTH ** (-0.5)

    def device(a, b, c, p):
        return (grp, a * n_b + b, c, p)

    loads = {}
    for n, name in enumerate(INPUTS):
        loads[name] = pltpu.make_async_copy(hbm[name], w[name], wsem.at[n])
    for name in INPUTS:
        loads[name].start()

    barrier = pltpu.get_barrier_semaphore()
    line = [(da, dp) for da in range(n_a) for dp in range(n_pb) if (da, dp) != (0, 0)]
    mates = [(db, dc) for db in range(n_b) for dc in range(n_c) if (db, dc) != (0, 0)]
    for da, dp in line:
        pl.semaphore_signal(
            barrier, inc=1, device_id=device((a_me + da) % n_a, b_me, c_me, (p_me + dp) % n_pb), device_id_type=MESH
        )
    for db, dc in mates:
        pl.semaphore_signal(
            barrier, inc=1, device_id=device(a_me, (b_me + db) % n_b, (c_me + dc) % n_c, p_me), device_id_type=MESH
        )

    def by_residue(block):
        flat_s[...] = block.astype(F32)
        return jnp.concatenate(
            [
                jnp.concatenate(
                    [flat_s[pl.ds(t * rows_i + r, seqs, stride=tiles * rows_i), :] for t in range(tiles)], axis=1
                )
                for r in range(rows_i)
            ],
            axis=0,
        )

    loads["x"].wait()
    x_own = by_residue(x_ref[...])
    xn_own = normalize(x_own)
    loads["chain"].wait()
    loads["duo"].wait()
    chain = w["chain"][...].astype(F32)
    own_chain = jnp.zeros((1, seqs), F32)
    for p in range(n_pb):
        own_chain = jnp.where(p_me == p, chain[:, p * seqs : (p + 1) * seqs], own_chain)
    rt = matmul_nt(w["duo"][factor:, :], xn_own) * jnp.concatenate([own_chain] * rows_i, axis=1)
    for j in range(rows_i):
        parts = jnp.concatenate(
            [rt[q * SUBLANES : (q + 1) * SUBLANES, j * seqs : (j + 1) * seqs] for q in range(eparts)], axis=1
        )
        for b in range(seq_blocks):
            at = b * factor_rows + j * SUBLANES
            opm_s[at : at + SUBLANES, :] = parts[:, b * LANES : (b + 1) * LANES]

    row_first = (row * n_c + c_me) * rows_i
    bins = 2 * RELPOS_MAX + 1
    loads["positions"].wait()
    loads["scalars"].wait()
    loads["rel"].wait()
    for i in range(rows_i):
        offset = jnp.clip(w["scalars"][row_first + i] - w["positions"][...], -RELPOS_MAX, RELPOS_MAX) + RELPOS_MAX
        hot = lax.broadcasted_iota(jnp.int32, (bins, residues), 0) == offset
        added = matmul_tn(jnp.where(hot, 1.0, 0.0).astype(BF16), w["rel"][...])
        for p in range(n_pb):
            pairin_s[p, i * cols : (i + 1) * cols] = added[p * cols : (p + 1) * cols]
    loads["pair"].wait()
    pair_in = pairin_s[p_me] + pair_ref[...].astype(F32)
    pn_own = normalize(pair_in)
    loads["tbias"].wait()
    bt = matmul_nt(w["tbias"][...], pn_own)
    for i in range(rows_i):
        for h in range(TRI_HEADS):
            at = base + h * rows_i + i
            opm_s[at : at + 1, :cols] = bt[h : h + 1, i * cols : (i + 1) * cols]
    msg_s[...] = opm_s[: msg_s.shape[0], :].astype(BF16)

    loads["qkvg"].wait()
    proj = matmul(xn_own, w["qkvg"][...])
    query = proj[:, :width].astype(BF16).astype(F32)
    for r in range(rows_i):
        q_s[r] = head_stack(query[r * seqs : (r + 1) * seqs], VERTICAL_ATTENDS)
    gate = jax.nn.sigmoid(proj[:, 3 * width :].astype(BF16).astype(F32))
    k_s[p_me] = proj[:, width : 2 * width].astype(BF16)
    v_s[p_me] = proj[:, 2 * width : 3 * width].astype(BF16)

    loads["tri"].wait()
    tri_w = w["tri"][...].astype(F32)
    tri_w = jnp.concatenate(
        [
            tri_w[:, (h * 4 + kind) * SUBSPACE_DEPTH : (h * 4 + kind + 1) * SUBSPACE_DEPTH]
            for kind in range(4)
            for h in range(TRI_HEADS)
        ],
        axis=1,
    ).astype(BF16)
    tproj = matmul(pn_own, tri_w)
    tkv_s[p_me] = tproj[:, pwidth : 3 * pwidth].astype(BF16)
    tri_q = tproj[:, :pwidth].astype(BF16).astype(F32)
    for i in range(rows_i):
        tq_s[i] = head_stack(tri_q[i * cols : (i + 1) * cols], TRI_HEADS)
    tri_gate = jax.nn.sigmoid(tproj[:, 3 * pwidth :].astype(BF16).astype(F32))
    loads["tensor"].wait()
    wf_s[...] = w["tensor"][...].astype(F32)
    for e in range(SUBLANES):
        for q in range(eparts):
            at = (e * eparts + q) * factor
            wp_s[at : at + factor, :] = wf_s[pl.ds(q * SUBLANES + e, factor, stride=factor), :].astype(BF16)

    left_w = jnp.concatenate([w["duo"][:factor, :]] * eparts, axis=0)
    lane_part = lax.broadcasted_iota(jnp.int32, (seqs, LANES), 1) // factor

    def put_left(p, xn):
        left4 = matmul_nt(xn, left_w)
        for i in range(rows_i):
            block = left4[i * seqs : (i + 1) * seqs]
            for q in range(eparts):
                left_s[p, q * seqs : (q + 1) * seqs, i * LANES : (i + 1) * LANES] = (
                    jnp.where(lane_part == q, block, 0.0).astype(BF16)
                )

    put_left(p_me, xn_own)

    pl.semaphore_wait(barrier, len(line) + len(mates))

    p_to, a_slot = a_me // n_as, a_me % n_as
    stays = p_to == p_me

    def slot_of(a, b, c):
        return (a * n_b + b) * n_c + c

    def first(d):
        return pltpu.make_async_remote_copy(
            src_ref=msg_s, dst_ref=gather.at[slot_of(a_slot, b_me, c_me), p_me], send_sem=s1.at[d],
            recv_sem=r1.at[a_slot * n_pb + p_me], device_id=device((a_me + d) % n_a, b_me, c_me, p_to),
            device_id_type=MESH)

    for d in range(1, n_a):
        first(d).start()

    @pl.when(jnp.logical_not(stays))
    def _():
        first(0).start()

    @pl.when(stays)
    def _():
        gather[slot_of(a_slot, b_me, c_me), p_me] = msg_s[...]

    exchange = []
    for d in range(1, n_pb):
        peer = device(a_me, b_me, c_me, (p_me + d) % n_pb)
        exchange.append((
            pltpu.make_async_remote_copy(
                src_ref=pair_ref, dst_ref=pg.at[n_pb - d], send_sem=sp.at[d], recv_sem=rp.at[n_pb - d],
                device_id=peer, device_id_type=MESH),
            pltpu.make_async_remote_copy(
                src_ref=x_ref, dst_ref=xg.at[n_pb - d], send_sem=sx.at[d], recv_sem=rx.at[n_pb - d],
                device_id=peer, device_id_type=MESH),
        ))
    for copy, _ in exchange:
        copy.start()
    for _, copy in exchange:
        copy.start()

    second = []
    for a in range(n_as):
        slot = slot_of(a, b_me, c_me)
        for p in range(n_pb):
            here = jnp.logical_and(stays, jnp.logical_and(a_slot == a, p_me == p))

            @pl.when(jnp.logical_not(here))
            def _():
                pltpu.make_async_remote_copy(
                    src_ref=msg_s, dst_ref=gather.at[slot, p], send_sem=s1.at[0], recv_sem=r1.at[a * n_pb + p],
                    device_id=device((a_me + 1) % n_a, b_me, c_me, p_me), device_id_type=MESH).wait_recv()

        for m, (db, dc) in enumerate(mates):
            copy = pltpu.make_async_remote_copy(
                src_ref=gather.at[slot], dst_ref=gather.at[slot], send_sem=s2.at[a * len(mates) + m],
                recv_sem=r2.at[slot],
                device_id=device(a_me, (b_me + db) % n_b, (c_me + dc) % n_c, p_me), device_id_type=MESH)
            copy.start()
            second.append(copy)

    for slot in range(1, n_pb):
        exchange[n_pb - slot - 1][0].wait_recv()
    for d in range(1, n_pb):
        p = (p_me + d) % n_pb
        pn = normalize(pairin_s[p] + pg[d].astype(F32))
        tkv_s[p] = matmul(pn, tri_w[:, pwidth : 3 * pwidth]).astype(BF16)

    for slot in range(1, n_pb):
        exchange[n_pb - slot - 1][1].wait_recv()
    for d in range(1, n_pb):
        p = (p_me + d) % n_pb
        xn = normalize(by_residue(xg[d]))
        put_left(p, xn)
        kv = matmul(xn, w["qkvg"][:, width : 3 * width])
        k_s[p] = kv[:, :width].astype(BF16)
        v_s[p] = kv[:, width:].astype(BF16)

    seq_bias = (chain - 1.0) * MASK_NEGATIVE
    mixed = []
    for r in range(rows_i):
        span = slice(r * seqs, (r + 1) * seqs)
        keys = jnp.concatenate([k_s[p, span, :] for p in range(n_pb)], axis=0)
        values = jnp.concatenate([v_s[p, span, :] for p in range(n_pb)], axis=0)
        attended = attend(q_s[r], keys, values, scale, seq_bias, VERTICAL_ATTENDS)
        mixed.append((gate[span] * attended).astype(BF16))

    loads["vproj"].wait()
    mid = x_own + matmul(jnp.concatenate(mixed, axis=0), w["vproj"][...])
    loads["expand"].wait()
    hidden = jnp.maximum(matmul(normalize(mid), w["expand"][...]), 0.0).astype(BF16)
    loads["contract"].wait()
    fresh = mid + matmul(hidden, w["contract"][...])
    for r in range(rows_i):
        for t in range(tiles):
            flat_s[pl.ds(t * rows_i + r, seqs, stride=tiles * rows_i), :] = fresh[
                r * seqs : (r + 1) * seqs, t * LANES : (t + 1) * LANES
            ]
    out_msa[...] = flat_s[...].astype(BF16)

    for a in range(n_as):
        for db, dc in mates:
            slot = slot_of(a, (b_me + db) % n_b, (c_me + dc) % n_c)
            pltpu.make_async_remote_copy(
                src_ref=gather.at[slot], dst_ref=gather.at[slot], send_sem=s2.at[0], recv_sem=r2.at[slot],
                device_id=device(a_me, (b_me + db) % n_b, (c_me + dc) % n_c, p_me), device_id_type=MESH).wait_recv()

    right_all = jnp.concatenate(
        [
            jnp.concatenate(
                [
                    gather[s, p, b * factor_rows : (b + 1) * factor_rows, :]
                    for p in range(n_pb)
                    for b in range(seq_blocks)
                ],
                axis=1,
            )
            for s in range(n_src)
        ],
        axis=0,
    )
    outer = matmul(right_all, left_s[...].reshape(n_pb * eparts * seqs, rows_i * LANES))
    opm_s[: cells * SUBLANES, :] = jnp.concatenate(
        [outer[:, i * LANES : (i + 1) * LANES] for i in range(rows_i)], axis=0
    )
    lhs = jnp.concatenate(
        [opm_s[pl.ds(e, cells, stride=SUBLANES), :].astype(BF16) for e in range(SUBLANES)], axis=1
    )
    opm = matmul(lhs, wp_s[...]) / jnp.sum(chain)

    for s in range(n_src):
        part = jnp.concatenate(
            [gather[s, p, base : base + rows_i * TRI_HEADS, :].astype(F32)[:, :cols] for p in range(n_pb)], axis=1
        )
        for h in range(TRI_HEADS):
            bias_s[h * cols + s * rows_i : h * cols + (s + 1) * rows_i, :] = part[h * rows_i : (h + 1) * rows_i, :]
    loads["resolved"].wait()
    bias = bias_s[...] + (w["resolved"][...].astype(F32) - 1.0) * MASK_NEGATIVE
    tri_mixed = []
    for i in range(rows_i):
        span = slice(i * cols, (i + 1) * cols)
        keys = jnp.concatenate([tkv_s[p, span, :pwidth] for p in range(n_pb)], axis=0)
        values = jnp.concatenate([tkv_s[p, span, pwidth:] for p in range(n_pb)], axis=0)
        attended = attend(tq_s[i], keys, values, scale, bias, TRI_HEADS)
        tri_mixed.append((tri_gate[span] * attended).astype(BF16))
    loads["tout"].wait()
    pair_mid = pair_in + matmul(jnp.concatenate(tri_mixed, axis=0), w["tout"][...]) + opm
    loads["up"].wait()
    pair_hidden = jnp.maximum(matmul(normalize(pair_mid), w["up"][...]), 0.0).astype(BF16)
    loads["down"].wait()
    out_pair[...] = (pair_mid + matmul(pair_hidden, w["down"][...])).astype(BF16)

    for copies in exchange:
        for copy in copies:
            copy.wait_send()
    for copy in second:
        copy.wait_send()
    for d in range(1, n_a):
        first(d).wait_send()

    @pl.when(jnp.logical_not(stays))
    def _():
        first(0).wait_send()


def finish(msa_ref, pair_ref, out_msa, out_pair, sem):
    copies = [
        pltpu.make_async_copy(msa_ref, out_msa, sem.at[0]),
        pltpu.make_async_copy(pair_ref, out_pair, sem.at[1]),
    ]
    for copy in copies:
        copy.start()
    for copy in copies:
        copy.wait()


def on_device(sizes, x, pair, chain, resolved, positions, *weights):
    seqs, rows_i, width = x.shape
    cols, pwidth = pair.shape[1:]
    n_pb, n_a, n_b, n_c = sizes
    cells = rows_i * cols
    chains, residues = chain.shape[0], resolved.shape[0]
    n_as = n_a // n_pb
    n_src = n_as * n_b * n_c
    arrays = dict(zip(WEIGHTS, weights))
    arrays["duo"] = arrays["duo"].T
    arrays["tbias"] = arrays["tbias"].T
    tiles = width // LANES
    arrays["x"] = x.reshape(seqs, rows_i, tiles, LANES).transpose(0, 2, 1, 3).reshape(-1, LANES)
    arrays["pair"] = pair.reshape(cells, pwidth)
    arrays["chain"] = chain.reshape(1, chains)
    arrays["resolved"] = resolved.reshape(1, residues)
    arrays["positions"] = positions.reshape(1, residues)
    arrays["scalars"] = positions
    inputs = [arrays[name] for name in INPUTS]
    factor = arrays["duo"].shape[0] // 2
    eparts = factor // SUBLANES
    msg_rows = eparts * seqs // LANES * rows_i * SUBLANES + rows_i * TRI_HEADS
    mates = n_b * n_c - 1
    dma = pltpu.SemaphoreType.DMA
    msa, pair_out = pl.pallas_call(
        functools.partial(kernel, sizes, (rows_i, seqs, width)),
        out_shape=(
            pltpu.VMEM(arrays["x"].shape, BF16),
            pltpu.VMEM((cells, pwidth), BF16),
        ),
        in_specs=[pl.BlockSpec(memory_space=pltpu.HBM)] * len(inputs),
        out_specs=(pl.BlockSpec(memory_space=pltpu.VMEM),) * 2,
        scratch_shapes=[
            (pltpu.SMEM if name == "scalars" else pltpu.VMEM)(v.shape, v.dtype) for name, v in zip(INPUTS, inputs)
        ]
        + [
            pltpu.VMEM((n_pb,) + arrays["x"].shape, BF16),
            pltpu.VMEM((n_pb, cells, pwidth), BF16),
            pltpu.VMEM((n_pb, rows_i * seqs, width), BF16),
            pltpu.VMEM((n_pb, rows_i * seqs, width), BF16),
            pltpu.VMEM((n_pb, eparts * seqs, rows_i * LANES), BF16),
            pltpu.VMEM((msg_rows, LANES), BF16),
            pltpu.VMEM((n_src, n_pb, msg_rows, LANES), BF16),
            pltpu.VMEM((TRI_HEADS * cols, residues), F32),
            pltpu.VMEM((n_pb, cells, pwidth), F32),
            pltpu.VMEM((n_pb, cells, 2 * pwidth), BF16),
            pltpu.VMEM(arrays["tensor"].shape, F32),
            pltpu.VMEM(arrays["tensor"].shape, BF16),
            pltpu.VMEM((max(cells * SUBLANES, msg_rows), LANES), F32),
            pltpu.VMEM(arrays["x"].shape, F32),
            pltpu.VMEM((rows_i, VERTICAL_ATTENDS * seqs, width), BF16),
            pltpu.VMEM((rows_i, TRI_HEADS * cols, pwidth), BF16),
            dma((len(inputs),)),
            dma((n_pb,)),
            dma((n_pb,)),
            dma((n_pb,)),
            dma((n_pb,)),
            dma((n_a,)),
            dma((n_as * n_pb,)),
            dma((n_as * mates,)),
            dma((n_src,)),
        ],
        compiler_params=pltpu.CompilerParams(
            collective_id=0, has_side_effects=True, vmem_limit_bytes=56 * 1024 * 1024
        ),
    )(*inputs)
    hbm = pl.BlockSpec(memory_space=pltpu.HBM)
    vmem = pl.BlockSpec(memory_space=pltpu.VMEM)
    msa, pair_out = pl.pallas_call(
        finish,
        out_shape=(
            jax.ShapeDtypeStruct(msa.shape, BF16),
            jax.ShapeDtypeStruct(pair_out.shape, BF16),
        ),
        in_specs=[vmem] * 2,
        out_specs=(hbm, hbm),
        scratch_shapes=[dma((2,))],
        compiler_params=pltpu.CompilerParams(vmem_limit_bytes=8 * 1024 * 1024),
    )(msa, pair_out)
    msa = msa.reshape(seqs, tiles, rows_i, LANES).transpose(0, 2, 1, 3).reshape(x.shape)
    return msa, pair_out.reshape(rows_i, cols, pwidth)


def solution(mesh):
    n_row, n_br, n_pb = mesh.shape["row"], mesh.shape["br"], mesh.shape["pb"]
    n_b = 2 if n_row % (2 * n_pb) == 0 else 1
    sizes = (n_pb, n_row // n_b, n_b, n_br)
    return jax.shard_map(
        functools.partial(on_device, sizes),
        mesh=mesh,
        in_specs=(
            P(("grp", "pb"), ("row", "br"), None),
            P(("grp", "row", "br"), "pb", None),
            P("grp"),
            P("grp"),
            P("grp"),
        )
        + (P(),) * 12,
        out_specs=(P(("grp", "pb"), ("row", "br"), None), P(("grp", "row", "br"), "pb", None)),
        check_vma=False,
    )
```

```python
import functools

import jax
import jax.numpy as jnp
from jax import lax
from jax.experimental import pallas as pl
from jax.experimental.pallas import tpu as pltpu
from jax.sharding import PartitionSpec as P

VERTICAL_ATTENDS = 8
TRI_HEADS = 4
SUBSPACE_DEPTH = 32
RELPOS_MAX = 32

NORM_EPS = 1e-05
MASK_NEGATIVE = 1000000000.0
LANES = 128
SUBLANES = 8
MESH = pl.DeviceIdType.MESH
F32 = jnp.float32
BF16 = jnp.bfloat16

WEIGHTS = (
    "rel", "qkvg", "vproj", "expand", "contract", "duo", "tensor", "tri", "tbias", "tout", "up", "down",
)


INPUTS = (
    "x", "chain", "duo", "positions", "scalars", "rel", "pair", "tbias", "qkvg", "tri", "tensor",
    "vproj", "expand", "contract", "resolved", "tout", "up", "down",
)


def normalize(values):
    centre = jnp.mean(values, axis=-1, keepdims=True)
    centred = values - centre
    spread = jnp.mean(centred * centred, axis=-1, keepdims=True)
    return (centred * lax.rsqrt(spread + NORM_EPS)).astype(BF16)


def matmul(a, b):
    return jnp.dot(a, b, preferred_element_type=F32)


def matmul_nt(a, b):
    return lax.dot_general(a, b, (((1,), (1,)), ((), ())), preferred_element_type=F32)


def matmul_tn(a, b):
    return lax.dot_general(a, b, (((0,), (0,)), ((), ())), preferred_element_type=F32)


def attend(stacked, keys, values, scale, bias, heads):
    scores = matmul_nt(stacked, keys) * scale + bias
    exp_scores = jnp.exp(scores - jnp.max(scores, axis=-1, keepdims=True))
    total = jnp.sum(exp_scores, axis=-1, keepdims=True)
    weighted = matmul(exp_scores.astype(BF16), values)
    return head_merge(weighted, heads) / head_merge(jnp.broadcast_to(total, weighted.shape), heads)


def head_stack(values, heads):
    rows, width = values.shape
    lane = lax.broadcasted_iota(jnp.int32, (rows, width), 1) // SUBSPACE_DEPTH
    return jnp.concatenate(
        [jnp.where(lane == h, values, 0.0) for h in range(heads)], axis=0
    ).astype(BF16)


def head_merge(stacked, heads):
    rows, width = stacked.shape[0] // heads, stacked.shape[1]
    lane = lax.broadcasted_iota(jnp.int32, (rows, width), 1) // SUBSPACE_DEPTH
    total = jnp.zeros((rows, width), F32)
    for h in range(heads):
        total = jnp.where(lane == h, stacked[h * rows : (h + 1) * rows], total)
    return total


def kernel(sizes, shape, *refs):
    n_pb, n_a, n_b, n_c = sizes
    count = len(INPUTS)
    hbm = dict(zip(INPUTS, refs[:count]))
    out_msa, out_pair = refs[count : 2 + count]
    w = dict(zip(INPUTS, refs[2 + count : 2 + 2 * count]))
    (xg, pg, k_s, v_s, left_s, msg_s, gather, bias_s, pairin_s, tkv_s, wf_s, wp_s, opm_s,
     flat_s, q_s, tq_s, wsem, sx, rx, sp, rp, s1, r1, s2, r2) = refs[2 + 2 * count :]
    x_ref, pair_ref = w["x"], w["pair"]
    rows_i, seqs, width = shape
    tiles = width // LANES
    cells, pwidth = pair_ref.shape
    cols = cells // rows_i
    residues = w["resolved"].shape[1]
    n_as = n_a // n_pb
    n_src = n_as * n_b * n_c
    factor = w["duo"].shape[0] // 2
    eparts = factor // SUBLANES
    seq_blocks = eparts * seqs // LANES
    factor_rows = rows_i * SUBLANES
    base = seq_blocks * factor_rows

    grp = lax.axis_index("grp")
    row = lax.axis_index("row")
    c_me = lax.axis_index("br")
    p_me = lax.axis_index("pb")
    a_me, b_me = row // n_b, row % n_b
    scale = SUBSPACE_DEPTH ** (-0.5)

    def device(a, b, c, p):
        return (grp, a * n_b + b, c, p)

    loads = {}
    for n, name in enumerate(INPUTS):
        loads[name] = pltpu.make_async_copy(hbm[name], w[name], wsem.at[n])
    for name in INPUTS:
        loads[name].start()

    barrier = pltpu.get_barrier_semaphore()
    line = [(da, dp) for da in range(n_a) for dp in range(n_pb) if (da, dp) != (0, 0)]
    mates = [(db, dc) for db in range(n_b) for dc in range(n_c) if (db, dc) != (0, 0)]
    for da, dp in line:
        pl.semaphore_signal(
            barrier, inc=1, device_id=device((a_me + da) % n_a, b_me, c_me, (p_me + dp) % n_pb), device_id_type=MESH
        )
    for db, dc in mates:
        pl.semaphore_signal(
            barrier, inc=1, device_id=device(a_me, (b_me + db) % n_b, (c_me + dc) % n_c, p_me), device_id_type=MESH
        )

    def by_residue(block):
        flat_s[...] = block.astype(F32)
        return jnp.concatenate(
            [
                jnp.concatenate(
                    [flat_s[pl.ds(t * rows_i + r, seqs, stride=tiles * rows_i), :] for t in range(tiles)], axis=1
                )
                for r in range(rows_i)
            ],
            axis=0,
        )

    loads["x"].wait()
    x_own = by_residue(x_ref[...])
    xn_own = normalize(x_own)
    loads["chain"].wait()
    loads["duo"].wait()
    chain = w["chain"][...].astype(F32)
    own_chain = jnp.zeros((1, seqs), F32)
    for p in range(n_pb):
        own_chain = jnp.where(p_me == p, chain[:, p * seqs : (p + 1) * seqs], own_chain)
    rt = matmul_nt(w["duo"][factor:, :], xn_own) * jnp.concatenate([own_chain] * rows_i, axis=1)
    for j in range(rows_i):
        parts = jnp.concatenate(
            [rt[q * SUBLANES : (q + 1) * SUBLANES, j * seqs : (j + 1) * seqs] for q in range(eparts)], axis=1
        )
        for b in range(seq_blocks):
            at = b * factor_rows + j * SUBLANES
            opm_s[at : at + SUBLANES, :] = parts[:, b * LANES : (b + 1) * LANES]

    row_first = (row * n_c + c_me) * rows_i
    bins = 2 * RELPOS_MAX + 1
    loads["positions"].wait()
    loads["scalars"].wait()
    loads["rel"].wait()
    for i in range(rows_i):
        offset = jnp.clip(w["scalars"][row_first + i] - w["positions"][...], -RELPOS_MAX, RELPOS_MAX) + RELPOS_MAX
        hot = lax.broadcasted_iota(jnp.int32, (bins, residues), 0) == offset
        added = matmul_tn(jnp.where(hot, 1.0, 0.0).astype(BF16), w["rel"][...])
        for p in range(n_pb):
            pairin_s[p, i * cols : (i + 1) * cols] = added[p * cols : (p + 1) * cols]
    loads["pair"].wait()
    pair_in = pairin_s[p_me] + pair_ref[...].astype(F32)
    pn_own = normalize(pair_in)
    loads["tbias"].wait()
    bt = matmul_nt(w["tbias"][...], pn_own)
    for i in range(rows_i):
        for h in range(TRI_HEADS):
            at = base + h * rows_i + i
            opm_s[at : at + 1, :cols] = bt[h : h + 1, i * cols : (i + 1) * cols]
    msg_s[...] = opm_s[: msg_s.shape[0], :].astype(BF16)

    loads["qkvg"].wait()
    proj = matmul(xn_own, w["qkvg"][...])
    query = proj[:, :width].astype(BF16).astype(F32)
    for r in range(rows_i):
        q_s[r] = head_stack(query[r * seqs : (r + 1) * seqs], VERTICAL_ATTENDS)
    gate = jax.nn.sigmoid(proj[:, 3 * width :].astype(BF16).astype(F32))
    k_s[p_me] = proj[:, width : 2 * width].astype(BF16)
    v_s[p_me] = proj[:, 2 * width : 3 * width].astype(BF16)

    loads["tri"].wait()
    tri_w = w["tri"][...].astype(F32)
    tri_w = jnp.concatenate(
        [
            tri_w[:, (h * 4 + kind) * SUBSPACE_DEPTH : (h * 4 + kind + 1) * SUBSPACE_DEPTH]
            for kind in range(4)
            for h in range(TRI_HEADS)
        ],
        axis=1,
    ).astype(BF16)
    tproj = matmul(pn_own, tri_w)
    tkv_s[p_me] = tproj[:, pwidth : 3 * pwidth].astype(BF16)
    tri_q = tproj[:, :pwidth].astype(BF16).astype(F32)
    for i in range(rows_i):
        tq_s[i] = head_stack(tri_q[i * cols : (i + 1) * cols], TRI_HEADS)
    tri_gate = jax.nn.sigmoid(tproj[:, 3 * pwidth :].astype(BF16).astype(F32))
    loads["tensor"].wait()
    wf_s[...] = w["tensor"][...].astype(F32)
    for e in range(SUBLANES):
        for q in range(eparts):
            at = (e * eparts + q) * factor
            wp_s[at : at + factor, :] = wf_s[pl.ds(q * SUBLANES + e, factor, stride=factor), :].astype(BF16)

    left_w = jnp.concatenate([w["duo"][:factor, :]] * eparts, axis=0)
    lane_part = lax.broadcasted_iota(jnp.int32, (seqs, LANES), 1) // factor

    def put_left(p, xn):
        left4 = matmul_nt(xn, left_w)
        for i in range(rows_i):
            block = left4[i * seqs : (i + 1) * seqs]
            for q in range(eparts):
                left_s[p, q * seqs : (q + 1) * seqs, i * LANES : (i + 1) * LANES] = (
                    jnp.where(lane_part == q, block, 0.0).astype(BF16)
                )

    put_left(p_me, xn_own)

    pl.semaphore_wait(barrier, len(line) + len(mates))

    exchange = []
    for d in range(1, n_pb):
        peer = device(a_me, b_me, c_me, (p_me + d) % n_pb)
        exchange.append((
            pltpu.make_async_remote_copy(
                src_ref=pair_ref, dst_ref=pg.at[n_pb - d], send_sem=sp.at[d], recv_sem=rp.at[n_pb - d],
                device_id=peer, device_id_type=MESH),
            pltpu.make_async_remote_copy(
                src_ref=x_ref, dst_ref=xg.at[n_pb - d], send_sem=sx.at[d], recv_sem=rx.at[n_pb - d],
                device_id=peer, device_id_type=MESH),
        ))
    for copy, _ in exchange:
        copy.start()
    for _, copy in exchange:
        copy.start()

    p_to, a_slot = a_me // n_as, a_me % n_as
    stays = p_to == p_me

    def slot_of(a, b, c):
        return (a * n_b + b) * n_c + c

    def first(d):
        return pltpu.make_async_remote_copy(
            src_ref=msg_s, dst_ref=gather.at[slot_of(a_slot, b_me, c_me), p_me], send_sem=s1.at[d],
            recv_sem=r1.at[a_slot * n_pb + p_me], device_id=device((a_me + d) % n_a, b_me, c_me, p_to),
            device_id_type=MESH)

    for d in range(1, n_a):
        first(d).start()

    @pl.when(jnp.logical_not(stays))
    def _():
        first(0).start()

    @pl.when(stays)
    def _():
        gather[slot_of(a_slot, b_me, c_me), p_me] = msg_s[...]

    second = []
    for a in range(n_as):
        slot = slot_of(a, b_me, c_me)
        for p in range(n_pb):
            here = jnp.logical_and(stays, jnp.logical_and(a_slot == a, p_me == p))

            @pl.when(jnp.logical_not(here))
            def _():
                pltpu.make_async_remote_copy(
                    src_ref=msg_s, dst_ref=gather.at[slot, p], send_sem=s1.at[0], recv_sem=r1.at[a * n_pb + p],
                    device_id=device((a_me + 1) % n_a, b_me, c_me, p_me), device_id_type=MESH).wait_recv()

        for m, (db, dc) in enumerate(mates):
            copy = pltpu.make_async_remote_copy(
                src_ref=gather.at[slot], dst_ref=gather.at[slot], send_sem=s2.at[a * len(mates) + m],
                recv_sem=r2.at[slot],
                device_id=device(a_me, (b_me + db) % n_b, (c_me + dc) % n_c, p_me), device_id_type=MESH)
            copy.start()
            second.append(copy)

    for slot in range(1, n_pb):
        exchange[n_pb - slot - 1][0].wait_recv()
    for d in range(1, n_pb):
        p = (p_me + d) % n_pb
        pn = normalize(pairin_s[p] + pg[d].astype(F32))
        tkv_s[p] = matmul(pn, tri_w[:, pwidth : 3 * pwidth]).astype(BF16)

    for slot in range(1, n_pb):
        exchange[n_pb - slot - 1][1].wait_recv()
    for d in range(1, n_pb):
        p = (p_me + d) % n_pb
        xn = normalize(by_residue(xg[d]))
        put_left(p, xn)
        kv = matmul(xn, w["qkvg"][:, width : 3 * width])
        k_s[p] = kv[:, :width].astype(BF16)
        v_s[p] = kv[:, width:].astype(BF16)

    seq_bias = (chain - 1.0) * MASK_NEGATIVE
    mixed = []
    for r in range(rows_i):
        span = slice(r * seqs, (r + 1) * seqs)
        keys = jnp.concatenate([k_s[p, span, :] for p in range(n_pb)], axis=0)
        values = jnp.concatenate([v_s[p, span, :] for p in range(n_pb)], axis=0)
        attended = attend(q_s[r], keys, values, scale, seq_bias, VERTICAL_ATTENDS)
        mixed.append((gate[span] * attended).astype(BF16))

    loads["vproj"].wait()
    mid = x_own + matmul(jnp.concatenate(mixed, axis=0), w["vproj"][...])
    loads["expand"].wait()
    hidden = jnp.maximum(matmul(normalize(mid), w["expand"][...]), 0.0).astype(BF16)
    loads["contract"].wait()
    fresh = mid + matmul(hidden, w["contract"][...])
    for r in range(rows_i):
        for t in range(tiles):
            flat_s[pl.ds(t * rows_i + r, seqs, stride=tiles * rows_i), :] = fresh[
                r * seqs : (r + 1) * seqs, t * LANES : (t + 1) * LANES
            ]
    out_msa[...] = flat_s[...].astype(BF16)

    for a in range(n_as):
        for db, dc in mates:
            slot = slot_of(a, (b_me + db) % n_b, (c_me + dc) % n_c)
            pltpu.make_async_remote_copy(
                src_ref=gather.at[slot], dst_ref=gather.at[slot], send_sem=s2.at[0], recv_sem=r2.at[slot],
                device_id=device(a_me, (b_me + db) % n_b, (c_me + dc) % n_c, p_me), device_id_type=MESH).wait_recv()

    right_all = jnp.concatenate(
        [
            jnp.concatenate(
                [
                    gather[s, p, b * factor_rows : (b + 1) * factor_rows, :]
                    for p in range(n_pb)
                    for b in range(seq_blocks)
                ],
                axis=1,
            )
            for s in range(n_src)
        ],
        axis=0,
    )
    outer = matmul(right_all, left_s[...].reshape(n_pb * eparts * seqs, rows_i * LANES))
    opm_s[: cells * SUBLANES, :] = jnp.concatenate(
        [outer[:, i * LANES : (i + 1) * LANES] for i in range(rows_i)], axis=0
    )
    lhs = jnp.concatenate(
        [opm_s[pl.ds(e, cells, stride=SUBLANES), :].astype(BF16) for e in range(SUBLANES)], axis=1
    )
    opm = matmul(lhs, wp_s[...]) / jnp.sum(chain)

    for s in range(n_src):
        part = jnp.concatenate(
            [gather[s, p, base : base + rows_i * TRI_HEADS, :].astype(F32)[:, :cols] for p in range(n_pb)], axis=1
        )
        for h in range(TRI_HEADS):
            bias_s[h * cols + s * rows_i : h * cols + (s + 1) * rows_i, :] = part[h * rows_i : (h + 1) * rows_i, :]
    loads["resolved"].wait()
    bias = bias_s[...] + (w["resolved"][...].astype(F32) - 1.0) * MASK_NEGATIVE
    tri_mixed = []
    for i in range(rows_i):
        span = slice(i * cols, (i + 1) * cols)
        keys = jnp.concatenate([tkv_s[p, span, :pwidth] for p in range(n_pb)], axis=0)
        values = jnp.concatenate([tkv_s[p, span, pwidth:] for p in range(n_pb)], axis=0)
        attended = attend(tq_s[i], keys, values, scale, bias, TRI_HEADS)
        tri_mixed.append((tri_gate[span] * attended).astype(BF16))
    loads["tout"].wait()
    pair_mid = pair_in + matmul(jnp.concatenate(tri_mixed, axis=0), w["tout"][...]) + opm
    loads["up"].wait()
    pair_hidden = jnp.maximum(matmul(normalize(pair_mid), w["up"][...]), 0.0).astype(BF16)
    loads["down"].wait()
    out_pair[...] = (pair_mid + matmul(pair_hidden, w["down"][...])).astype(BF16)

    for copies in exchange:
        for copy in copies:
            copy.wait_send()
    for copy in second:
        copy.wait_send()
    for d in range(1, n_a):
        first(d).wait_send()

    @pl.when(jnp.logical_not(stays))
    def _():
        first(0).wait_send()


def finish(msa_ref, pair_ref, out_msa, out_pair, sem):
    copies = [
        pltpu.make_async_copy(msa_ref, out_msa, sem.at[0]),
        pltpu.make_async_copy(pair_ref, out_pair, sem.at[1]),
    ]
    for copy in copies:
        copy.start()
    for copy in copies:
        copy.wait()


def on_device(sizes, x, pair, chain, resolved, positions, *weights):
    seqs, rows_i, width = x.shape
    cols, pwidth = pair.shape[1:]
    n_pb, n_a, n_b, n_c = sizes
    cells = rows_i * cols
    chains, residues = chain.shape[0], resolved.shape[0]
    n_as = n_a // n_pb
    n_src = n_as * n_b * n_c
    arrays = dict(zip(WEIGHTS, weights))
    arrays["duo"] = arrays["duo"].T
    arrays["tbias"] = arrays["tbias"].T
    tiles = width // LANES
    arrays["x"] = x.reshape(seqs, rows_i, tiles, LANES).transpose(0, 2, 1, 3).reshape(-1, LANES)
    arrays["pair"] = pair.reshape(cells, pwidth)
    arrays["chain"] = chain.reshape(1, chains)
    arrays["resolved"] = resolved.reshape(1, residues)
    arrays["positions"] = positions.reshape(1, residues)
    arrays["scalars"] = positions
    inputs = [arrays[name] for name in INPUTS]
    factor = arrays["duo"].shape[0] // 2
    eparts = factor // SUBLANES
    msg_rows = eparts * seqs // LANES * rows_i * SUBLANES + rows_i * TRI_HEADS
    mates = n_b * n_c - 1
    dma = pltpu.SemaphoreType.DMA
    msa, pair_out = pl.pallas_call(
        functools.partial(kernel, sizes, (rows_i, seqs, width)),
        out_shape=(
            pltpu.VMEM(arrays["x"].shape, BF16),
            pltpu.VMEM((cells, pwidth), BF16),
        ),
        in_specs=[pl.BlockSpec(memory_space=pltpu.HBM)] * len(inputs),
        out_specs=(pl.BlockSpec(memory_space=pltpu.VMEM),) * 2,
        scratch_shapes=[
            (pltpu.SMEM if name == "scalars" else pltpu.VMEM)(v.shape, v.dtype) for name, v in zip(INPUTS, inputs)
        ]
        + [
            pltpu.VMEM((n_pb,) + arrays["x"].shape, BF16),
            pltpu.VMEM((n_pb, cells, pwidth), BF16),
            pltpu.VMEM((n_pb, rows_i * seqs, width), BF16),
            pltpu.VMEM((n_pb, rows_i * seqs, width), BF16),
            pltpu.VMEM((n_pb, eparts * seqs, rows_i * LANES), BF16),
            pltpu.VMEM((msg_rows, LANES), BF16),
            pltpu.VMEM((n_src, n_pb, msg_rows, LANES), BF16),
            pltpu.VMEM((TRI_HEADS * cols, residues), F32),
            pltpu.VMEM((n_pb, cells, pwidth), F32),
            pltpu.VMEM((n_pb, cells, 2 * pwidth), BF16),
            pltpu.VMEM(arrays["tensor"].shape, F32),
            pltpu.VMEM(arrays["tensor"].shape, BF16),
            pltpu.VMEM((max(cells * SUBLANES, msg_rows), LANES), F32),
            pltpu.VMEM(arrays["x"].shape, F32),
            pltpu.VMEM((rows_i, VERTICAL_ATTENDS * seqs, width), BF16),
            pltpu.VMEM((rows_i, TRI_HEADS * cols, pwidth), BF16),
            dma((len(inputs),)),
            dma((n_pb,)),
            dma((n_pb,)),
            dma((n_pb,)),
            dma((n_pb,)),
            dma((n_a,)),
            dma((n_as * n_pb,)),
            dma((n_as * mates,)),
            dma((n_src,)),
        ],
        compiler_params=pltpu.CompilerParams(
            collective_id=0, has_side_effects=True, vmem_limit_bytes=56 * 1024 * 1024
        ),
    )(*inputs)
    hbm = pl.BlockSpec(memory_space=pltpu.HBM)
    vmem = pl.BlockSpec(memory_space=pltpu.VMEM)
    msa, pair_out = pl.pallas_call(
        finish,
        out_shape=(
            jax.ShapeDtypeStruct(msa.shape, BF16),
            jax.ShapeDtypeStruct(pair_out.shape, BF16),
        ),
        in_specs=[vmem] * 2,
        out_specs=(hbm, hbm),
        scratch_shapes=[dma((2,))],
        compiler_params=pltpu.CompilerParams(vmem_limit_bytes=8 * 1024 * 1024),
    )(msa, pair_out)
    msa = msa.reshape(seqs, tiles, rows_i, LANES).transpose(0, 2, 1, 3).reshape(x.shape)
    return msa, pair_out.reshape(rows_i, cols, pwidth)


def solution(mesh):
    n_row, n_br, n_pb = mesh.shape["row"], mesh.shape["br"], mesh.shape["pb"]
    n_b = 2 if n_row % (2 * n_pb) == 0 else 1
    sizes = (n_pb, n_row // n_b, n_b, n_br)
    return jax.shard_map(
        functools.partial(on_device, sizes),
        mesh=mesh,
        in_specs=(
            P(("grp", "pb"), ("row", "br"), None),
            P(("grp", "row", "br"), "pb", None),
            P("grp"),
            P("grp"),
            P("grp"),
        )
        + (P(),) * 12,
        out_specs=(P(("grp", "pb"), ("row", "br"), None), P(("grp", "row", "br"), "pb", None)),
        check_vma=False,
    )
```
